32 devices in a mesh: grp: 8 (over z, y), row: 4 (over x, core).
Axes of the slice: x: 2, y: 2, z: 4, core: 2. Of those that a mesh axis runs over, the one named last changes fastest.
Arguments:
- frames: bfloat16 [16384, 1024], P(('grp', 'row')), may hold values from -6 to 6
- time_embed: float32 [8, 4, 1024], P('grp'), may hold values from -6 to 6
- lengths: int32 [8, 4], P('grp'), may hold values from 1 to 1792, 2048 in all within a row
- mod_weight: bfloat16 [1024, 6144], replicated, may hold values from -0.1875 to 0.1875
- mod_bias: float32 [6144], replicated, may hold values from -2 to 2
- query_weight: bfloat16 [1024, 1024], replicated, may hold values from -0.1875 to 0.1875
- query_bias: float32 [1024], replicated, may hold values from -3 to 3
- key_weight: bfloat16 [1024, 1024], replicated, may hold values from -0.1875 to 0.1875
- key_bias: float32 [1024], replicated, may hold values from -3 to 3
- value_weight: bfloat16 [1024, 1024], replicated, may hold values from -0.1875 to 0.1875
- value_bias: float32 [1024], replicated, may hold values from -3 to 3
- out_weight: bfloat16 [1024, 1024], replicated, may hold values from -0.75 to 0.75
- out_bias: float32 [1024], replicated, may hold values from -3 to 3
- up_weight: bfloat16 [1024, 2048], replicated, may hold values from -0.1875 to 0.1875
- up_bias: float32 [2048], replicated, may hold values from -3 to 3
- down_weight: bfloat16 [2048, 1024], replicated, may hold values from -0.125 to 0.125
- down_bias: float32 [1024], replicated, may hold values from -3 to 3
- cotangent: bfloat16 [16384, 1024], P(('grp', 'row')), may hold values from -6 to 6
Outputs:
- output: bfloat16 [16384, 1024], P(('grp', 'row'))
- frames_grad: bfloat16 [16384, 1024], P(('grp', 'row'))
- embed_grad: float32 [8, 4, 1024], P('grp')
- mod_weight_grad: float32 [1024, 6144], P('row')
- mod_bias_grad: float32 [6144], P('row')
- query_weight_grad: float32 [1024, 1024], P('row')
- query_bias_grad: float32 [1024], P('row')
- key_weight_grad: float32 [1024, 1024], P('row')
- key_bias_grad: float32 [1024], P('row')
- value_weight_grad: float32 [1024, 1024], P('row')
- value_bias_grad: float32 [1024], P('row')
- out_weight_grad: float32 [1024, 1024], P('row')
- out_bias_grad: float32 [1024], P('row')
- up_weight_grad: float32 [1024, 2048], P('row')
- up_bias_grad: float32 [2048], P('row')
- down_weight_grad: float32 [2048, 1024], P('row')
- down_bias_grad: float32 [1024], P('row')
The draws below stay inside these ranges and needn't reach their ends.
Inputs may be any that keep to these rules, and one draw needn't show every extreme that they name: Each row of lengths is one group: its 4 lengths add up to 2048, and the largest is exactly 1792.
All inputs are finite; a program needn't handle non-finite values.
Results may differ from the reference program's by a relative error of at most 0.028.
Values may be sent and summed in bfloat16 or wider, within the bound.
A program may use at most 256 MiB of HBM per device.

```python
import math
import jax
import jax.numpy as jnp
import numpy as np
from jax import lax

D = 1024
HEADS = 16
HEAD_DIM = 64
FF = 2048
UTT = 4
GROUP_TOK = 2048
GROUPS = 8
TOKENS = 16384
LONGEST = 1792


def level_of(rng, shape, pieces, smallest, top_value):
    def one(axis_at, blocks):
        heights = jax.random.uniform(jax.random.fold_in(jax.random.fold_in(rng, 6), axis_at), (blocks,), jnp.float32, smallest / len(pieces), top_value / len(pieces))
        return jnp.repeat(jnp.exp(heights), shape[axis_at] // blocks).reshape((-1,) + (1,) * (len(shape) - axis_at - 1))

    factor_of = one(*pieces[0])
    for cut in pieces[1:]:
        factor_of = factor_of * one(*cut)
    return factor_of


def length_profile(number_of, total, most, skew):
    loads = [(1 << 20) // math.isqrt(standing ** skew) + 1 for standing in range(2, number_of + 1)]
    spare, holding = total - most - (number_of - 1), [1] * (number_of - 1)
    while spare > 0:
        candidates = [i for i in range(number_of - 1) if holding[i] < most]
        pool, left = sum([loads[i] for i in candidates]), spare
        for i in candidates:
            extra = min(most - holding[i], max(1, left * loads[i] // pool), spare)
            holding[i] = holding[i] + extra
            spare = spare - extra
    return np.array([most] + holding)


def uneven_parts(own_key, amount, total, bound, skew):
    if amount == 2:
        one = jax.random.randint(own_key, (), max(1, total - bound), min(bound, total - 1) + 1)
        return jnp.stack([one, total - one])
    sizes = jnp.asarray(length_profile(amount, total, bound, skew), jnp.int32)
    twos = (amount - 1) // 2
    giver, receiver = sizes[1:1 + 2 * twos:2], sizes[2:2 + 2 * twos:2]
    margin = jnp.minimum(giver - 1, bound - receiver)
    passed = jax.random.randint(jax.random.fold_in(own_key, 1), (twos,), 0, 1 << 20) % (margin + 1)
    sizes = sizes.at[1:1 + 2 * twos:2].set(giver - passed).at[2:2 + 2 * twos:2].set(receiver + passed)
    return sizes[jax.random.permutation(jax.random.fold_in(own_key, 2), amount)]


def noise(rng, extent, spread, limit, cuts=(), kind=jnp.bfloat16):
    values = spread * jax.random.normal(rng, extent, jnp.float32)
    if cuts:
        values = values * level_of(rng, extent, cuts, -0.22, 0.18)
    return jnp.clip(values, -limit, limit).astype(kind)


def setup_inputs(seed: int = 0) -> dict:
    key_of = jax.random.split(jax.random.key(seed), 19)
    frames = noise(key_of[0], (TOKENS, D), 1.0, 6.0, ((0, 32),))
    time_embed = noise(key_of[1], (GROUPS, UTT, D), 1.0, 6.0, ((0, 8),), jnp.float32)
    lengths = jax.vmap(lambda own: uneven_parts(own, UTT, GROUP_TOK, LONGEST, 2))(jax.random.split(key_of[2], GROUPS)).reshape((GROUPS, UTT)).astype(jnp.int32)
    mod_weight = noise(key_of[3], (D, 6 * D), D ** -0.5, 0.1875)
    mod_bias = noise(key_of[4], (6 * D,), 0.3, 2.0, (), jnp.float32)
    query_weight = noise(key_of[5], (D, D), D ** -0.5, 0.1875)
    query_bias = noise(key_of[6], (D,), 0.5, 3.0, (), jnp.float32)
    key_weight = noise(key_of[7], (D, D), D ** -0.5, 0.1875)
    key_bias = noise(key_of[8], (D,), 0.5, 3.0, (), jnp.float32)
    value_weight = noise(key_of[9], (D, D), D ** -0.5, 0.1875)
    value_bias = noise(key_of[10], (D,), 0.5, 3.0, (), jnp.float32)
    out_weight = noise(key_of[11], (D, D), (D // 16) ** -0.5, 0.75)
    out_bias = noise(key_of[12], (D,), 0.5, 3.0, (), jnp.float32)
    up_weight = noise(key_of[13], (D, FF), D ** -0.5, 0.1875)
    up_bias = noise(key_of[14], (FF,), 0.5, 3.0, (), jnp.float32)
    down_weight = noise(key_of[15], (FF, D), FF ** -0.5, 0.125)
    down_bias = noise(key_of[16], (D,), 0.5, 3.0, (), jnp.float32)
    cotangent = noise(key_of[17], (TOKENS, D), 1.0, 6.0, ((0, 32),))
    return {"frames": frames, "time_embed": time_embed, "lengths": lengths, "mod_weight": mod_weight, "mod_bias": mod_bias, "query_weight": query_weight, "query_bias": query_bias, "key_weight": key_weight, "key_bias": key_bias, "value_weight": value_weight, "value_bias": value_bias, "out_weight": out_weight, "out_bias": out_bias, "up_weight": up_weight, "up_bias": up_bias, "down_weight": down_weight, "down_bias": down_bias, "cotangent": cotangent}


@jax.custom_vjp
def low(v):
    return lax.optimization_barrier(v.astype(jnp.bfloat16)).astype(jnp.float32)

@jax.custom_vjp
def low_back(v):
    return v

def low_keep(v):
    return (low(v), None)

def low_pass(kept, grad):
    return (grad,)

def back_keep(v):
    return (v, None)

def back_low(kept, grad):
    return (low(grad),)
low.defvjp(low_keep, low_pass)
low_back.defvjp(back_keep, back_low)
highest = lax.Precision.HIGHEST

def matmul(left, right):
    return jnp.dot(left, right, precision=highest, preferred_element_type=jnp.float32)

def layer_norm(tensor):
    centred = tensor - lax.optimization_barrier(jnp.mean(tensor, axis=-1, keepdims=True))
    return centred * lax.rsqrt(lax.optimization_barrier(jnp.mean(centred * centred, axis=-1, keepdims=True)) + 1e-06)

def rotary_tables(position):
    half_dim = HEAD_DIM // 2
    frequency = jnp.exp(jnp.arange(half_dim, dtype=jnp.float32) * (-2.0 * math.log(10000.0) / HEAD_DIM))
    angles = position.astype(jnp.float32)[:, None] * frequency[None, :]
    angles = jnp.concatenate([angles, angles], axis=1)
    return (jnp.cos(angles), jnp.sin(angles))

def rotate(tensor, cosine, sine_table):
    half_dim = tensor.shape[-1] // 2
    turned = jnp.concatenate([-tensor[..., half_dim:], tensor[..., :half_dim]], axis=-1)
    return tensor * cosine[:, None, :] + turned * sine_table[:, None, :]

def segment_layout(utt_sizes, total_rows):
    finish = jnp.cumsum(utt_sizes).astype(jnp.int32)
    starts = finish - utt_sizes.astype(jnp.int32)
    places = jnp.arange(total_rows, dtype=jnp.int32)
    segment = lax.optimization_barrier(jnp.sum((places[:, None] >= finish[None, :]).astype(jnp.int32), axis=1)).astype(jnp.int32)
    is_member = segment[:, None] == jnp.arange(utt_sizes.shape[0], dtype=jnp.int32)[None, :]
    position = places - lax.optimization_barrier(jnp.sum(jnp.where(is_member, starts[None, :], 0), axis=1)).astype(jnp.int32)
    return (segment, is_member.astype(jnp.float32), position)

def block_forward(frames_in, embedding, params, segment, member, cosine, sine_table):
    mod_weight, mod_bias, query_weight, query_bias, key_weight, key_bias, value_weight, value_bias, out_weight, out_bias, up_weight, up_bias, down_weight, down_bias = params
    row_count = frames_in.shape[0]
    modulation = low_back(matmul(low(jax.nn.silu(embedding)), mod_weight) + mod_bias)
    per_token = matmul(member, modulation)
    shift_attn, scale_attn, gate_attn, shift_ffn, scale_ffn, gate_ffn = jnp.split(per_token, 6, axis=1)
    normed = low(layer_norm(frames_in) * (1.0 + scale_attn) + shift_attn)
    queries = low_back(matmul(normed, query_weight) + query_bias)
    keys = low_back(matmul(normed, key_weight) + key_bias)
    values = low(low_back(matmul(normed, value_weight) + value_bias)).reshape(row_count, HEADS, HEAD_DIM)
    queries = low(rotate(queries.reshape(row_count, HEADS, HEAD_DIM), cosine, sine_table))
    keys = low(rotate(keys.reshape(row_count, HEADS, HEAD_DIM), cosine, sine_table))
    scores = jnp.einsum('qhd,khd->hqk', queries, keys, precision=highest) * HEAD_DIM ** (-0.5)
    same_utt = segment[:, None] == segment[None, :]
    scores = low_back(jnp.where(same_utt[None], scores, -1e+30))
    weights = low(jax.nn.softmax(scores, axis=-1))
    mixed_heads = jnp.einsum('hqk,khd->qhd', weights, values, precision=highest).reshape(row_count, D)
    mixed_heads = low(low_back(mixed_heads))
    attended = low_back(matmul(mixed_heads, out_weight) + out_bias)
    middle = frames_in + gate_attn * attended
    normed_ffn = low(layer_norm(middle) * (1.0 + scale_ffn) + shift_ffn)
    hidden = low_back(matmul(normed_ffn, up_weight) + up_bias)
    active = low(jax.nn.gelu(hidden, approximate=True))
    branch = low_back(matmul(active, down_weight) + down_bias)
    return middle + gate_ffn * branch

def reference(frames, time_embed, lengths, mod_weight, mod_bias, query_weight, query_bias, key_weight, key_bias, value_weight, value_bias, out_weight, out_bias, up_weight, up_bias, down_weight, down_bias, cotangent):
    params = tuple((tensor.astype(jnp.float32) for tensor in (mod_weight, mod_bias, query_weight, query_bias, key_weight, key_bias, value_weight, value_bias, out_weight, out_bias, up_weight, up_bias, down_weight, down_bias)))
    frame_groups = frames.astype(jnp.float32).reshape(GROUPS, GROUP_TOK, D)
    cot_groups = cotangent.astype(jnp.float32).reshape(GROUPS, GROUP_TOK, D)

    def one_group(totals, inputs):
        rows_in, embedding, utt_sizes, cot_in = inputs
        segment, member, position = segment_layout(utt_sizes, GROUP_TOK)
        cosine, sine_table = rotary_tables(position)

        def forward(rows_arg, embed_arg, params_arg):
            return block_forward(rows_arg, embed_arg, params_arg, segment, member, cosine, sine_table)
        result, pullback = jax.vjp(forward, rows_in, embedding, params)
        d_rows, d_embed, d_params = pullback(cot_in)
        totals = jax.tree.map(lambda running, update: running + update, totals, d_params)
        return (totals, (result.astype(jnp.bfloat16), d_rows.astype(jnp.bfloat16), d_embed))
    zero_grads = jax.tree.map(jnp.zeros_like, params)
    totals, (outputs, grads_in, embed_grads) = lax.scan(one_group, zero_grads, (frame_groups, time_embed.astype(jnp.float32), lengths, cot_groups))
    return (outputs.reshape(TOKENS, D), grads_in.reshape(TOKENS, D), embed_grads, totals[0], totals[1], totals[2], totals[3], totals[4], totals[5], totals[6], totals[7], totals[8], totals[9], totals[10], totals[11], totals[12], totals[13])
```

```python
import functools
import math

import jax
import jax.numpy as jnp
from jax import lax
from jax.experimental import pallas as pl
from jax.experimental.pallas import tpu as pltpu
from jax.sharding import PartitionSpec as P

D = 1024
HEADS = 16
HEAD_DIM = 64
LONGEST = 1792
TILE = 256
BF = jnp.bfloat16
F32 = jnp.float32

highest = lax.Precision.HIGHEST
VMEM = pltpu.VMEM
SMEM = pltpu.SMEM
LIMIT = 60 << 20


def matdot(left, right, left_dim, right_dim):
    return lax.dot_general(
        left, right, (((left_dim,), (right_dim,)), ((), ())), preferred_element_type=F32
    )


def contract_rows(left, right):
    return matdot(left, right, 0, 0)


def against(left, weight):
    return matdot(left, weight, 1, 1)


def column_sum(tensor):
    return jnp.sum(tensor.astype(F32), axis=0)


def normalize(tensor):
    centred = tensor - jnp.mean(tensor, axis=-1, keepdims=True)
    factor = lax.rsqrt(jnp.mean(centred * centred, axis=-1, keepdims=True) + 1e-06)
    return (centred * factor, factor)


def normalize_back(grad_normed, normed, factor):
    mean_grad = jnp.mean(grad_normed, axis=-1, keepdims=True)
    mean_cross = jnp.mean(grad_normed * normed, axis=-1, keepdims=True)
    return (grad_normed - mean_grad - normed * mean_cross) * factor


def exchange(tensor, axis, bit):
    size = lax.axis_size(axis)
    return lax.ppermute(tensor, axis, [(i, i ^ bit) for i in range(size)])


def add_low(left, right):
    return (left.astype(F32) + right.astype(F32)).astype(BF)


def grp_bit(bit):
    return (lax.axis_index("grp") // bit) % 2


def halve(tensor, dim, bit):
    side = grp_bit(bit)
    half = tensor.shape[dim] // 2
    send = lax.dynamic_slice_in_dim(tensor, (1 - side) * half, half, dim)
    keep = lax.dynamic_slice_in_dim(tensor, side * half, half, dim)
    return add_low(keep, exchange(send, "grp", bit))


def grow(tensor, dim, bit):
    other = exchange(tensor, "grp", bit)
    return jnp.where(
        grp_bit(bit) == 0,
        jnp.concatenate([tensor, other], dim),
        jnp.concatenate([other, tensor], dim),
    )


def bits_of(count):
    return [1 << i for i in range(count.bit_length() - 1)]


def roll_matrix(offset):
    row = lax.broadcasted_iota(jnp.int32, (TILE, 2 * TILE), 0)
    col = lax.broadcasted_iota(jnp.int32, (TILE, 2 * TILE), 1)
    return (col == row + offset).astype(F32).astype(BF)


def project_kernel(
    place, x0, x1, x2, x3, mod_all, mod_long, member, weight_t, bias, cos_t, sin_t,
    mixed_out, qt_out, kt_out, vt_out, k_out, v_out, rows_ref, roll_ref,
):
    step = pl.program_id(0)
    block = x0.shape[0]
    total = 4 * block

    @pl.when(step == 0)
    def _():
        for j, source in enumerate((x0, x1, x2, x3)):
            at = pl.multiple_of((place[0] ^ j) * block, block)
            rows_ref[pl.ds(at, block), :] = source[...]
        rows_ref[pl.ds(total, TILE), :] = rows_ref[pl.ds(0, TILE), :]
        roll_ref[...] = roll_matrix(place[1])

    pair = rows_ref[pl.ds(pl.multiple_of(step * TILE, TILE), 2 * TILE), :]
    normed, _ = normalize(matdot(roll_ref[...], pair, 1, 0))
    last = step == total // TILE - 1

    @pl.when(jnp.logical_not(last))
    def _():
        mixed_out[...] = (normed * (1.0 + mod_long[:, D:]) + mod_long[:, :D]).astype(BF)

    @pl.when(last)
    def _():
        per_row = jnp.zeros((TILE, 2 * D), F32)
        for u in range(mod_all.shape[0]):
            per_row = per_row + member[:, u : u + 1] * mod_all[u : u + 1, :]
        mixed_out[...] = (normed * (1.0 + per_row[:, D:]) + per_row[:, :D]).astype(BF)

    wide = matdot(weight_t[...], mixed_out[...], 1, 1) + bias[...]
    cosine, sine = cos_t[...], sin_t[...]
    half = HEAD_DIM // 2
    width = qt_out.shape[0]

    def turned(base):
        parts = []
        for at in range(base, base + width, HEAD_DIM):
            first, second = wide[at : at + half], wide[at + half : at + HEAD_DIM]
            parts.append(first * cosine - second * sine)
            parts.append(second * cosine + first * sine)
        return jnp.concatenate(parts, 0)

    keys = turned(width)
    values = wide[2 * width :]
    qt_out[...] = turned(0).astype(BF) * jnp.asarray(HEAD_DIM**-0.5, BF)
    kt_out[...] = keys.astype(BF)
    vt_out[...] = values.astype(BF)
    k_out[...] = keys.T.astype(BF)
    v_out[...] = values.T.astype(BF)


def project(place, blocks, mod_all, mod_long, member, weight_t, bias, cos_t, sin_t):
    block = blocks[0].shape[0]
    total = 4 * block
    width = weight_t.shape[0] // 3
    whole = lambda a: pl.BlockSpec(a.shape, lambda i: (0, 0))
    rows = lambda n: pl.BlockSpec((TILE, n), lambda i: (i, 0))
    cols = lambda n: pl.BlockSpec((n, TILE), lambda i: (0, i))
    return pl.pallas_call(
        project_kernel,
        grid=(total // TILE,),
        out_shape=[
            jax.ShapeDtypeStruct((total, D), BF),
            jax.ShapeDtypeStruct((width, total), BF),
            jax.ShapeDtypeStruct((width, total), BF),
            jax.ShapeDtypeStruct((width, total), BF),
            jax.ShapeDtypeStruct((total, width), BF),
            jax.ShapeDtypeStruct((total, width), BF),
        ],
        in_specs=[pl.BlockSpec(memory_space=SMEM)]
        + [whole(a) for a in blocks]
        + [whole(mod_all), whole(mod_long), whole(member), whole(weight_t), whole(bias)]
        + [cols(HEAD_DIM // 2), cols(HEAD_DIM // 2)],
        out_specs=[rows(D), cols(width), cols(width), cols(width), rows(width), rows(width)],
        scratch_shapes=[VMEM((total + TILE, D), BF), VMEM((TILE, 2 * TILE), BF)],
        compiler_params=pltpu.CompilerParams(vmem_limit_bytes=LIMIT),
        cost_estimate=pl.CostEstimate(
            flops=2 * total * D * 3 * width, bytes_accessed=16 << 20, transcendentals=total
        ),
        name="project",
    )(place, *blocks, mod_all, mod_long, member, weight_t, bias, cos_t, sin_t)


def one_head(pair, head):
    part = pair[head * HEAD_DIM : (head + 1) * HEAD_DIM]
    empty = jnp.zeros_like(part)
    return jnp.concatenate([part, empty] if head == 0 else [empty, part], 0)


def unroll(outs, rolled_ref, place, block):
    total = 4 * block
    rolled_ref[:, pl.ds(0, TILE)] = rolled_ref[:, pl.ds(total, TILE)]
    back = roll_matrix(TILE - place[1])
    for j, out in enumerate(outs):
        for part in range(block // TILE):
            at = pl.multiple_of((place[0] ^ j) * block + part * TILE, TILE)
            rows = matdot(back, rolled_ref[:, pl.ds(at, 2 * TILE)], 1, 1)
            out[part * TILE : (part + 1) * TILE, :] = rows.astype(BF)


def attend_kernel(
    place, qt, k, vt, seg_col, seg_row, ot_out, lse_out, o0, o1, o2, o3, rolled_ref
):
    step = pl.program_id(0)
    total = k.shape[0]
    block = total // 4
    last = step == total // TILE - 1

    def run(first, count, allowed):
        outs, tops = [], []
        for head in range(2):
            scores = matdot(k[pl.ds(first, count), :], one_head(qt[...], head), 1, 0)
            if allowed is not None:
                scores = jnp.where(allowed, scores, -1e30)
            top = jnp.max(scores, axis=0, keepdims=True)
            weights = jnp.exp(scores - top)
            exp_sum = jnp.sum(weights, axis=0, keepdims=True)
            mixed = matdot(
                vt[head * HEAD_DIM : (head + 1) * HEAD_DIM, pl.ds(first, count)],
                weights.astype(BF),
                1,
                0,
            )
            outs.append(mixed / exp_sum)
            tops.append(top + jnp.log(exp_sum))
        mixed = jnp.concatenate(outs, 0)
        low = mixed.astype(BF)
        ot_out[...] = low
        lse_out[...] = jnp.concatenate(tops * 4, 0)
        rolled_ref[:, pl.ds(pl.multiple_of(TILE + step * TILE, TILE), TILE)] = low

    @pl.when(jnp.logical_not(last))
    def _():
        run(0, LONGEST, None)

    @pl.when(last)
    def _():
        run(LONGEST, total - LONGEST, seg_col[...] == seg_row[...])
        unroll((o0, o1, o2, o3), rolled_ref, place, block)


def attend(place, pair, qt, k, vt, seg_col, seg_row):
    total = k.shape[0]
    block = total // 4
    whole = lambda a: pl.BlockSpec(a.shape, lambda i: (0, 0))
    return pl.pallas_call(
        attend_kernel,
        grid=(total // TILE,),
        out_shape=[
            jax.ShapeDtypeStruct((128, total), BF),
            jax.ShapeDtypeStruct((8, total), F32),
        ]
        + [jax.ShapeDtypeStruct((block, 128), BF)] * 4,
        in_specs=[
            pl.BlockSpec(memory_space=SMEM),
            pl.BlockSpec((128, TILE), lambda i: (pair, i)),
            pl.BlockSpec((total, 128), lambda i: (0, pair)),
            pl.BlockSpec((128, total), lambda i: (pair, 0)),
            whole(seg_col),
            whole(seg_row),
        ],
        out_specs=[
            pl.BlockSpec((128, TILE), lambda i: (0, i)),
            pl.BlockSpec((8, TILE), lambda i: (0, i)),
        ]
        + [pl.BlockSpec((block, 128), lambda i: (0, 0))] * 4,
        scratch_shapes=[VMEM((128, total + TILE), BF)],
        compiler_params=pltpu.CompilerParams(vmem_limit_bytes=LIMIT),
        cost_estimate=pl.CostEstimate(
            flops=2 * 2 * 2 * total * LONGEST * 256,
            bytes_accessed=4 << 20,
            transcendentals=2 * total * LONGEST,
        ),
        name="attend",
    )(place, qt, k, vt, seg_col, seg_row)


def attend_back_kernel(
    place, qt, k, kt, v, ot, lse, g0, g1, g2, g3, seg_col, seg_row, cos_t, sin_t,
    rolled_out, bias_out, s0, s1, s2, s3,
    grad_rows, grad_t, row_dots, dqt, dkt, dvt, nat_ref,
):
    step = pl.program_id(0)
    total = k.shape[0]
    block = total // 4
    steps = total // TILE
    last = step == steps - 1
    half = HEAD_DIM // 2

    @pl.when(step == 0)
    def _():
        for j, source in enumerate((g0, g1, g2, g3)):
            at = pl.multiple_of((place[0] ^ j) * block, block)
            grad_rows[pl.ds(at, block), :] = source[...]
        grad_rows[pl.ds(total, TILE), :] = grad_rows[pl.ds(0, TILE), :]
        dkt[...] = jnp.zeros_like(dkt)
        dvt[...] = jnp.zeros_like(dvt)

        ahead = roll_matrix(place[1])

        def turn(i, carry):
            cols = pl.ds(pl.multiple_of(i * TILE, TILE), TILE)
            two = grad_rows[pl.ds(pl.multiple_of(i * TILE, TILE), 2 * TILE), :]
            part = matdot(ahead, two, 1, 0).T
            grad_t[:, cols] = part.astype(BF)
            crossed = part * ot[:, cols].astype(F32)
            row_dots[0:1, cols] = jnp.sum(crossed[:HEAD_DIM], axis=0, keepdims=True)
            row_dots[1:2, cols] = jnp.sum(crossed[HEAD_DIM:], axis=0, keepdims=True)
            return carry

        lax.fori_loop(0, steps, turn, 0)

    here = pl.ds(pl.multiple_of(step * TILE, TILE), TILE)

    def run(first, count, allowed):
        keys = pl.ds(first, count)
        for head in range(2):
            mine = slice(head * HEAD_DIM, (head + 1) * HEAD_DIM)
            scores = matdot(k[keys, :], one_head(qt[:, here], head), 1, 0)
            if allowed is not None:
                scores = jnp.where(allowed, scores, -1e30)
            probs = jnp.exp(scores - lse[head : head + 1, here])
            grad_probs = matdot(v[keys, :], one_head(grad_t[:, here], head), 1, 0)
            grad_scores = (probs * (grad_probs - row_dots[head : head + 1, here])).astype(BF)
            dqt[mine, here] = matdot(kt[mine, keys], grad_scores, 1, 0) * HEAD_DIM**-0.5
            dkt[mine, keys] += matdot(qt[mine, here], grad_scores, 1, 1)
            dvt[mine, keys] += matdot(grad_t[mine, here], probs.astype(BF), 1, 1)

    @pl.when(jnp.logical_not(last))
    def _():
        run(0, LONGEST, None)

    @pl.when(last)
    def _():
        run(LONGEST, total - LONGEST, seg_col[...] == seg_row[...])

        def finish(i, sums):
            cols = pl.ds(pl.multiple_of(i * TILE, TILE), TILE)
            cosine, sine = cos_t[:, cols], sin_t[:, cols]

            def turned(ref):
                parts = []
                for at in range(0, 128, HEAD_DIM):
                    first, second = ref[at : at + half, cols], ref[at + half : at + HEAD_DIM, cols]
                    parts.append(first * cosine + second * sine)
                    parts.append(second * cosine - first * sine)
                return jnp.concatenate(parts, 0)

            columns = jnp.concatenate([turned(dqt), turned(dkt), dvt[:, cols]], 0)
            nat_ref[:, pl.ds(pl.multiple_of(TILE + i * TILE, TILE), TILE)] = columns.astype(BF)
            low = columns.T.astype(BF)
            rolled_out[cols, :] = low
            return sums + jnp.sum(low.astype(F32), axis=0, keepdims=True)

        sums = lax.fori_loop(0, steps, finish, jnp.zeros((1, 384), F32))
        bias_out[...] = jnp.broadcast_to(sums, bias_out.shape)
        unroll((s0, s1, s2, s3), nat_ref, place, block)


def attend_back(place, pair, qt, k, kt, v, ot, lse, grads, seg_col, seg_row, cos_t, sin_t):
    total = k.shape[0]
    block = total // 4
    whole = lambda a: pl.BlockSpec(a.shape, lambda i: (0, 0))
    wide = pl.BlockSpec((128, total), lambda i: (pair, 0))
    tall = pl.BlockSpec((total, 128), lambda i: (0, pair))
    return pl.pallas_call(
        attend_back_kernel,
        grid=(total // TILE,),
        out_shape=[
            jax.ShapeDtypeStruct((total, 384), BF),
            jax.ShapeDtypeStruct((8, 384), F32),
        ]
        + [jax.ShapeDtypeStruct((block, 384), BF)] * 4,
        in_specs=[
            pl.BlockSpec(memory_space=SMEM),
            wide,
            tall,
            wide,
            tall,
            whole(ot),
            whole(lse),
        ]
        + [whole(g) for g in grads]
        + [whole(seg_col), whole(seg_row), whole(cos_t), whole(sin_t)],
        out_specs=[
            pl.BlockSpec((total, 384), lambda i: (0, 0)),
            pl.BlockSpec((8, 384), lambda i: (0, 0)),
        ]
        + [pl.BlockSpec((block, 384), lambda i: (0, 0))] * 4,
        scratch_shapes=[
            VMEM((total + TILE, 128), BF),
            VMEM((128, total), BF),
            VMEM((8, total), F32),
            VMEM((128, total), F32),
            VMEM((128, total), F32),
            VMEM((128, total), F32),
            VMEM((384, total + TILE), BF),
        ],
        compiler_params=pltpu.CompilerParams(vmem_limit_bytes=LIMIT),
        cost_estimate=pl.CostEstimate(
            flops=2 * 2 * 5 * total * LONGEST * 256,
            bytes_accessed=8 << 20,
            transcendentals=2 * total * LONGEST,
        ),
        name="attend_back",
    )(place, qt, k, kt, v, ot, lse, *grads, seg_col, seg_row, cos_t, sin_t)


def weight_grad_kernel(place, o, h, a, e_att, e_z, e_b, out):
    out[0, :256] = contract_rows(o[...], e_att[...]).astype(BF)
    out[0, 256:512] = contract_rows(h[...], e_z[:, :D]).astype(BF)
    out[0, 512:768] = contract_rows(h[...], e_z[:, D:]).astype(BF)
    out[0, 768:] = contract_rows(a[...], e_b[...]).astype(BF)


def weight_grads(place, order, o, h, a, e_att, e_z, e_b):
    rows = o.shape[0]
    first, second = order
    pick = lambda i: first + i * (second - first)
    whole = lambda t: pl.BlockSpec(t.shape, lambda i, p: (0, 0))
    return pl.pallas_call(
        weight_grad_kernel,
        grid_spec=pltpu.PrefetchScalarGridSpec(
            num_scalar_prefetch=1,
            grid=(2,),
            in_specs=[
                pl.BlockSpec((rows, 256), lambda i, p: (0, pick(i))),
                pl.BlockSpec((rows, 256), lambda i, p: (0, p[0] ^ pick(i))),
                pl.BlockSpec((rows, 512), lambda i, p: (0, p[0] ^ pick(i))),
                whole(e_att),
                whole(e_z),
                whole(e_b),
            ],
            out_specs=pl.BlockSpec((1, 1280, D), lambda i, p: (i, 0, 0)),
        ),
        out_shape=jax.ShapeDtypeStruct((2, 1280, D), BF),
        compiler_params=pltpu.CompilerParams(vmem_limit_bytes=LIMIT),
        cost_estimate=pl.CostEstimate(
            flops=2 * 2 * rows * 1280 * D, bytes_accessed=12 << 20, transcendentals=0
        ),
        name="weight_grads",
    )(place, o, h, a, e_att, e_z, e_b)


def local(
    frames, time_embed, lengths, mod_weight, mod_bias, query_weight, query_bias, key_weight, key_bias,
    value_weight, value_bias, out_weight, out_bias, up_weight, up_bias, down_weight, down_bias, cotangent,
):
    n_grp = lax.axis_size("grp")
    row_count = frames.shape[0]
    my_row = lax.axis_index("row")
    group_rows = row_count * lax.axis_size("row")
    width = D // 4

    from_core = exchange(frames, "row", 1)
    from_x = exchange(frames, "row", 2)
    from_both = exchange(from_x, "row", 1)

    utt_sizes = lengths[0]
    finish = jnp.cumsum(utt_sizes)
    starts = finish - utt_sizes
    longest = jnp.argmax(utt_sizes)
    offset = starts[longest]
    place = jnp.stack([my_row, offset]).astype(jnp.int32)
    utts = jnp.arange(utt_sizes.shape[0], dtype=jnp.int32)

    def layout(rows):
        segment = jnp.sum((rows[:, None] >= finish[None, :]).astype(jnp.int32), axis=1)
        is_member = segment[:, None] == utts[None, :]
        position = rows - jnp.sum(jnp.where(is_member, starts[None, :], 0), axis=1)
        return segment, is_member.astype(F32), position

    rolled_rows = (jnp.arange(group_rows, dtype=jnp.int32) + offset) % group_rows
    segment, member_rolled, position = layout(rolled_rows)
    half = HEAD_DIM // 2
    frequency = jnp.exp(jnp.arange(half, dtype=F32) * (-2.0 * math.log(10000.0) / HEAD_DIM))
    angles = frequency[:, None] * position.astype(F32)[None, :]
    cos_t, sin_t = jnp.cos(angles), jnp.sin(angles)
    seg_tail = segment[LONGEST:]
    seg_col, seg_row = seg_tail[:, None], seg_tail[None, :]
    own_rows = my_row * row_count + jnp.arange(row_count, dtype=jnp.int32)
    _, member, _ = layout(own_rows)

    col_part = lambda w, j: lax.dynamic_slice_in_dim(w, (my_row ^ j) * width, width, 1)
    q_parts, k_parts, v_parts = (
        [col_part(w, j) for j in range(4)] for w in (query_weight, key_weight, value_weight)
    )
    weight_t = jnp.concatenate([q_parts[0].T, k_parts[0].T, v_parts[0].T], 0)
    own_part = lambda b: lax.dynamic_slice_in_dim(b, my_row * width, width, 0)
    bias_t = jnp.concatenate([own_part(query_bias), own_part(key_bias), own_part(value_bias)])[:, None]
    back_weight = jnp.concatenate(
        [
            part[j][:, pair * 128 : (pair + 1) * 128]
            for pair in range(2)
            for j in range(4)
            for part in (q_parts, k_parts, v_parts)
        ],
        1,
    )
    out_perm = jnp.concatenate(
        [lax.dynamic_slice_in_dim(out_weight, (my_row ^ j) * width, width, 0) for j in range(4)], 0
    )

    embedding = time_embed[0]
    act_low = jax.nn.silu(embedding).astype(BF)
    modulation = jnp.dot(act_low, mod_weight, preferred_element_type=F32) + mod_bias
    mod_long = lax.dynamic_slice_in_dim(modulation[:, : 2 * D], longest, 1, 0)
    act_all = act_low
    for bit in bits_of(n_grp):
        act_all = jnp.concatenate([act_all, exchange(act_all, "grp", bit)], 0)

    mixed, qt, kt, vt, k_rows, v_rows = project(
        place, (frames, from_core, from_x, from_both), modulation[:, : 2 * D], mod_long,
        member_rolled[LONGEST:], weight_t, bias_t, cos_t, sin_t,
    )

    heads_t, log_totals, pieces = [], [], []
    for pair in range(2):
        ot, lse, *outs = attend(place, pair, qt, k_rows, vt, seg_col, seg_row)
        heads_t.append(ot)
        log_totals.append(lse)
        pieces.append([outs[0]] + [exchange(outs[j], "row", j) for j in range(1, 4)])
    attn_low = jnp.concatenate([pieces[pair][j] for j in range(4) for pair in range(2)], 1)

    per_token = jnp.dot(member, modulation, precision=highest, preferred_element_type=F32)
    shift_attn, scale_attn, gate_attn, shift_ffn, scale_ffn, gate_ffn = jnp.split(per_token, 6, axis=1)
    residual = frames.astype(F32)
    normed_attn, factor_attn = normalize(residual)
    attended = jnp.dot(attn_low, out_perm, preferred_element_type=F32) + out_bias
    middle = residual + gate_attn * attended
    normed_ffn, factor_ffn = normalize(middle)
    ffn_in = (normed_ffn * (1.0 + scale_ffn) + shift_ffn).astype(BF)
    hidden = jnp.dot(ffn_in, up_weight, preferred_element_type=F32) + up_bias
    active_low = jax.nn.gelu(hidden, approximate=True).astype(BF)
    branch = jnp.dot(active_low, down_weight, preferred_element_type=F32) + down_bias
    output = (middle + gate_ffn * branch).astype(BF)
    upstream = cotangent.astype(F32)
    grad_branch = (upstream * gate_ffn).astype(BF)
    grad_gate_ffn = upstream * branch
    grad_active = against(grad_branch, down_weight)
    _, gelu_pull = jax.vjp(lambda tensor: jax.nn.gelu(tensor, approximate=True), hidden)
    grad_hidden = gelu_pull(grad_active)[0].astype(BF)
    grad_ffn_in = against(grad_hidden, up_weight)
    grad_scale_ffn = grad_ffn_in * normed_ffn
    grad_middle = upstream + normalize_back(grad_ffn_in * (1.0 + scale_ffn), normed_ffn, factor_ffn)
    grad_attended = (grad_middle * gate_attn).astype(BF)
    grad_gate_attn = grad_middle * attended
    grad_heads = against(grad_attended, out_perm).astype(BF)

    grad_pieces = []
    for pair in range(2):
        cut = [
            grad_heads[:, j * width + pair * 128 : j * width + pair * 128 + 128] for j in range(4)
        ]
        grad_pieces.append([cut[0]] + [exchange(cut[j], "row", j) for j in range(1, 4)])

    operands = (attn_low, ffn_in, active_low, grad_attended, grad_hidden, grad_branch)
    to_core = exchange(weight_grads(place, (1, 3), *operands), "row", 1)
    packed = add_low(weight_grads(place, (0, 2), *operands), to_core)
    cut_row = packed.shape[1] // 2
    upper = add_low(packed[0, :cut_row], exchange(packed[1, :cut_row], "row", 2))
    lower = packed[:, cut_row:]
    for bit in bits_of(n_grp):
        upper = halve(upper, 0, bit)
        lower = halve(lower, 1, bit)
    lower = add_low(lower[0], exchange(lower[1], "row", 2))
    for bit in reversed(bits_of(n_grp)):
        upper = grow(upper, 0, bit)
        lower = grow(lower, 0, bit)
    packed_total = jnp.concatenate([upper, lower], 0).astype(F32)
    out_grad = packed_total[:256]
    up_grad = jnp.concatenate([packed_total[256:512], packed_total[512:768]], 1)
    down_grad = packed_total[768:]

    back_pieces, qkv_grads, qkv_bias = [], [], []
    for pair in range(2):
        rolled, sums, *outs = attend_back(
            place, pair, qt, k_rows, kt, v_rows, heads_t[pair], log_totals[pair], grad_pieces[pair],
            seg_col, seg_row, cos_t, sin_t,
        )
        back_pieces += [outs[0]] + [exchange(outs[j], "row", j) for j in range(1, 4)]
        qkv_bias.append(sums[0].reshape(3, 128))
        total = contract_rows(mixed, rolled).astype(BF).reshape(4, width, 384)
        for bit in bits_of(n_grp):
            total = halve(total, 1, bit)
        shard = lambda j: lax.dynamic_index_in_dim(total, my_row ^ j, 0, keepdims=False)
        total = jnp.stack([shard(0)] + [exchange(shard(j), "row", j) for j in range(1, 4)])
        for bit in reversed(bits_of(n_grp)):
            total = grow(total, 1, bit)
        qkv_grads.append(total)
    by_owner = jnp.stack(qkv_grads)[:, my_row ^ jnp.arange(4)]
    qkv_full = by_owner.transpose(2, 1, 0, 3).reshape(width, 4, 2, 3, 128).astype(F32)
    query_grad, key_grad, value_grad = (qkv_full[:, :, :, i].reshape(width, D) for i in range(3))

    grad_mixed_in = against(jnp.concatenate(back_pieces, 1), back_weight)
    grad_frames = grad_middle + normalize_back(
        grad_mixed_in * (1.0 + scale_attn), normed_attn, factor_attn
    )

    def by_utterance(parts):
        return lax.dot_general(
            member,
            jnp.concatenate(parts, 1),
            (((0,), (0,)), ((), ())),
            precision=highest,
            preferred_element_type=F32,
        )

    def group_sum(tensor):
        for bit in (1, 2):
            tensor = tensor + exchange(tensor, "row", bit)
        return tensor

    late = group_sum(by_utterance([grad_mixed_in, grad_mixed_in * normed_attn]))
    early = group_sum(
        by_utterance([grad_gate_attn, grad_ffn_in, grad_scale_ffn, grad_gate_ffn])
    )
    grad_modulation = jnp.concatenate([late, early], 1).astype(BF)
    grad_activated = against(grad_modulation, mod_weight)
    _, silu_pull = jax.vjp(jax.nn.silu, embedding)
    grad_embedding = silu_pull(grad_activated)[0]
    mod_all = grad_modulation
    for bit in bits_of(n_grp):
        mod_all = jnp.concatenate([mod_all, exchange(mod_all, "grp", bit)], 0)
    act_slice = lax.dynamic_slice_in_dim(act_all, my_row * width, width, 1)
    mod_weight_grad = contract_rows(act_slice, mod_all)
    mod_bias_grad = lax.dynamic_slice_in_dim(column_sum(mod_all), my_row * 6 * width, 6 * width, 0)

    ffn_bias = group_sum(
        jnp.concatenate([column_sum(grad_attended), column_sum(grad_hidden), column_sum(grad_branch)])
    )
    mine = lambda start, size: lax.dynamic_slice_in_dim(ffn_bias, start + my_row * size, size, 0)
    qkv_sum = jnp.stack(qkv_bias, 1).reshape(3 * width)
    biases = jnp.concatenate([qkv_sum, mine(0, width), mine(D, 2 * width), mine(3 * D, width)])
    for bit in bits_of(n_grp):
        biases = biases + exchange(biases, "grp", bit)
    query_b, key_b, value_b, out_b, up_b, down_b = jnp.split(
        biases, [width, 2 * width, 3 * width, 4 * width, 6 * width]
    )
    return (
        output,
        grad_frames.astype(BF),
        grad_embedding[None],
        mod_weight_grad,
        mod_bias_grad,
        query_grad,
        query_b,
        key_grad,
        key_b,
        value_grad,
        value_b,
        out_grad,
        out_b,
        up_grad,
        up_b,
        down_grad,
        down_b,
    )


def solution(mesh):
    placed = (
        (P(("grp", "row"), None), P("grp", None, None), P("grp", None))
        + (P(),) * 14
        + (P(("grp", "row"), None),)
    )
    return jax.shard_map(
        local,
        mesh=mesh,
        in_specs=placed,
        out_specs=(
            P(("grp", "row"), None),
            P(("grp", "row"), None),
            P("grp", None, None),
        )
        + (P("row", None), P("row")) * 7,
        check_vma=False,
    )
```

```python
import functools
import math

import jax
import jax.numpy as jnp
from jax import lax
from jax.experimental import pallas as pl
from jax.experimental.pallas import tpu as pltpu
from jax.sharding import PartitionSpec as P

D = 1024
HEADS = 16
HEAD_DIM = 64
LONGEST = 1792
TILE = 256
BF = jnp.bfloat16
F32 = jnp.float32

highest = lax.Precision.HIGHEST
VMEM = pltpu.VMEM
SMEM = pltpu.SMEM
LIMIT = 60 << 20
MESH = pl.DeviceIdType.MESH


def matdot(left, right, left_dim, right_dim):
    return lax.dot_general(
        left, right, (((left_dim,), (right_dim,)), ((), ())), preferred_element_type=F32
    )


def contract_rows(left, right):
    return matdot(left, right, 0, 0)


def against(left, weight):
    return matdot(left, weight, 1, 1)


def column_sum(tensor):
    return jnp.sum(tensor.astype(F32), axis=0)


def normalize(tensor):
    centred = tensor - jnp.mean(tensor, axis=-1, keepdims=True)
    factor = lax.rsqrt(jnp.mean(centred * centred, axis=-1, keepdims=True) + 1e-06)
    return (centred * factor, factor)


def normalize_back(grad_normed, normed, factor):
    mean_grad = jnp.mean(grad_normed, axis=-1, keepdims=True)
    mean_cross = jnp.mean(grad_normed * normed, axis=-1, keepdims=True)
    return (grad_normed - mean_grad - normed * mean_cross) * factor


def exchange(tensor, axis, bit):
    size = lax.axis_size(axis)
    return lax.ppermute(tensor, axis, [(i, i ^ bit) for i in range(size)])


def add_low(left, right):
    return (left.astype(F32) + right.astype(F32)).astype(BF)


def grp_bit(bit):
    return (lax.axis_index("grp") // bit) % 2


def halve(tensor, dim, bit):
    side = grp_bit(bit)
    half = tensor.shape[dim] // 2
    send = lax.dynamic_slice_in_dim(tensor, (1 - side) * half, half, dim)
    keep = lax.dynamic_slice_in_dim(tensor, side * half, half, dim)
    return add_low(keep, exchange(send, "grp", bit))


def grow(tensor, dim, bit):
    other = exchange(tensor, "grp", bit)
    return jnp.where(
        grp_bit(bit) == 0,
        jnp.concatenate([tensor, other], dim),
        jnp.concatenate([other, tensor], dim),
    )


def bits_of(count):
    return [1 << i for i in range(count.bit_length() - 1)]


def roll_matrix(offset):
    row = lax.broadcasted_iota(jnp.int32, (TILE, 2 * TILE), 0)
    col = lax.broadcasted_iota(jnp.int32, (TILE, 2 * TILE), 1)
    return (col == row + offset).astype(F32).astype(BF)


def project_kernel(
    place, x0, x1, x2, x3, mod_all, mod_long, member, weight_t, bias, cos_t, sin_t,
    mixed_out, qt_out, kt_out, vt_out, k_out, v_out, rows_ref, roll_ref,
):
    step = pl.program_id(0)
    block = x0.shape[0]
    total = 4 * block

    @pl.when(step == 0)
    def _():
        for j, source in enumerate((x0, x1, x2, x3)):
            at = pl.multiple_of((place[0] ^ j) * block, block)
            rows_ref[pl.ds(at, block), :] = source[...]
        rows_ref[pl.ds(total, TILE), :] = rows_ref[pl.ds(0, TILE), :]
        roll_ref[...] = roll_matrix(place[1])

    pair = rows_ref[pl.ds(pl.multiple_of(step * TILE, TILE), 2 * TILE), :]
    normed, _ = normalize(matdot(roll_ref[...], pair, 1, 0))
    last = step == total // TILE - 1

    @pl.when(jnp.logical_not(last))
    def _():
        mixed_out[...] = (normed * (1.0 + mod_long[:, D:]) + mod_long[:, :D]).astype(BF)

    @pl.when(last)
    def _():
        per_row = jnp.zeros((TILE, 2 * D), F32)
        for u in range(mod_all.shape[0]):
            per_row = per_row + member[:, u : u + 1] * mod_all[u : u + 1, :]
        mixed_out[...] = (normed * (1.0 + per_row[:, D:]) + per_row[:, :D]).astype(BF)

    wide = matdot(weight_t[...], mixed_out[...], 1, 1) + bias[...]
    cosine, sine = cos_t[...], sin_t[...]
    half = HEAD_DIM // 2
    width = qt_out.shape[0]

    def turned(base):
        parts = []
        for at in range(base, base + width, HEAD_DIM):
            first, second = wide[at : at + half], wide[at + half : at + HEAD_DIM]
            parts.append(first * cosine - second * sine)
            parts.append(second * cosine + first * sine)
        return jnp.concatenate(parts, 0)

    keys = turned(width)
    values = wide[2 * width :]
    qt_out[...] = turned(0).astype(BF) * jnp.asarray(HEAD_DIM**-0.5, BF)
    kt_out[...] = keys.astype(BF)
    vt_out[...] = values.astype(BF)
    k_out[...] = keys.T.astype(BF)
    v_out[...] = values.T.astype(BF)


def project(place, blocks, mod_all, mod_long, member, weight_t, bias, cos_t, sin_t):
    block = blocks[0].shape[0]
    total = 4 * block
    width = weight_t.shape[0] // 3
    whole = lambda a: pl.BlockSpec(a.shape, lambda i: (0, 0))
    rows = lambda n: pl.BlockSpec((TILE, n), lambda i: (i, 0))
    cols = lambda n: pl.BlockSpec((n, TILE), lambda i: (0, i))
    return pl.pallas_call(
        project_kernel,
        grid=(total // TILE,),
        out_shape=[
            jax.ShapeDtypeStruct((total, D), BF),
            jax.ShapeDtypeStruct((width, total), BF),
            jax.ShapeDtypeStruct((width, total), BF),
            jax.ShapeDtypeStruct((width, total), BF),
            jax.ShapeDtypeStruct((total, width), BF),
            jax.ShapeDtypeStruct((total, width), BF),
        ],
        in_specs=[pl.BlockSpec(memory_space=SMEM)]
        + [whole(a) for a in blocks]
        + [whole(mod_all), whole(mod_long), whole(member), whole(weight_t), whole(bias)]
        + [cols(HEAD_DIM // 2), cols(HEAD_DIM // 2)],
        out_specs=[rows(D), cols(width), cols(width), cols(width), rows(width), rows(width)],
        scratch_shapes=[VMEM((total + TILE, D), BF), VMEM((TILE, 2 * TILE), BF)],
        compiler_params=pltpu.CompilerParams(vmem_limit_bytes=LIMIT),
        cost_estimate=pl.CostEstimate(
            flops=2 * total * D * 3 * width, bytes_accessed=16 << 20, transcendentals=total
        ),
        name="project",
    )(place, *blocks, mod_all, mod_long, member, weight_t, bias, cos_t, sin_t)


def one_head(pair, head):
    part = pair[head * HEAD_DIM : (head + 1) * HEAD_DIM]
    empty = jnp.zeros_like(part)
    return jnp.concatenate([part, empty] if head == 0 else [empty, part], 0)


def unroll(outs, rolled_ref, my_row, offset, block):
    total = 4 * block
    rolled_ref[:, pl.ds(0, TILE)] = rolled_ref[:, pl.ds(total, TILE)]
    back = roll_matrix(TILE - offset)
    for j, out in enumerate(outs):
        for part in range(block // TILE):
            at = pl.multiple_of((my_row ^ j) * block + part * TILE, TILE)
            rows = matdot(back, rolled_ref[:, pl.ds(at, 2 * TILE)], 1, 1)
            out[part * TILE : (part + 1) * TILE, :] = rows.astype(BF)


def attend_kernel(
    place, qt, k, vt, seg_col, seg_row, ot_out, lse_out, o0, o1, o2, o3, rolled_ref
):
    step = pl.program_id(0)
    total = k.shape[0]
    block = total // 4
    last = step == total // TILE - 1

    def run(first, count, allowed):
        outs, tops = [], []
        for head in range(2):
            scores = matdot(k[pl.ds(first, count), :], one_head(qt[...], head), 1, 0)
            if allowed is not None:
                scores = jnp.where(allowed, scores, -1e30)
            top = jnp.max(scores, axis=0, keepdims=True)
            weights = jnp.exp(scores - top)
            exp_sum = jnp.sum(weights, axis=0, keepdims=True)
            mixed = matdot(
                vt[head * HEAD_DIM : (head + 1) * HEAD_DIM, pl.ds(first, count)],
                weights.astype(BF),
                1,
                0,
            )
            outs.append(mixed / exp_sum)
            tops.append(top + jnp.log(exp_sum))
        mixed = jnp.concatenate(outs, 0)
        low = mixed.astype(BF)
        ot_out[...] = low
        lse_out[...] = jnp.concatenate(tops * 4, 0)
        rolled_ref[:, pl.ds(pl.multiple_of(TILE + step * TILE, TILE), TILE)] = low

    @pl.when(jnp.logical_not(last))
    def _():
        run(0, LONGEST, None)

    @pl.when(last)
    def _():
        run(LONGEST, total - LONGEST, seg_col[...] == seg_row[...])
        unroll((o0, o1, o2, o3), rolled_ref, place[0], place[1], block)


def attend(place, pair, qt, k, vt, seg_col, seg_row):
    total = k.shape[0]
    block = total // 4
    whole = lambda a: pl.BlockSpec(a.shape, lambda i: (0, 0))
    return pl.pallas_call(
        attend_kernel,
        grid=(total // TILE,),
        out_shape=[
            jax.ShapeDtypeStruct((128, total), BF),
            jax.ShapeDtypeStruct((8, total), F32),
        ]
        + [jax.ShapeDtypeStruct((block, 128), BF)] * 4,
        in_specs=[
            pl.BlockSpec(memory_space=SMEM),
            pl.BlockSpec((128, TILE), lambda i: (pair, i)),
            pl.BlockSpec((total, 128), lambda i: (0, pair)),
            pl.BlockSpec((128, total), lambda i: (pair, 0)),
            whole(seg_col),
            whole(seg_row),
        ],
        out_specs=[
            pl.BlockSpec((128, TILE), lambda i: (0, i)),
            pl.BlockSpec((8, TILE), lambda i: (0, i)),
        ]
        + [pl.BlockSpec((block, 128), lambda i: (0, 0))] * 4,
        scratch_shapes=[VMEM((128, total + TILE), BF)],
        compiler_params=pltpu.CompilerParams(vmem_limit_bytes=LIMIT),
        cost_estimate=pl.CostEstimate(
            flops=2 * 2 * 2 * total * LONGEST * 256,
            bytes_accessed=4 << 20,
            transcendentals=2 * total * LONGEST,
        ),
        name="attend",
    )(place, qt, k, vt, seg_col, seg_row)


def attend_back_kernel(
    place, qt, k, kt, v, ot, lse, g0, g1, g2, g3, seg_col, seg_row, cos_t, sin_t,
    rolled_out, bias_out, s0, r1, r2, r3,
    grad_rows, grad_t, row_dots, dqt, dkt, dvt, nat_ref, s1, s2, s3, send_sem, recv_sem,
):
    step = pl.program_id(0)
    my_row = lax.axis_index("row")
    there = lambda j: {"row": my_row ^ j}
    total = k.shape[0]
    block = total // 4
    steps = total // TILE
    last = step == steps - 1
    half = HEAD_DIM // 2

    @pl.when(step == 0)
    def _():
        for j, source in enumerate((g0, g1, g2, g3)):
            at = pl.multiple_of((my_row ^ j) * block, block)
            grad_rows[pl.ds(at, block), :] = source[...]
        grad_rows[pl.ds(total, TILE), :] = grad_rows[pl.ds(0, TILE), :]
        barrier = pltpu.get_barrier_semaphore()
        for j in range(1, 4):
            pl.semaphore_signal(barrier, inc=1, device_id=there(j), device_id_type=MESH)
        pl.semaphore_wait(barrier, 3)
        dkt[...] = jnp.zeros_like(dkt)
        dvt[...] = jnp.zeros_like(dvt)

        ahead = roll_matrix(place[1])

        def turn(i, carry):
            cols = pl.ds(pl.multiple_of(i * TILE, TILE), TILE)
            two = grad_rows[pl.ds(pl.multiple_of(i * TILE, TILE), 2 * TILE), :]
            part = matdot(ahead, two, 1, 0).T
            grad_t[:, cols] = part.astype(BF)
            crossed = part * ot[:, cols].astype(F32)
            row_dots[0:1, cols] = jnp.sum(crossed[:HEAD_DIM], axis=0, keepdims=True)
            row_dots[1:2, cols] = jnp.sum(crossed[HEAD_DIM:], axis=0, keepdims=True)
            return carry

        lax.fori_loop(0, steps, turn, 0)

    here = pl.ds(pl.multiple_of(step * TILE, TILE), TILE)

    def run(first, count, allowed):
        keys = pl.ds(first, count)
        for head in range(2):
            mine = slice(head * HEAD_DIM, (head + 1) * HEAD_DIM)
            scores = matdot(k[keys, :], one_head(qt[:, here], head), 1, 0)
            if allowed is not None:
                scores = jnp.where(allowed, scores, -1e30)
            probs = jnp.exp(scores - lse[head : head + 1, here])
            grad_probs = matdot(v[keys, :], one_head(grad_t[:, here], head), 1, 0)
            grad_scores = (probs * (grad_probs - row_dots[head : head + 1, here])).astype(BF)
            dqt[mine, here] = matdot(kt[mine, keys], grad_scores, 1, 0) * HEAD_DIM**-0.5
            dkt[mine, keys] += matdot(qt[mine, here], grad_scores, 1, 1)
            dvt[mine, keys] += matdot(grad_t[mine, here], probs.astype(BF), 1, 1)

    @pl.when(jnp.logical_not(last))
    def _():
        run(0, LONGEST, None)

    @pl.when(last)
    def _():
        run(LONGEST, total - LONGEST, seg_col[...] == seg_row[...])

        def finish(i, sums):
            cols = pl.ds(pl.multiple_of(i * TILE, TILE), TILE)
            cosine, sine = cos_t[:, cols], sin_t[:, cols]

            def turned(ref):
                parts = []
                for at in range(0, 128, HEAD_DIM):
                    first, second = ref[at : at + half, cols], ref[at + half : at + HEAD_DIM, cols]
                    parts.append(first * cosine + second * sine)
                    parts.append(second * cosine - first * sine)
                return jnp.concatenate(parts, 0)

            columns = jnp.concatenate([turned(dqt), turned(dkt), dvt[:, cols]], 0)
            nat_ref[:, pl.ds(pl.multiple_of(TILE + i * TILE, TILE), TILE)] = columns.astype(BF)
            low = columns.T.astype(BF)
            rolled_out[cols, :] = low
            return sums + jnp.sum(low.astype(F32), axis=0, keepdims=True)

        sums = lax.fori_loop(0, steps, finish, jnp.zeros((1, 384), F32))
        bias_out[...] = jnp.broadcast_to(sums, bias_out.shape)
        unroll((s0, s1, s2, s3), nat_ref, my_row, place[1], block)
        copies = [
            pltpu.make_async_remote_copy(
                src, dst, send_sem.at[j], recv_sem.at[j], device_id=there(j + 1), device_id_type=MESH
            )
            for j, (src, dst) in enumerate(((s1, r1), (s2, r2), (s3, r3)))
        ]
        for copy in copies:
            copy.start()
        for copy in copies:
            copy.wait()


def attend_back(place, pair, qt, k, kt, v, ot, lse, grads, seg_col, seg_row, cos_t, sin_t):
    total = k.shape[0]
    block = total // 4
    whole = lambda a: pl.BlockSpec(a.shape, lambda i: (0, 0))
    wide = pl.BlockSpec((128, total), lambda i: (pair, 0))
    tall = pl.BlockSpec((total, 128), lambda i: (0, pair))
    return pl.pallas_call(
        attend_back_kernel,
        grid=(total // TILE,),
        out_shape=[
            jax.ShapeDtypeStruct((total, 384), BF),
            jax.ShapeDtypeStruct((8, 384), F32),
        ]
        + [jax.ShapeDtypeStruct((block, 384), BF)] * 4,
        in_specs=[
            pl.BlockSpec(memory_space=SMEM),
            wide,
            tall,
            wide,
            tall,
            whole(ot),
            whole(lse),
        ]
        + [whole(g) for g in grads]
        + [whole(seg_col), whole(seg_row), whole(cos_t), whole(sin_t)],
        out_specs=[
            pl.BlockSpec((total, 384), lambda i: (0, 0)),
            pl.BlockSpec((8, 384), lambda i: (0, 0)),
        ]
        + [pl.BlockSpec((block, 384), lambda i: (0, 0))]
        + [pl.BlockSpec(memory_space=pl.ANY)] * 3,
        scratch_shapes=[
            VMEM((total + TILE, 128), BF),
            VMEM((128, total), BF),
            VMEM((8, total), F32),
            VMEM((128, total), F32),
            VMEM((128, total), F32),
            VMEM((128, total), F32),
            VMEM((384, total + TILE), BF),
            VMEM((block, 384), BF),
            VMEM((block, 384), BF),
            VMEM((block, 384), BF),
            pltpu.SemaphoreType.DMA((3,)),
            pltpu.SemaphoreType.DMA((3,)),
        ],
        compiler_params=pltpu.CompilerParams(
            vmem_limit_bytes=LIMIT, collective_id=1 + pair, has_side_effects=True
        ),
        cost_estimate=pl.CostEstimate(
            flops=2 * 2 * 5 * total * LONGEST * 256,
            bytes_accessed=8 << 20,
            transcendentals=2 * total * LONGEST,
        ),
        name=f"attend_back{pair}",
    )(place, qt, k, kt, v, ot, lse, *grads, seg_col, seg_row, cos_t, sin_t)


def weight_grad_kernel(place, o, h, a, e_att, e_z, e_b, out):
    out[0, :256] = contract_rows(o[...], e_att[...]).astype(BF)
    out[0, 256:512] = contract_rows(h[...], e_z[:, :D]).astype(BF)
    out[0, 512:768] = contract_rows(h[...], e_z[:, D:]).astype(BF)
    out[0, 768:] = contract_rows(a[...], e_b[...]).astype(BF)


def weight_grads(place, order, o, h, a, e_att, e_z, e_b):
    rows = o.shape[0]
    first, second = order
    pick = lambda i: first + i * (second - first)
    whole = lambda t: pl.BlockSpec(t.shape, lambda i, p: (0, 0))
    return pl.pallas_call(
        weight_grad_kernel,
        grid_spec=pltpu.PrefetchScalarGridSpec(
            num_scalar_prefetch=1,
            grid=(2,),
            in_specs=[
                pl.BlockSpec((rows, 256), lambda i, p: (0, pick(i))),
                pl.BlockSpec((rows, 256), lambda i, p: (0, p[0] ^ pick(i))),
                pl.BlockSpec((rows, 512), lambda i, p: (0, p[0] ^ pick(i))),
                whole(e_att),
                whole(e_z),
                whole(e_b),
            ],
            out_specs=pl.BlockSpec((1, 1280, D), lambda i, p: (i, 0, 0)),
        ),
        out_shape=jax.ShapeDtypeStruct((2, 1280, D), BF),
        compiler_params=pltpu.CompilerParams(vmem_limit_bytes=LIMIT),
        cost_estimate=pl.CostEstimate(
            flops=2 * 2 * rows * 1280 * D, bytes_accessed=12 << 20, transcendentals=0
        ),
        name="weight_grads",
    )(place, o, h, a, e_att, e_z, e_b)


def local(
    frames, time_embed, lengths, mod_weight, mod_bias, query_weight, query_bias, key_weight, key_bias,
    value_weight, value_bias, out_weight, out_bias, up_weight, up_bias, down_weight, down_bias, cotangent,
):
    n_grp = lax.axis_size("grp")
    row_count = frames.shape[0]
    my_row = lax.axis_index("row")
    group_rows = row_count * lax.axis_size("row")
    width = D // 4

    from_core = exchange(frames, "row", 1)
    from_x = exchange(frames, "row", 2)
    from_both = exchange(from_x, "row", 1)

    utt_sizes = lengths[0]
    finish = jnp.cumsum(utt_sizes)
    starts = finish - utt_sizes
    longest = jnp.argmax(utt_sizes)
    offset = starts[longest]
    place = jnp.stack([my_row, offset]).astype(jnp.int32)
    utts = jnp.arange(utt_sizes.shape[0], dtype=jnp.int32)

    def layout(rows):
        segment = jnp.sum((rows[:, None] >= finish[None, :]).astype(jnp.int32), axis=1)
        is_member = segment[:, None] == utts[None, :]
        position = rows - jnp.sum(jnp.where(is_member, starts[None, :], 0), axis=1)
        return segment, is_member.astype(F32), position

    rolled_rows = (jnp.arange(group_rows, dtype=jnp.int32) + offset) % group_rows
    segment, member_rolled, position = layout(rolled_rows)
    half = HEAD_DIM // 2
    frequency = jnp.exp(jnp.arange(half, dtype=F32) * (-2.0 * math.log(10000.0) / HEAD_DIM))
    angles = frequency[:, None] * position.astype(F32)[None, :]
    cos_t, sin_t = jnp.cos(angles), jnp.sin(angles)
    seg_tail = segment[LONGEST:]
    seg_col, seg_row = seg_tail[:, None], seg_tail[None, :]
    own_rows = my_row * row_count + jnp.arange(row_count, dtype=jnp.int32)
    _, member, _ = layout(own_rows)

    col_part = lambda w, j: lax.dynamic_slice_in_dim(w, (my_row ^ j) * width, width, 1)
    q_parts, k_parts, v_parts = (
        [col_part(w, j) for j in range(4)] for w in (query_weight, key_weight, value_weight)
    )
    weight_t = jnp.concatenate([q_parts[0].T, k_parts[0].T, v_parts[0].T], 0)
    own_part = lambda b: lax.dynamic_slice_in_dim(b, my_row * width, width, 0)
    bias_t = jnp.concatenate([own_part(query_bias), own_part(key_bias), own_part(value_bias)])[:, None]
    back_weight = jnp.concatenate(
        [
            part[j][:, pair * 128 : (pair + 1) * 128]
            for pair in range(2)
            for j in range(4)
            for part in (q_parts, k_parts, v_parts)
        ],
        1,
    )
    out_perm = jnp.concatenate(
        [lax.dynamic_slice_in_dim(out_weight, (my_row ^ j) * width, width, 0) for j in range(4)], 0
    )

    embedding = time_embed[0]
    act_low = jax.nn.silu(embedding).astype(BF)
    modulation = jnp.dot(act_low, mod_weight, preferred_element_type=F32) + mod_bias
    mod_long = lax.dynamic_slice_in_dim(modulation[:, : 2 * D], longest, 1, 0)
    act_all = act_low
    for bit in bits_of(n_grp):
        act_all = jnp.concatenate([act_all, exchange(act_all, "grp", bit)], 0)

    mixed, qt, kt, vt, k_rows, v_rows = project(
        place, (frames, from_core, from_x, from_both), modulation[:, : 2 * D], mod_long,
        member_rolled[LONGEST:], weight_t, bias_t, cos_t, sin_t,
    )

    heads_t, log_totals, pieces = [], [], []
    for pair in range(2):
        ot, lse, *outs = attend(place, pair, qt, k_rows, vt, seg_col, seg_row)
        heads_t.append(ot)
        log_totals.append(lse)
        pieces.append([outs[0]] + [exchange(outs[j], "row", j) for j in range(1, 4)])
    attn_low = jnp.concatenate([pieces[pair][j] for j in range(4) for pair in range(2)], 1)

    per_token = jnp.dot(member, modulation, precision=highest, preferred_element_type=F32)
    shift_attn, scale_attn, gate_attn, shift_ffn, scale_ffn, gate_ffn = jnp.split(per_token, 6, axis=1)
    residual = frames.astype(F32)
    normed_attn, factor_attn = normalize(residual)
    attended = jnp.dot(attn_low, out_perm, preferred_element_type=F32) + out_bias
    middle = residual + gate_attn * attended
    normed_ffn, factor_ffn = normalize(middle)
    ffn_in = (normed_ffn * (1.0 + scale_ffn) + shift_ffn).astype(BF)
    hidden = jnp.dot(ffn_in, up_weight, preferred_element_type=F32) + up_bias
    active_low = jax.nn.gelu(hidden, approximate=True).astype(BF)
    branch = jnp.dot(active_low, down_weight, preferred_element_type=F32) + down_bias
    output = (middle + gate_ffn * branch).astype(BF)
    upstream = cotangent.astype(F32)
    grad_branch = (upstream * gate_ffn).astype(BF)
    grad_gate_ffn = upstream * branch
    grad_active = against(grad_branch, down_weight)
    _, gelu_pull = jax.vjp(lambda tensor: jax.nn.gelu(tensor, approximate=True), hidden)
    grad_hidden = gelu_pull(grad_active)[0].astype(BF)
    grad_ffn_in = against(grad_hidden, up_weight)
    grad_scale_ffn = grad_ffn_in * normed_ffn
    grad_middle = upstream + normalize_back(grad_ffn_in * (1.0 + scale_ffn), normed_ffn, factor_ffn)
    grad_attended = (grad_middle * gate_attn).astype(BF)
    grad_gate_attn = grad_middle * attended
    grad_heads = against(grad_attended, out_perm).astype(BF)

    grad_pieces = []
    for pair in range(2):
        cut = [
            grad_heads[:, j * width + pair * 128 : j * width + pair * 128 + 128] for j in range(4)
        ]
        grad_pieces.append([cut[0]] + [exchange(cut[j], "row", j) for j in range(1, 4)])

    operands = (attn_low, ffn_in, active_low, grad_attended, grad_hidden, grad_branch)
    to_core = exchange(weight_grads(place, (1, 3), *operands), "row", 1)
    packed = add_low(weight_grads(place, (0, 2), *operands), to_core)
    cut_row = packed.shape[1] // 2
    upper = add_low(packed[0, :cut_row], exchange(packed[1, :cut_row], "row", 2))
    lower = packed[:, cut_row:]
    for bit in bits_of(n_grp):
        upper = halve(upper, 0, bit)
        lower = halve(lower, 1, bit)
    lower = add_low(lower[0], exchange(lower[1], "row", 2))
    for bit in reversed(bits_of(n_grp)):
        upper = grow(upper, 0, bit)
        lower = grow(lower, 0, bit)
    packed_total = jnp.concatenate([upper, lower], 0).astype(F32)
    out_grad = packed_total[:256]
    up_grad = jnp.concatenate([packed_total[256:512], packed_total[512:768]], 1)
    down_grad = packed_total[768:]

    back_pieces, qkv_grads, qkv_bias = [], [], []
    for pair in range(2):
        rolled, sums, *outs = attend_back(
            place, pair, qt, k_rows, kt, v_rows, heads_t[pair], log_totals[pair], grad_pieces[pair],
            seg_col, seg_row, cos_t, sin_t,
        )
        back_pieces += outs
        qkv_bias.append(sums[0].reshape(3, 128))
        total = contract_rows(mixed, rolled).astype(BF).reshape(4, width, 384)
        for bit in bits_of(n_grp):
            total = halve(total, 1, bit)
        shard = lambda j: lax.dynamic_index_in_dim(total, my_row ^ j, 0, keepdims=False)
        total = jnp.stack([shard(0)] + [exchange(shard(j), "row", j) for j in range(1, 4)])
        for bit in reversed(bits_of(n_grp)):
            total = grow(total, 1, bit)
        qkv_grads.append(total)
    by_owner = jnp.stack(qkv_grads)[:, my_row ^ jnp.arange(4)]
    qkv_full = by_owner.transpose(2, 1, 0, 3).reshape(width, 4, 2, 3, 128).astype(F32)
    query_grad, key_grad, value_grad = (qkv_full[:, :, :, i].reshape(width, D) for i in range(3))

    grad_mixed_in = against(jnp.concatenate(back_pieces, 1), back_weight)
    grad_frames = grad_middle + normalize_back(
        grad_mixed_in * (1.0 + scale_attn), normed_attn, factor_attn
    )

    def by_utterance(parts):
        return lax.dot_general(
            member,
            jnp.concatenate(parts, 1),
            (((0,), (0,)), ((), ())),
            precision=highest,
            preferred_element_type=F32,
        )

    def group_sum(tensor):
        for bit in (1, 2):
            tensor = tensor + exchange(tensor, "row", bit)
        return tensor

    late = group_sum(by_utterance([grad_mixed_in, grad_mixed_in * normed_attn]))
    early = group_sum(
        by_utterance([grad_gate_attn, grad_ffn_in, grad_scale_ffn, grad_gate_ffn])
    )
    grad_modulation = jnp.concatenate([late, early], 1).astype(BF)
    grad_activated = against(grad_modulation, mod_weight)
    _, silu_pull = jax.vjp(jax.nn.silu, embedding)
    grad_embedding = silu_pull(grad_activated)[0]
    mod_all = grad_modulation
    for bit in bits_of(n_grp):
        mod_all = jnp.concatenate([mod_all, exchange(mod_all, "grp", bit)], 0)
    act_slice = lax.dynamic_slice_in_dim(act_all, my_row * width, width, 1)
    mod_weight_grad = contract_rows(act_slice, mod_all)
    mod_bias_grad = lax.dynamic_slice_in_dim(column_sum(mod_all), my_row * 6 * width, 6 * width, 0)

    ffn_bias = group_sum(
        jnp.concatenate([column_sum(grad_attended), column_sum(grad_hidden), column_sum(grad_branch)])
    )
    mine = lambda start, size: lax.dynamic_slice_in_dim(ffn_bias, start + my_row * size, size, 0)
    qkv_sum = jnp.stack(qkv_bias, 1).reshape(3 * width)
    biases = jnp.concatenate([qkv_sum, mine(0, width), mine(D, 2 * width), mine(3 * D, width)])
    for bit in bits_of(n_grp):
        biases = biases + exchange(biases, "grp", bit)
    query_b, key_b, value_b, out_b, up_b, down_b = jnp.split(
        biases, [width, 2 * width, 3 * width, 4 * width, 6 * width]
    )
    return (
        output,
        grad_frames.astype(BF),
        grad_embedding[None],
        mod_weight_grad,
        mod_bias_grad,
        query_grad,
        query_b,
        key_grad,
        key_b,
        value_grad,
        value_b,
        out_grad,
        out_b,
        up_grad,
        up_b,
        down_grad,
        down_b,
    )


def solution(mesh):
    placed = (
        (P(("grp", "row"), None), P("grp", None, None), P("grp", None))
        + (P(),) * 14
        + (P(("grp", "row"), None),)
    )
    return jax.shard_map(
        local,
        mesh=mesh,
        in_specs=placed,
        out_specs=(
            P(("grp", "row"), None),
            P(("grp", "row"), None),
            P("grp", None, None),
        )
        + (P("row", None), P("row")) * 7,
        check_vma=False,
    )
```

```python
import functools
import math

import jax
import jax.numpy as jnp
from jax import lax
from jax.experimental import pallas as pl
from jax.experimental.pallas import tpu as pltpu
from jax.sharding import PartitionSpec as P

D = 1024
HEADS = 16
HEAD_DIM = 64
LONGEST = 1792
TILE = 256
BF = jnp.bfloat16
F32 = jnp.float32

highest = lax.Precision.HIGHEST
VMEM = pltpu.VMEM
SMEM = pltpu.SMEM
LIMIT = 60 << 20
MESH = pl.DeviceIdType.MESH
BACK_SPANS = [(0, 896), (896, 896)]


def matdot(left, right, left_dim, right_dim):
    return lax.dot_general(
        left, right, (((left_dim,), (right_dim,)), ((), ())), preferred_element_type=F32
    )


def contract_rows(left, right):
    return matdot(left, right, 0, 0)


def against(left, weight):
    return matdot(left, weight, 1, 1)


def column_sum(tensor):
    return jnp.sum(tensor.astype(F32), axis=0)


def normalize(tensor):
    centred = tensor - jnp.mean(tensor, axis=-1, keepdims=True)
    factor = lax.rsqrt(jnp.mean(centred * centred, axis=-1, keepdims=True) + 1e-06)
    return (centred * factor, factor)


def normalize_back(grad_normed, normed, factor):
    mean_grad = jnp.mean(grad_normed, axis=-1, keepdims=True)
    mean_cross = jnp.mean(grad_normed * normed, axis=-1, keepdims=True)
    return (grad_normed - mean_grad - normed * mean_cross) * factor


def exchange(tensor, axis, bit):
    size = lax.axis_size(axis)
    return lax.ppermute(tensor, axis, [(i, i ^ bit) for i in range(size)])


def add_low(left, right):
    return (left.astype(F32) + right.astype(F32)).astype(BF)


def bits_of(count):
    return [1 << i for i in range(count.bit_length() - 1)]


def roll_matrix(offset):
    row = lax.broadcasted_iota(jnp.int32, (TILE, 2 * TILE), 0)
    col = lax.broadcasted_iota(jnp.int32, (TILE, 2 * TILE), 1)
    return (col == row + offset).astype(F32).astype(BF)


def project_kernel(
    place, x0, x1, x2, x3, mod_all, mod_long, member, weight_t, bias, cos_t, sin_t,
    mixed_out, qt_out, kt_out, vt_out, k_out, v_out, rows_ref, roll_ref,
):
    step = pl.program_id(0)
    block = x0.shape[0]
    total = 4 * block

    @pl.when(step == 0)
    def _():
        for j, source in enumerate((x0, x1, x2, x3)):
            at = pl.multiple_of((place[0] ^ j) * block, block)
            rows_ref[pl.ds(at, block), :] = source[...]
        rows_ref[pl.ds(total, TILE), :] = rows_ref[pl.ds(0, TILE), :]
        roll_ref[...] = roll_matrix(place[1])

    pair = rows_ref[pl.ds(pl.multiple_of(step * TILE, TILE), 2 * TILE), :]
    normed, _ = normalize(matdot(roll_ref[...], pair, 1, 0))
    last = step == total // TILE - 1

    @pl.when(jnp.logical_not(last))
    def _():
        mixed_out[...] = (normed * (1.0 + mod_long[:, D:]) + mod_long[:, :D]).astype(BF)

    @pl.when(last)
    def _():
        per_row = jnp.zeros((TILE, 2 * D), F32)
        for u in range(mod_all.shape[0]):
            per_row = per_row + member[:, u : u + 1] * mod_all[u : u + 1, :]
        mixed_out[...] = (normed * (1.0 + per_row[:, D:]) + per_row[:, :D]).astype(BF)

    wide = matdot(weight_t[...], mixed_out[...], 1, 1) + bias[...]
    cosine, sine = cos_t[...], sin_t[...]
    half = HEAD_DIM // 2
    width = qt_out.shape[0]

    def turned(base):
        parts = []
        for at in range(base, base + width, HEAD_DIM):
            first, second = wide[at : at + half], wide[at + half : at + HEAD_DIM]
            parts.append(first * cosine - second * sine)
            parts.append(second * cosine + first * sine)
        return jnp.concatenate(parts, 0)

    keys = turned(width)
    values = wide[2 * width :]
    qt_out[...] = turned(0).astype(BF) * jnp.asarray(HEAD_DIM**-0.5, BF)
    kt_out[...] = keys.astype(BF)
    vt_out[...] = values.astype(BF)
    k_out[...] = keys.T.astype(BF)
    v_out[...] = values.T.astype(BF)


def project(place, blocks, mod_all, mod_long, member, weight_t, bias, cos_t, sin_t):
    block = blocks[0].shape[0]
    total = 4 * block
    width = weight_t.shape[0] // 3
    whole = lambda a: pl.BlockSpec(a.shape, lambda i: (0, 0))
    rows = lambda n: pl.BlockSpec((TILE, n), lambda i: (i, 0))
    cols = lambda n: pl.BlockSpec((n, TILE), lambda i: (0, i))
    return pl.pallas_call(
        project_kernel,
        grid=(total // TILE,),
        out_shape=[
            jax.ShapeDtypeStruct((total, D), BF),
            jax.ShapeDtypeStruct((width, total), BF),
            jax.ShapeDtypeStruct((width, total), BF),
            jax.ShapeDtypeStruct((width, total), BF),
            jax.ShapeDtypeStruct((total, width), BF),
            jax.ShapeDtypeStruct((total, width), BF),
        ],
        in_specs=[pl.BlockSpec(memory_space=SMEM)]
        + [whole(a) for a in blocks]
        + [whole(mod_all), whole(mod_long), whole(member), whole(weight_t), whole(bias)]
        + [cols(HEAD_DIM // 2), cols(HEAD_DIM // 2)],
        out_specs=[rows(D), cols(width), cols(width), cols(width), rows(width), rows(width)],
        scratch_shapes=[VMEM((total + TILE, D), BF), VMEM((TILE, 2 * TILE), BF)],
        compiler_params=pltpu.CompilerParams(vmem_limit_bytes=LIMIT),
        cost_estimate=pl.CostEstimate(
            flops=2 * total * D * 3 * width, bytes_accessed=16 << 20, transcendentals=total
        ),
        name="project",
    )(place, *blocks, mod_all, mod_long, member, weight_t, bias, cos_t, sin_t)


def one_head(pair, head):
    part = pair[head * HEAD_DIM : (head + 1) * HEAD_DIM]
    empty = jnp.zeros_like(part)
    return jnp.concatenate([part, empty] if head == 0 else [empty, part], 0)


def unroll(outs, rolled_ref, my_row, offset, block):
    total = 4 * block
    rolled_ref[:, pl.ds(0, TILE)] = rolled_ref[:, pl.ds(total, TILE)]
    back = roll_matrix(TILE - offset)
    for j, out in enumerate(outs):
        for part in range(block // TILE):
            at = pl.multiple_of((my_row ^ j) * block + part * TILE, TILE)
            rows = matdot(back, rolled_ref[:, pl.ds(at, 2 * TILE)], 1, 1)
            out[part * TILE : (part + 1) * TILE, :] = rows.astype(BF)


def attend_kernel(
    place, qt, k, vt, seg_col, seg_row, ot_out, lse_out, o0, o1, o2, o3, rolled_ref
):
    step = pl.program_id(0)
    total = k.shape[0]
    block = total // 4
    last = step == total // TILE - 1

    def run(first, count, allowed):
        outs, tops = [], []
        for head in range(2):
            scores = matdot(k[pl.ds(first, count), :], one_head(qt[...], head), 1, 0)
            if allowed is not None:
                scores = jnp.where(allowed, scores, -1e30)
            top = jnp.max(scores, axis=0, keepdims=True)
            weights = jnp.exp(scores - top)
            exp_sum = jnp.sum(weights, axis=0, keepdims=True)
            mixed = matdot(
                vt[head * HEAD_DIM : (head + 1) * HEAD_DIM, pl.ds(first, count)],
                weights.astype(BF),
                1,
                0,
            )
            outs.append(mixed / exp_sum)
            tops.append(top + jnp.log(exp_sum))
        mixed = jnp.concatenate(outs, 0)
        low = mixed.astype(BF)
        ot_out[...] = low
        lse_out[...] = jnp.concatenate(tops * 4, 0)
        rolled_ref[:, pl.ds(pl.multiple_of(TILE + step * TILE, TILE), TILE)] = low

    @pl.when(jnp.logical_not(last))
    def _():
        run(0, LONGEST, None)

    @pl.when(last)
    def _():
        run(LONGEST, total - LONGEST, seg_col[...] == seg_row[...])
        unroll((o0, o1, o2, o3), rolled_ref, place[0], place[1], block)


def attend(place, pair, qt, k, vt, seg_col, seg_row):
    total = k.shape[0]
    block = total // 4
    whole = lambda a: pl.BlockSpec(a.shape, lambda i: (0, 0))
    return pl.pallas_call(
        attend_kernel,
        grid=(total // TILE,),
        out_shape=[
            jax.ShapeDtypeStruct((128, total), BF),
            jax.ShapeDtypeStruct((8, total), F32),
        ]
        + [jax.ShapeDtypeStruct((block, 128), BF)] * 4,
        in_specs=[
            pl.BlockSpec(memory_space=SMEM),
            pl.BlockSpec((128, TILE), lambda i: (pair, i)),
            pl.BlockSpec((total, 128), lambda i: (0, pair)),
            pl.BlockSpec((128, total), lambda i: (pair, 0)),
            whole(seg_col),
            whole(seg_row),
        ],
        out_specs=[
            pl.BlockSpec((128, TILE), lambda i: (0, i)),
            pl.BlockSpec((8, TILE), lambda i: (0, i)),
        ]
        + [pl.BlockSpec((block, 128), lambda i: (0, 0))] * 4,
        scratch_shapes=[VMEM((128, total + TILE), BF)],
        compiler_params=pltpu.CompilerParams(vmem_limit_bytes=LIMIT),
        cost_estimate=pl.CostEstimate(
            flops=2 * 2 * 2 * total * LONGEST * 256,
            bytes_accessed=4 << 20,
            transcendentals=2 * total * LONGEST,
        ),
        name="attend",
    )(place, qt, k, vt, seg_col, seg_row)


def back_kernel(
    n_grp, place, qt, k, kt, v, ot0, ot1, lse0, lse1, seg_col, seg_row, cos_t, sin_t,
    early_in, member, member_t, scale_rows,
    g0, g1, g2, g3, mixed_hbm, packed_hbm, wq_hbm, wk_hbm, wv_hbm, frames_hbm, middle_hbm,
    frames_grad, upper_out, lower_out, qg0, qg1, early_out, late_out,
    grad_t, row_dots, dqt, dkt, dvt, nat_ref, rolled, mixed, packed, weights, frames, middle,
    from_x, lower_x, dw, send_d, got_d, early_got, late_got, summed_low, summed_up, summed_q, q_extra,
    send_sem, recv_sem, load_sem,
):
    my_row, my_grp = lax.axis_index("row"), lax.axis_index("grp")
    total = k.shape[0]
    block = total // 4
    steps = total // TILE
    half = HEAD_DIM // 2
    bits = bits_of(n_grp)
    halving, extra = bits[:3], bits[3:]
    side = lambda bit: (my_grp // bit) % 2
    by_row = lambda j: {"row": my_row ^ j}
    by_grp = lambda bit: {"grp": my_grp ^ bit}
    cut = from_x.shape[0]
    low_rows = packed.shape[1] - cut

    numbers = {}

    def remote(name, src, dst, device):
        number = numbers.setdefault(name, len(numbers))
        return pltpu.make_async_remote_copy(
            src, dst, send_sem.at[number], recv_sem.at[number], device_id=device, device_id_type=MESH
        )

    sent = {}

    class Copy:
        def __init__(self, name, parts):
            self.describe = lambda: remote(name, *parts())
            self.start = lambda: self.describe().start()
            self.wait_recv = lambda: self.describe().wait_recv()
            self.wait_send = lambda: self.describe().wait_send()
            self.wait = lambda: self.describe().wait()

    def start(name, parts):
        sent[name] = Copy(name, parts)
        sent[name].start()

    def regions(size):
        out = [(0, size)]
        for bit in halving:
            offset, size = out[-1]
            out.append((offset + side(bit) * (size // 2), size // 2))
        return out

    def away(region, bit):
        offset, size = region
        return pl.ds(pl.multiple_of(offset + (1 - side(bit)) * (size // 2), 16), size // 2)

    def at(region):
        return pl.ds(pl.multiple_of(region[0], 16), region[1])

    loads = [
        pltpu.make_async_copy(src, dst, load_sem.at[i])
        for i, (src, dst) in enumerate(
            (
                (packed_hbm, packed),
                (mixed_hbm, mixed),
                (wq_hbm, mixed.at[pl.ds(0, D)]),
                (wk_hbm, mixed.at[pl.ds(D, D)]),
                (wv_hbm, weights),
                (frames_hbm, frames),
                (middle_hbm, middle),
            )
        )
    ]
    for load in loads[:1] + loads[4:]:
        load.start()

    barrier = pltpu.get_barrier_semaphore()
    for device in [by_row(j) for j in (1, 2, 3)] + [by_grp(bit) for bit in bits]:
        pl.semaphore_signal(barrier, inc=1, device_id=device, device_id_type=MESH)
    pl.semaphore_wait(barrier, 3 + len(bits))

    up_at, low_at = regions(cut), [(cut + o, s) for o, s in regions(low_rows)]
    q_at = regions(256)

    def upper_x():
        start("a0", lambda: (packed_hbm.at[1, pl.ds(0, cut)], from_x, by_row(2)))

    def upper_x_done():
        loads[0].wait()
        sent["a0"].wait_recv()
        packed[0, :cut] = add_low(packed[0, :cut], from_x[...])

    def upper_send(i):
        start(f"a{i + 1}", lambda i=i: (packed.at[0, away(up_at[i], halving[i])], summed_up.at[at((cut - 2 * up_at[i + 1][1], up_at[i + 1][1]))], by_grp(halving[i])))

    def upper_take(i):
        sent[f"a{i + 1}"].wait_recv()
        mine, size = at(up_at[i + 1]), up_at[i + 1][1]
        got = summed_up[cut - 2 * size : cut - size]
        packed[0, mine] = add_low(packed[0, mine], got)

    def lower_send(i):
        source = packed_hbm if i == 0 else packed
        size = low_at[i + 1][1]
        start(f"b{i + 1}", lambda i=i, size=size, source=source: (source.at[:, away(low_at[i], halving[i])], summed_low.at[:, at((low_rows - 2 * size, size))], by_grp(halving[i])))

    def lower_take(i):
        sent[f"b{i + 1}"].wait_recv()
        mine, size = at(low_at[i + 1]), low_at[i + 1][1]
        got = summed_low[:, low_rows - 2 * size : low_rows - size]
        packed[:, mine] = add_low(packed[:, mine], got)

    def whole_sum(name, ref, region, first):
        for number, bit in enumerate(extra):
            start(f"{name}{number}", lambda bit=bit, number=number, ref=ref, region=region: (ref.at[at(region)], lower_x.at[first + number], by_grp(bit)))
            sent[f"{name}{number}"].wait()
            ref[at(region)] = add_low(ref[at(region)], lower_x[first + number])

    def lower_x_send():
        start("bx", lambda: (packed.at[1, at(low_at[-1])], lower_x.at[0], by_row(2)))

    def lower_x_take():
        sent["bx"].wait_recv()
        packed[0, at(low_at[-1])] = add_low(packed[0, at(low_at[-1])], lower_x[0])

    def spread_send(name, ref, areas, i):
        part = at(areas[i + 1])
        start(f"{name}{i}", lambda i=i, part=part, ref=ref: (ref.at[part], ref.at[part], by_grp(halving[i])))

    def spread_take(name, i):
        sent[f"{name}{i}"].wait_recv()

    lower_areas = regions(low_rows)

    def upper_own():
        whole_sum("ax", packed.at[0], up_at[-1], 1)
        upper_out[at(up_at[-1])] = packed[0, at(up_at[-1])]

    def lower_own():
        whole_sum("by", packed.at[0], low_at[-1], 1 + len(extra))
        lower_out[at(lower_areas[-1])] = packed[0, at(low_at[-1])]

    q_out = (qg0, qg1)

    def heads_send(pair, i):
        size = q_at[i + 1][1]
        start(f"q{pair}{i}", lambda i=i, pair=pair, size=size: (dw.at[pair, :, away(q_at[i], halving[i])], summed_q.at[pair, :, at((256 - 2 * size, size))], by_grp(halving[i])))

    def heads_take(pair, i):
        sent[f"q{pair}{i}"].wait_recv()
        mine, size = at(q_at[i + 1]), q_at[i + 1][1]
        got = summed_q[pair, :, 256 - 2 * size : 256 - size]
        dw[pair, :, mine] = add_low(dw[pair, :, mine], got)

    def heads_shard_send(pair):
        part, size = at(q_at[-1]), q_at[-1][1]
        for number, bit in enumerate(extra):
            name, slot = f"qe{pair}{number}", 4 * (pair * len(extra) + number)
            landing = q_extra.at[pl.ds(slot, 4)]
            start(name, lambda: (dw.at[pair, :, part], landing, by_grp(bit)))
            sent[name].wait()
            dw[pair, :, part] = add_low(dw[pair, :, part], q_extra[slot : slot + 4])
        q_out[pair][0, part] = dw[pair, my_row, part]
        for j in (1, 2, 3):
            start(f"qs{pair}{j}", lambda j=j, pair=pair, part=part: (dw.at[pair, my_row ^ j, part], q_out[pair].at[j, part], by_row(j)))

    def heads_shard_take(pair):
        for j in (1, 2, 3):
            sent[f"qs{pair}{j}"].wait_recv()

    def heads_spread_send(pair, i):
        part = at(q_at[i + 1])
        ref = q_out[pair]
        start(f"qg{pair}{i}", lambda i=i, part=part, ref=ref: (ref.at[:, part], ref.at[:, part], by_grp(halving[i])))

    def heads_spread_take(pair, i):
        sent[f"qg{pair}{i}"].wait_recv()

    def row_sum_send(name, got):
        for j in (1, 2, 3):
            start(f"{name}{j}", lambda j=j: (got.at[my_row], got.at[my_row], by_row(j)))

    def row_sum_take(name, got):
        for j in (1, 2, 3):
            sent[f"{name}{j}"].wait_recv()
        return (got[0] + got[1]) + (got[2] + got[3])

    def fold(sums):
        width = sums.shape[1] // 2
        return jnp.concatenate([sums[:, :width], sums[:, width:]], 0).astype(BF)

    def gather_send(name, ref, i):
        start(f"{name}{i}", lambda i=i, ref=ref: (ref.at[pl.ds(0, 1 << i)], ref.at[pl.ds(1 << i, 1 << i)], by_grp(bits[i])))

    def gather_take(name, i):
        sent[f"{name}{i}"].wait_recv()

    def early_fold():
        early_out[0] = fold(row_sum_take("es", early_got))

    upper_x()
    lower_send(0)
    early_got[my_row] = early_in[...]
    row_sum_send("es", early_got)

    lanes_of = slice(0, 256)
    for j, source in enumerate((g0, g1, g2, g3)):
        mixed[pl.ds(pl.multiple_of((my_row ^ j) * block, block), block), lanes_of] = source[...]
    ahead = roll_matrix(place[1])

    def turn(i, carry):
        cols = pl.ds(pl.multiple_of(i * TILE, TILE), TILE)
        after = pl.ds(pl.multiple_of((i + 1) % steps * TILE, TILE), TILE)
        part = matdot(ahead[:, :TILE], mixed[cols, lanes_of], 1, 0)
        part = (part + matdot(ahead[:, TILE:], mixed[after, lanes_of], 1, 0)).T
        grad_t[:, cols] = part.astype(BF)
        for head in range(4):
            mine = slice((head % 2) * HEAD_DIM, (head % 2 + 1) * HEAD_DIM)
            crossed = part[head * HEAD_DIM : (head + 1) * HEAD_DIM] * (ot0, ot1)[head // 2][
                mine, cols
            ].astype(F32)
            row_dots[head : head + 1, cols] = jnp.sum(crossed, axis=0, keepdims=True)
        return carry

    lax.fori_loop(0, steps, turn, 0)
    loads[1].start()

    def run(pair, here, spans, allowed):
        lanes = slice(pair * 128, (pair + 1) * 128)
        lse = (lse0, lse1)[pair]
        for head in range(2):
            mine = slice(head * HEAD_DIM, (head + 1) * HEAD_DIM)
            wide = slice(pair * 128 + head * HEAD_DIM, pair * 128 + (head + 1) * HEAD_DIM)
            dots = slice(2 * pair + head, 2 * pair + head + 1)
            grad_query = None
            for first, count in spans:
                keys = pl.ds(first, count)
                scores = matdot(k[keys, lanes], one_head(qt[lanes, here], head), 1, 0)
                if allowed is not None:
                    scores = jnp.where(allowed, scores, -1e30)
                probs = jnp.exp(scores - lse[head : head + 1, here])
                grad_probs = matdot(v[keys, lanes], one_head(grad_t[lanes, here], head), 1, 0)
                grad_scores = (probs * (grad_probs - row_dots[dots, here])).astype(BF)
                part = matdot(kt[wide, keys], grad_scores, 1, 0)
                grad_query = part if grad_query is None else grad_query + part
                dkt[mine, keys] += matdot(qt[wide, here], grad_scores, 1, 1)
                dvt[mine, keys] += matdot(grad_t[wide, here], probs.astype(BF), 1, 1)
            dqt[mine, here] = grad_query * HEAD_DIM**-0.5

    def finish(pair):
        def part(i, sums):
            cols = pl.ds(pl.multiple_of(i * TILE, TILE), TILE)
            cosine, sine = cos_t[:, cols], sin_t[:, cols]

            def turned(ref):
                parts = []
                for at_row in range(0, 128, HEAD_DIM):
                    first = ref[at_row : at_row + half, cols]
                    second = ref[at_row + half : at_row + HEAD_DIM, cols]
                    parts.append(first * cosine + second * sine)
                    parts.append(second * cosine - first * sine)
                return jnp.concatenate(parts, 0)

            columns = jnp.concatenate([turned(dqt), turned(dkt), dvt[:, cols]], 0)
            nat_ref[:, pl.ds(pl.multiple_of(TILE + i * TILE, TILE), TILE)] = columns.astype(BF)
            low = columns.T.astype(BF)
            rolled[cols, :] = low
            return sums + jnp.sum(low.astype(F32), axis=0, keepdims=True)

        sums = lax.fori_loop(0, steps, part, jnp.zeros((1, 384), F32))
        if pair == 1:
            for j in (1, 2, 3):
                sent[f"d0{j}"].wait_send()
        outs = [got_d.at[my_row, pair]] + [send_d.at[j] for j in range(3)]
        unroll(outs, nat_ref, my_row, place[1], block)
        for j in (1, 2, 3):
            start(f"d{pair}{j}", lambda j=j, pair=pair: (send_d.at[j - 1], got_d.at[my_row, pair], by_row(j)))
        if pair == 0:
            loads[1].wait()
        for shard in range(4):
            columns = mixed[:, shard * 256 : (shard + 1) * 256]
            dw[pair, shard] = contract_rows(columns, rolled[...]).astype(BF)
        heads_send(pair, 0)
        return sums

    bias_sums = []
    hooks = (
        {
            2: lambda: (early_fold(), gather_send("eg", early_out, 0)),
            4: lambda: (gather_take("eg", 0), gather_send("eg", early_out, 1)),
            6: lambda: (gather_take("eg", 1), gather_send("eg", early_out, 2)),
        },
        {
            0: lambda: (upper_x_done(), upper_send(0)),
            1: lambda: (lower_take(0), lower_send(1)),
            4: lambda: (heads_take(0, 0), heads_send(0, 1)),
            5: lambda: (upper_take(0), upper_send(1)),
            6: lambda: (lower_take(1), lower_send(2)),
        },
    )
    for pair in range(2):
        dkt[...] = jnp.zeros_like(dkt)
        dvt[...] = jnp.zeros_like(dvt)

        def tile(i, carry):
            run(pair, pl.ds(pl.multiple_of(i * TILE, TILE), TILE), BACK_SPANS, None)
            for when, hook in hooks[pair].items():
                pl.when(i == when)(lambda: (hook(), None)[1])
            return carry

        lax.fori_loop(0, steps - 1, tile, 0)
        tail = total - LONGEST
        run(pair, pl.ds(LONGEST, tail), [(LONGEST, tail)], seg_col[...] == seg_row[...])
        bias_sums.append(finish(pair))

    for load in loads[2:4]:
        load.start()
    for number in range(2, len(bits)):
        gather_take("eg", number)
        if number + 1 < len(bits):
            gather_send("eg", early_out, number + 1)
    heads_take(0, 1), heads_send(0, 2)
    upper_take(1), upper_send(2)
    lower_take(2), lower_x_send()
    heads_take(0, 2), heads_shard_send(0)
    upper_take(2), upper_own(), spread_send("ag", upper_out, up_at, 2)
    heads_take(1, 0), heads_send(1, 1)
    lower_x_take(), lower_own(), spread_send("bg", lower_out, lower_areas, 2)
    heads_shard_take(0), heads_spread_send(0, 2)

    for pair in range(2):
        for j in (1, 2, 3):
            sent[f"d{pair}{j}"].wait_recv()
    for load in loads[2:]:
        load.wait()
    late = jnp.zeros((8, 2 * D), F32)
    for part in range(block // TILE):
        rows = slice(part * TILE, (part + 1) * TILE)
        grad = jnp.zeros((TILE, D), F32)
        for kind in range(3):
            pieces = [
                got_d[owner, pair, rows, kind * 128 : (kind + 1) * 128]
                for owner in range(4)
                for pair in range(2)
            ]
            weight = weights[...] if kind == 2 else mixed[kind * D : (kind + 1) * D]
            grad = grad + against(jnp.concatenate(pieces, 1), weight)
        normed, factor = normalize(frames[rows, :].astype(F32))
        scale = jnp.ones((TILE, D), F32)
        for u in range(scale_rows.shape[0]):
            scale = scale + member[rows, u : u + 1] * scale_rows[u : u + 1, :]
        back = normalize_back(grad * scale, normed, factor)
        frames_grad[rows, :] = (middle[rows, :] + back).astype(BF)
        late = late + lax.dot_general(
            member_t[:, rows],
            jnp.concatenate([grad, grad * normed], 1),
            (((1,), (0,)), ((), ())),
            precision=highest,
            preferred_element_type=F32,
        )
    late_got[my_row] = late
    row_sum_send("ls", late_got)
    heads_take(1, 1), heads_send(1, 2)
    spread_take("ag", 2), spread_send("ag", upper_out, up_at, 1)
    spread_take("bg", 2), spread_send("bg", lower_out, lower_areas, 1)
    heads_spread_take(0, 2), heads_spread_send(0, 1)
    late_sum = row_sum_take("ls", late_got)
    widths = [slice(kind * 128, (kind + 1) * 128) for kind in range(3)]
    bias_row = jnp.concatenate(
        [bias_sums[pair][:, w] for w in widths for pair in range(2)]
        + [jnp.zeros((1, 2 * D - 768), F32)],
        1,
    )
    index = lax.broadcasted_iota(jnp.int32, (8, 2 * D), 0)
    late_out[0] = fold(jnp.where(index == 4, bias_row, late_sum))
    gather_send("lg", late_out, 0)
    heads_take(1, 2), heads_shard_send(1)
    gather_take("lg", 0), gather_send("lg", late_out, 1)
    heads_shard_take(1), heads_spread_send(1, 2)
    spread_take("ag", 1), spread_send("ag", upper_out, up_at, 0)
    spread_take("bg", 1), spread_send("bg", lower_out, lower_areas, 0)
    gather_take("lg", 1), gather_send("lg", late_out, 2)
    heads_spread_take(0, 1), heads_spread_send(0, 0)
    heads_spread_take(1, 2), heads_spread_send(1, 1)
    for number in range(2, len(bits)):
        gather_take("lg", number)
        if number + 1 < len(bits):
            gather_send("lg", late_out, number + 1)
    heads_spread_take(1, 1), heads_spread_send(1, 0)
    spread_take("ag", 0)
    spread_take("bg", 0)
    heads_spread_take(0, 0)
    heads_spread_take(1, 0)
    waited = {f"{name}{i}" for name in ("ax", "by", "qe0", "qe1") for i in range(len(extra))}
    waited |= {"d01", "d02", "d03"}
    for name, copy in sent.items():
        if name not in waited:
            copy.wait_send()


def attend_back(
    n_grp, place, qt, k, kt, v, heads_t, lse, seg_col, seg_row, cos_t, sin_t, early, member, member_t,
    scale_rows, grads, mixed, packed, weights, frames, middle,
):
    total = k.shape[0]
    block = total // 4
    rows = packed.shape[1]
    cut = rows // 2
    extra = max(0, len(bits_of(n_grp)) - 3)
    inputs = [
        qt, k, kt, v, *heads_t, *lse, seg_col, seg_row, cos_t, sin_t, early, member, member_t, scale_rows,
        *grads,
    ]
    far = [mixed, packed, *weights, frames, middle]
    copies = 100
    return pl.pallas_call(
        functools.partial(back_kernel, n_grp),
        out_shape=[
            jax.ShapeDtypeStruct((block, D), BF),
            jax.ShapeDtypeStruct((cut, D), BF),
            jax.ShapeDtypeStruct((rows - cut, D), BF),
            jax.ShapeDtypeStruct((4, 256, 384), BF),
            jax.ShapeDtypeStruct((4, 256, 384), BF),
            jax.ShapeDtypeStruct((n_grp, 16, 2 * D), BF),
            jax.ShapeDtypeStruct((n_grp, 16, D), BF),
        ],
        in_specs=[pl.BlockSpec(memory_space=SMEM)]
        + [pl.BlockSpec(memory_space=VMEM)] * len(inputs)
        + [pl.BlockSpec(memory_space=pl.ANY)] * len(far),
        out_specs=[pl.BlockSpec(memory_space=VMEM)] * 7,
        scratch_shapes=[
            VMEM((256, total), BF),
            VMEM((8, total), F32),
            VMEM((128, total), F32),
            VMEM((128, total), F32),
            VMEM((128, total), F32),
            VMEM((384, total + TILE), BF),
            VMEM((total, 384), BF),
            VMEM((total, D), BF),
            VMEM((2, rows, D), BF),
            VMEM((D, D), BF),
            VMEM((block, D), BF),
            VMEM((block, D), F32),
            VMEM((cut, D), BF),
            VMEM((1 + 2 * extra, (rows - cut) // 8, D), BF),
            VMEM((2, 4, 256, 384), BF),
            VMEM((3, block, 384), BF),
            VMEM((4, 2, block, 384), BF),
            VMEM((4, 8, 4 * D), F32),
            VMEM((4, 8, 2 * D), F32),
            VMEM((2, rows - cut, D), BF),
            VMEM((cut, D), BF),
            VMEM((2, 4, 256, 384), BF),
            VMEM((max(1, 8 * extra), 32, 384), BF),
            pltpu.SemaphoreType.DMA((copies,)),
            pltpu.SemaphoreType.DMA((copies,)),
            pltpu.SemaphoreType.DMA((len(far),)),
        ],
        compiler_params=pltpu.CompilerParams(
            vmem_limit_bytes=62 << 20, collective_id=1, has_side_effects=True
        ),
        cost_estimate=pl.CostEstimate(
            flops=4 * 2 * 5 * total * LONGEST * 256,
            bytes_accessed=40 << 20,
            transcendentals=4 * total * LONGEST,
        ),
        name="attend_back",
    )(place, *inputs, *far)


def weight_grad_kernel(place, o, h, a, e_att, e_z, e_b, out):
    out[0, :256] = contract_rows(o[...], e_att[...]).astype(BF)
    out[0, 256:512] = contract_rows(h[...], e_z[:, :D]).astype(BF)
    out[0, 512:768] = contract_rows(h[...], e_z[:, D:]).astype(BF)
    out[0, 768:] = contract_rows(a[...], e_b[...]).astype(BF)


def weight_grads(place, order, o, h, a, e_att, e_z, e_b):
    rows = o.shape[0]
    first, second = order
    pick = lambda i: first + i * (second - first)
    whole = lambda t: pl.BlockSpec(t.shape, lambda i, p: (0, 0))
    return pl.pallas_call(
        weight_grad_kernel,
        grid_spec=pltpu.PrefetchScalarGridSpec(
            num_scalar_prefetch=1,
            grid=(2,),
            in_specs=[
                pl.BlockSpec((rows, 256), lambda i, p: (0, pick(i))),
                pl.BlockSpec((rows, 256), lambda i, p: (0, p[0] ^ pick(i))),
                pl.BlockSpec((rows, 512), lambda i, p: (0, p[0] ^ pick(i))),
                whole(e_att),
                whole(e_z),
                whole(e_b),
            ],
            out_specs=pl.BlockSpec((1, 1280, D), lambda i, p: (i, 0, 0)),
        ),
        out_shape=jax.ShapeDtypeStruct((2, 1280, D), BF),
        compiler_params=pltpu.CompilerParams(vmem_limit_bytes=LIMIT),
        cost_estimate=pl.CostEstimate(
            flops=2 * 2 * rows * 1280 * D, bytes_accessed=12 << 20, transcendentals=0
        ),
        name="weight_grads",
    )(place, o, h, a, e_att, e_z, e_b)


def local(
    frames, time_embed, lengths, mod_weight, mod_bias, query_weight, query_bias, key_weight, key_bias,
    value_weight, value_bias, out_weight, out_bias, up_weight, up_bias, down_weight, down_bias, cotangent,
):
    n_grp = lax.axis_size("grp")
    row_count = frames.shape[0]
    my_row = lax.axis_index("row")
    group_rows = row_count * lax.axis_size("row")
    width = D // 4

    from_core = exchange(frames, "row", 1)
    from_x = exchange(frames, "row", 2)
    from_both = exchange(from_x, "row", 1)

    utt_sizes = lengths[0]
    finish = jnp.cumsum(utt_sizes)
    starts = finish - utt_sizes
    longest = jnp.argmax(utt_sizes)
    offset = starts[longest]
    place = jnp.stack([my_row, offset]).astype(jnp.int32)
    utts = jnp.arange(utt_sizes.shape[0], dtype=jnp.int32)

    def layout(rows):
        segment = jnp.sum((rows[:, None] >= finish[None, :]).astype(jnp.int32), axis=1)
        is_member = segment[:, None] == utts[None, :]
        position = rows - jnp.sum(jnp.where(is_member, starts[None, :], 0), axis=1)
        return segment, is_member.astype(F32), position

    rolled_rows = (jnp.arange(group_rows, dtype=jnp.int32) + offset) % group_rows
    segment, member_rolled, position = layout(rolled_rows)
    half = HEAD_DIM // 2
    frequency = jnp.exp(jnp.arange(half, dtype=F32) * (-2.0 * math.log(10000.0) / HEAD_DIM))
    angles = frequency[:, None] * position.astype(F32)[None, :]
    cos_t, sin_t = jnp.cos(angles), jnp.sin(angles)
    seg_tail = segment[LONGEST:]
    seg_col, seg_row = seg_tail[:, None], seg_tail[None, :]
    own_rows = my_row * row_count + jnp.arange(row_count, dtype=jnp.int32)
    _, member, _ = layout(own_rows)

    col_part = lambda w, j: lax.dynamic_slice_in_dim(w, (my_row ^ j) * width, width, 1)
    weight_t = jnp.concatenate(
        [col_part(w, 0).T for w in (query_weight, key_weight, value_weight)], 0
    )
    own_part = lambda b: lax.dynamic_slice_in_dim(b, my_row * width, width, 0)
    bias_t = jnp.concatenate([own_part(query_bias), own_part(key_bias), own_part(value_bias)])[:, None]
    out_perm = jnp.concatenate(
        [lax.dynamic_slice_in_dim(out_weight, (my_row ^ j) * width, width, 0) for j in range(4)], 0
    )

    embedding = time_embed[0]
    act_low = jax.nn.silu(embedding).astype(BF)
    modulation = jnp.dot(act_low, mod_weight, preferred_element_type=F32) + mod_bias
    mod_long = lax.dynamic_slice_in_dim(modulation[:, : 2 * D], longest, 1, 0)
    act_all = act_low
    for bit in bits_of(n_grp):
        act_all = jnp.concatenate([act_all, exchange(act_all, "grp", bit)], 0)

    mixed, qt, kt, vt, k_rows, v_rows = project(
        place, (frames, from_core, from_x, from_both), modulation[:, : 2 * D], mod_long,
        member_rolled[LONGEST:], weight_t, bias_t, cos_t, sin_t,
    )

    heads_t, log_totals, pieces = [], [], []
    for pair in range(2):
        ot, lse, *outs = attend(place, pair, qt, k_rows, vt, seg_col, seg_row)
        heads_t.append(ot)
        log_totals.append(lse)
        pieces.append([outs[0]] + [exchange(outs[j], "row", j) for j in range(1, 4)])
    attn_low = jnp.concatenate([pieces[pair][j] for j in range(4) for pair in range(2)], 1)

    per_token = jnp.dot(member, modulation, precision=highest, preferred_element_type=F32)
    shift_attn, scale_attn, gate_attn, shift_ffn, scale_ffn, gate_ffn = jnp.split(per_token, 6, axis=1)
    residual = frames.astype(F32)
    normed_attn, factor_attn = normalize(residual)
    attended = jnp.dot(attn_low, out_perm, preferred_element_type=F32) + out_bias
    middle = residual + gate_attn * attended
    normed_ffn, factor_ffn = normalize(middle)
    ffn_in = (normed_ffn * (1.0 + scale_ffn) + shift_ffn).astype(BF)
    hidden = jnp.dot(ffn_in, up_weight, preferred_element_type=F32) + up_bias
    active_low = jax.nn.gelu(hidden, approximate=True).astype(BF)
    branch = jnp.dot(active_low, down_weight, preferred_element_type=F32) + down_bias
    output = (middle + gate_ffn * branch).astype(BF)
    upstream = cotangent.astype(F32)
    grad_branch = (upstream * gate_ffn).astype(BF)
    grad_gate_ffn = upstream * branch
    grad_active = against(grad_branch, down_weight)
    _, gelu_pull = jax.vjp(lambda tensor: jax.nn.gelu(tensor, approximate=True), hidden)
    grad_hidden = gelu_pull(grad_active)[0].astype(BF)
    grad_ffn_in = against(grad_hidden, up_weight)
    grad_scale_ffn = grad_ffn_in * normed_ffn
    grad_middle = upstream + normalize_back(grad_ffn_in * (1.0 + scale_ffn), normed_ffn, factor_ffn)
    grad_attended = (grad_middle * gate_attn).astype(BF)
    grad_gate_attn = grad_middle * attended
    grad_heads = against(grad_attended, out_perm).astype(BF)

    cut = [grad_heads[:, j * width : (j + 1) * width] for j in range(4)]
    grad_pieces = [cut[0]] + [exchange(cut[j], "row", j) for j in range(1, 4)]

    operands = (attn_low, ffn_in, active_low, grad_attended, grad_hidden, grad_branch)
    to_core = exchange(weight_grads(place, (1, 3), *operands), "row", 1)
    packed = add_low(weight_grads(place, (0, 2), *operands), to_core)

    early = lax.dot_general(
        member,
        jnp.concatenate([grad_gate_attn, grad_ffn_in, grad_scale_ffn, grad_gate_ffn], 1),
        (((0,), (0,)), ((), ())),
        precision=highest,
        preferred_element_type=F32,
    )
    ffn_bias = jnp.concatenate(
        [column_sum(grad_attended), column_sum(grad_hidden), column_sum(grad_branch)]
    )
    early = jnp.concatenate([early, ffn_bias[None], jnp.zeros((3, 4 * D), F32)], 0)
    pad = ((0, 0), (0, 4))
    member_8 = jnp.pad(member, pad)
    grad_frames, upper, lower, heads_0, heads_1, early_all, late_all = attend_back(
        n_grp, place, qt, k_rows, kt, v_rows, heads_t, log_totals, seg_col, seg_row, cos_t, sin_t,
        early, member_8, member_8.T, modulation[:, D : 2 * D], grad_pieces, mixed, packed,
        (query_weight, key_weight, value_weight), frames, grad_middle,
    )

    packed_total = jnp.concatenate([upper, lower], 0).astype(F32)
    out_grad = packed_total[:256]
    up_grad = jnp.concatenate([packed_total[256:512], packed_total[512:768]], 1)
    down_grad = packed_total[768:]
    by_owner = jnp.stack([heads_0, heads_1])[:, my_row ^ jnp.arange(4)]
    qkv_full = by_owner.transpose(2, 1, 0, 3).reshape(width, 4, 2, 3, 128).astype(F32)
    query_grad, key_grad, value_grad = (qkv_full[:, :, :, i].reshape(width, D) for i in range(3))

    unfold = lambda t: jnp.concatenate([t[:, :8], t[:, 8:]], 2)
    late_all, early_all = unfold(late_all), unfold(early_all)
    mod_all = jnp.concatenate([late_all[:, :4], early_all[:, :4]], 2)
    grad_activated = against(mod_all[0], mod_weight)
    _, silu_pull = jax.vjp(jax.nn.silu, embedding)
    grad_embedding = silu_pull(grad_activated)[0]
    mod_all = mod_all.reshape(n_grp * 4, 6 * D)
    act_slice = lax.dynamic_slice_in_dim(act_all, my_row * width, width, 1)
    mod_weight_grad = contract_rows(act_slice, mod_all)
    mod_bias_grad = lax.dynamic_slice_in_dim(column_sum(mod_all), my_row * 6 * width, 6 * width, 0)
    ffn_bias = column_sum(early_all[:, 4])
    mine = lambda start, size: lax.dynamic_slice_in_dim(ffn_bias, start + my_row * size, size, 0)
    out_b, up_b, down_b = mine(0, width), mine(D, 2 * width), mine(3 * D, width)
    query_b, key_b, value_b = jnp.split(column_sum(late_all[:, 4, : 3 * width]), 3)
    return (
        output,
        grad_frames,
        grad_embedding[None],
        mod_weight_grad,
        mod_bias_grad,
        query_grad,
        query_b,
        key_grad,
        key_b,
        value_grad,
        value_b,
        out_grad,
        out_b,
        up_grad,
        up_b,
        down_grad,
        down_b,
    )


def solution(mesh):
    placed = (
        (P(("grp", "row"), None), P("grp", None, None), P("grp", None))
        + (P(),) * 14
        + (P(("grp", "row"), None),)
    )
    return jax.shard_map(
        local,
        mesh=mesh,
        in_specs=placed,
        out_specs=(
            P(("grp", "row"), None),
            P(("grp", "row"), None),
            P("grp", None, None),
        )
        + (P("row", None), P("row")) * 7,
        check_vma=False,
    )
```

```python
import functools
import math

import jax
import jax.numpy as jnp
from jax import lax
from jax.experimental import pallas as pl
from jax.experimental.pallas import tpu as pltpu
from jax.sharding import PartitionSpec as P

D = 1024
HEADS = 16
HEAD_DIM = 64
LONGEST = 1792
TILE = 256
BF = jnp.bfloat16
F32 = jnp.float32

highest = lax.Precision.HIGHEST
VMEM = pltpu.VMEM
SMEM = pltpu.SMEM
LIMIT = 60 << 20
MESH = pl.DeviceIdType.MESH
BACK_SPANS = [(0, 896), (896, 896)]


def matdot(left, right, left_dim, right_dim):
    return lax.dot_general(
        left, right, (((left_dim,), (right_dim,)), ((), ())), preferred_element_type=F32
    )


def contract_rows(left, right):
    return matdot(left, right, 0, 0)


def against(left, weight):
    return matdot(left, weight, 1, 1)


def column_sum(tensor):
    return jnp.sum(tensor.astype(F32), axis=0)


def normalize(tensor):
    centred = tensor - jnp.mean(tensor, axis=-1, keepdims=True)
    factor = lax.rsqrt(jnp.mean(centred * centred, axis=-1, keepdims=True) + 1e-06)
    return (centred * factor, factor)


def normalize_back(grad_normed, normed, factor):
    mean_grad = jnp.mean(grad_normed, axis=-1, keepdims=True)
    mean_cross = jnp.mean(grad_normed * normed, axis=-1, keepdims=True)
    return (grad_normed - mean_grad - normed * mean_cross) * factor


def exchange(tensor, axis, bit):
    size = lax.axis_size(axis)
    return lax.ppermute(tensor, axis, [(i, i ^ bit) for i in range(size)])


def add_low(left, right):
    return (left.astype(F32) + right.astype(F32)).astype(BF)


def bits_of(count):
    return [1 << i for i in range(count.bit_length() - 1)]


def roll_matrix(offset):
    row = lax.broadcasted_iota(jnp.int32, (TILE, 2 * TILE), 0)
    col = lax.broadcasted_iota(jnp.int32, (TILE, 2 * TILE), 1)
    return (col == row + offset).astype(F32).astype(BF)


def project_kernel(
    place, x0, x1, x2, x3, mod_all, mod_long, member, weight_t, bias, cos_t, sin_t,
    mixed_out, qt_out, kt_out, vt_out, k_out, v_out, rows_ref, roll_ref,
):
    step = pl.program_id(0)
    block = x0.shape[0]
    total = 4 * block

    @pl.when(step == 0)
    def _():
        for j, source in enumerate((x0, x1, x2, x3)):
            at = pl.multiple_of((place[0] ^ j) * block, block)
            rows_ref[pl.ds(at, block), :] = source[...]
        rows_ref[pl.ds(total, TILE), :] = rows_ref[pl.ds(0, TILE), :]
        roll_ref[...] = roll_matrix(place[1])

    pair = rows_ref[pl.ds(pl.multiple_of(step * TILE, TILE), 2 * TILE), :]
    normed, _ = normalize(matdot(roll_ref[...], pair, 1, 0))
    last = step == total // TILE - 1

    @pl.when(jnp.logical_not(last))
    def _():
        mixed_out[...] = (normed * (1.0 + mod_long[:, D:]) + mod_long[:, :D]).astype(BF)

    @pl.when(last)
    def _():
        per_row = jnp.zeros((TILE, 2 * D), F32)
        for u in range(mod_all.shape[0]):
            per_row = per_row + member[:, u : u + 1] * mod_all[u : u + 1, :]
        mixed_out[...] = (normed * (1.0 + per_row[:, D:]) + per_row[:, :D]).astype(BF)

    wide = matdot(weight_t[...], mixed_out[...], 1, 1) + bias[...]
    cosine, sine = cos_t[...], sin_t[...]
    half = HEAD_DIM // 2
    width = qt_out.shape[0]

    def turned(base):
        parts = []
        for at in range(base, base + width, HEAD_DIM):
            first, second = wide[at : at + half], wide[at + half : at + HEAD_DIM]
            parts.append(first * cosine - second * sine)
            parts.append(second * cosine + first * sine)
        return jnp.concatenate(parts, 0)

    keys = turned(width)
    values = wide[2 * width :]
    qt_out[...] = turned(0).astype(BF) * jnp.asarray(HEAD_DIM**-0.5, BF)
    kt_out[...] = keys.astype(BF)
    vt_out[...] = values.astype(BF)
    k_out[...] = keys.T.astype(BF)
    v_out[...] = values.T.astype(BF)


def project(place, blocks, mod_all, mod_long, member, weight_t, bias, cos_t, sin_t):
    block = blocks[0].shape[0]
    total = 4 * block
    width = weight_t.shape[0] // 3
    whole = lambda a: pl.BlockSpec(a.shape, lambda i: (0, 0))
    rows = lambda n: pl.BlockSpec((TILE, n), lambda i: (i, 0))
    cols = lambda n: pl.BlockSpec((n, TILE), lambda i: (0, i))
    return pl.pallas_call(
        project_kernel,
        grid=(total // TILE,),
        out_shape=[
            jax.ShapeDtypeStruct((total, D), BF),
            jax.ShapeDtypeStruct((width, total), BF),
            jax.ShapeDtypeStruct((width, total), BF),
            jax.ShapeDtypeStruct((width, total), BF),
            jax.ShapeDtypeStruct((total, width), BF),
            jax.ShapeDtypeStruct((total, width), BF),
        ],
        in_specs=[pl.BlockSpec(memory_space=SMEM)]
        + [whole(a) for a in blocks]
        + [whole(mod_all), whole(mod_long), whole(member), whole(weight_t), whole(bias)]
        + [cols(HEAD_DIM // 2), cols(HEAD_DIM // 2)],
        out_specs=[rows(D), cols(width), cols(width), cols(width), rows(width), rows(width)],
        scratch_shapes=[VMEM((total + TILE, D), BF), VMEM((TILE, 2 * TILE), BF)],
        compiler_params=pltpu.CompilerParams(vmem_limit_bytes=LIMIT),
        cost_estimate=pl.CostEstimate(
            flops=2 * total * D * 3 * width, bytes_accessed=16 << 20, transcendentals=total
        ),
        name="project",
    )(place, *blocks, mod_all, mod_long, member, weight_t, bias, cos_t, sin_t)


def one_head(pair, head):
    part = pair[head * HEAD_DIM : (head + 1) * HEAD_DIM]
    empty = jnp.zeros_like(part)
    return jnp.concatenate([part, empty] if head == 0 else [empty, part], 0)


def unroll(outs, rolled_ref, my_row, offset, block):
    total = 4 * block
    rolled_ref[:, pl.ds(0, TILE)] = rolled_ref[:, pl.ds(total, TILE)]
    back = roll_matrix(TILE - offset)
    for j, out in enumerate(outs):
        for part in range(block // TILE):
            at = pl.multiple_of((my_row ^ j) * block + part * TILE, TILE)
            rows = matdot(back, rolled_ref[:, pl.ds(at, 2 * TILE)], 1, 1)
            out[part * TILE : (part + 1) * TILE, :] = rows.astype(BF)


def attend_kernel(
    place, qt, k, vt, seg_col, seg_row, ot0, ot1, lse0, lse1, o_all,
    rolled_ref, send_o, send_sem, recv_sem,
):
    my_row = lax.axis_index("row")
    total = k.shape[0]
    block = total // 4
    tail = total - LONGEST
    barrier = pltpu.get_barrier_semaphore()
    for j in (1, 2, 3):
        pl.semaphore_signal(barrier, inc=1, device_id={"row": my_row ^ j}, device_id_type=MESH)
    pl.semaphore_wait(barrier, 3)

    def run(pair, here, first, count, allowed):
        outs, tops = [], []
        lanes = slice(pair * 128, (pair + 1) * 128)
        for head in range(2):
            wide = slice(pair * 128 + head * HEAD_DIM, pair * 128 + (head + 1) * HEAD_DIM)
            scores = matdot(k[first : first + count, lanes], one_head(qt[lanes, here], head), 1, 0)
            if allowed is not None:
                scores = jnp.where(allowed, scores, -1e30)
            top = jnp.max(scores, axis=0, keepdims=True)
            weights = jnp.exp(scores - top)
            exp_sum = jnp.sum(weights, axis=0, keepdims=True)
            mixed = matdot(vt[wide, first : first + count], weights.astype(BF), 1, 0)
            outs.append(mixed / exp_sum)
            tops.append(top + jnp.log(exp_sum))
        low = jnp.concatenate(outs, 0).astype(BF)
        (ot0, ot1)[pair][:, here] = low
        (lse0, lse1)[pair][:, here] = jnp.concatenate(tops * 4, 0)
        return low

    copies = []
    for pair in range(2):

        def tile(i, carry):
            low = run(pair, pl.ds(pl.multiple_of(i * TILE, TILE), TILE), 0, LONGEST, None)
            rolled_ref[:, pl.ds(pl.multiple_of(TILE + i * TILE, TILE), TILE)] = low
            return carry

        lax.fori_loop(0, LONGEST // TILE, tile, 0)
        low = run(pair, pl.ds(LONGEST, tail), LONGEST, tail, seg_col[...] == seg_row[...])
        rolled_ref[:, pl.ds(total, TILE)] = low
        lanes = pl.ds(pair * 128, 128)
        outs = [o_all.at[0, :, lanes]] + [send_o.at[3 * pair + j] for j in range(3)]
        unroll(outs, rolled_ref, my_row, place[1], block)
        for j in (1, 2, 3):
            number = 3 * pair + j - 1
            copies.append(
                pltpu.make_async_remote_copy(
                    send_o.at[number], o_all.at[j, :, lanes], send_sem.at[number], recv_sem.at[number],
                    device_id={"row": my_row ^ j}, device_id_type=MESH,
                )
            )
            copies[-1].start()
    for copy in copies:
        copy.wait()


def attend(place, qt, k, vt, seg_col, seg_row):
    total = k.shape[0]
    block = total // 4
    return pl.pallas_call(
        attend_kernel,
        out_shape=[jax.ShapeDtypeStruct((128, total), BF)] * 2
        + [jax.ShapeDtypeStruct((8, total), F32)] * 2
        + [jax.ShapeDtypeStruct((4, block, 256), BF)],
        in_specs=[pl.BlockSpec(memory_space=SMEM)] + [pl.BlockSpec(memory_space=VMEM)] * 5,
        out_specs=[pl.BlockSpec(memory_space=VMEM)] * 5,
        scratch_shapes=[
            VMEM((128, total + TILE), BF),
            VMEM((6, block, 128), BF),
            pltpu.SemaphoreType.DMA((6,)),
            pltpu.SemaphoreType.DMA((6,)),
        ],
        compiler_params=pltpu.CompilerParams(
            vmem_limit_bytes=LIMIT, collective_id=3, has_side_effects=True
        ),
        cost_estimate=pl.CostEstimate(
            flops=2 * 2 * 4 * total * LONGEST * 256,
            bytes_accessed=8 << 20,
            transcendentals=4 * total * LONGEST,
        ),
        name="attend",
    )(place, qt, k, vt, seg_col, seg_row)


FEED_PIECES = ((384, ("x", 1, 2, 4)), (384, (2, 1, "x", 4)), (256, (1, 2, 4, "x")), (256, ("x", 1, 2, 4)),)
HEAD_PIECES = (
    ((384, (1, 2, 4)),),
    ((128, (1, 2, 4)), (128, (1, 2, 4)), (128, (1, 2, 4)),),
)
HOOKS = {
    ("tile", 0, 1): [("e", 0)],
    ("tile", 0, 2): [("f2", 0)],
    ("tile", 0, 3): [("e", 1)],
    ("tile", 0, 4): [("f1", 0)],
    ("tile", 0, 5): [("f0", 0), ("f2", 1)],
    ("tile", 0, 6): [("e", 2)],
    ("tile", 0, 7): [("f1", 1)],
    ("fin", 0, 0): [("f2", 2), ("f3", 0)],
    ("fin", 0, 1): [("f1", 2)],
    ("tile", 1, 0): [("f0", 1)],
    ("tile", 1, 1): [("e", 3), ("f3", 1)],
    ("tile", 1, 2): [("f1", 3)],
    ("tile", 1, 3): [("f0", 2), ("q00", 0)],
    ("tile", 1, 4): [("f2", 3), ("f3", 2)],
    ("tile", 1, 5): [("f1", 4)],
    ("tile", 1, 6): [("f0", 3)],
    ("tile", 1, 7): [("f1", 5), ("q00", 1)],
    ("fin", 1, 0): [("f2", 4), ("f3", 3)],
    ("fin", 1, 1): [("f0", 4), ("q10", 0), ("q11", 0), ("f1", 6), ("q12", 0), ("q00", 2)],
    ("epi", 0, 0): [("f2", 5), ("f3", 4), ("q00", 3)],
    ("epi", 1, 0): [("f0", 5), ("q10", 1), ("q11", 1), ("q12", 1), ("f2", 6), ("f3", 5), ("l", 0), ("q00", 4), ("q10", 2), ("f0", 6), ("q11", 2), ("q10", 3), ("q12", 2), ("q11", 3), ("q12", 3), ("f3", 6), ("l", 1), ("q00", 5), ("q10", 4), ("q11", 4), ("q12", 4), ("l", 2), ("q10", 5), ("q11", 5), ("q12", 5), ("q00", 6), ("q10", 6), ("l", 3), ("q11", 6), ("q12", 6)],
}


def back_kernel(
    n_grp, place, qt, k, kt, v, ot0, ot1, lse0, lse1, seg_col, seg_row, cos_t, sin_t,
    early_in, member, scale_rows,
    grads_in, mixed_hbm, packed_hbm, wq_hbm, wk_hbm, wv_hbm, frames_hbm, middle_hbm,
    frames_grad, packed_out, qg0, qg1, early_out, late_out,
    grad_t, row_dots, dqt, dkt, dvt, nat_ref, rolled, mixed, packed, weights, frames, middle,
    landing, dw, send_d, got_d, early_got, late_got, summed_q, q_extra,
    send_sem, recv_sem, load_sem,
):
    my_row, my_grp = lax.axis_index("row"), lax.axis_index("grp")
    total = k.shape[0]
    block = total // 4
    steps = total // TILE
    half = HEAD_DIM // 2
    bits = bits_of(n_grp)
    extra = bits[3:]
    side = lambda bit: (my_grp // bit) % 2
    by_row = lambda j: {"row": my_row ^ j}
    by_grp = lambda bit: {"grp": my_grp ^ bit}
    q_out = (qg0, qg1)

    chains, numbers, started = {}, {}, []

    def copies_of(name, step):
        out = []
        for index, (src, dst, device) in enumerate(chains[name][step][0]()):
            number = numbers.setdefault((name, step, index), len(numbers))
            out.append(
                pltpu.make_async_remote_copy(
                    src, dst, send_sem.at[number], recv_sem.at[number],
                    device_id=device, device_id_type=MESH,
                )
            )
        return out

    def start(name, step=0):
        started.append((name, step))
        for copy in copies_of(name, step):
            copy.start()

    def advance(name, step):
        for copy in copies_of(name, step):
            copy.wait_recv()
        chains[name][step][1]()
        if step + 1 < len(chains[name]):
            start(name, step + 1)

    def run_hook(mark):
        for name, step in HOOKS.get(mark, ()):
            advance(name, step)

    def one_step(number, src, dst, device):
        copy = pltpu.make_async_remote_copy(
            src, dst, send_sem.at[number], recv_sem.at[number], device_id=device, device_id_type=MESH
        )
        copy.start()
        copy.wait()

    def away(region, bit):
        offset, size = region
        return pl.ds(pl.multiple_of(offset + (1 - side(bit)) * (size // 2), 16), size // 2)

    def kept(region, bit):
        offset, size = region
        return (offset + side(bit) * (size // 2), size // 2)

    def at(region):
        return pl.ds(pl.multiple_of(region[0], 16), region[1])

    nothing = lambda: None

    def feed_chain(name, region, order, land):
        chain, areas, shards = [], [], (1, 0)
        for op in order:
            source = packed if chain else packed_hbm
            if op == "x":

                def parts(region=region, land=land, source=source):
                    return [(source.at[1, at(region)], landing.at[pl.ds(land, region[1])], by_row(2))]

                def take(region=region, land=land):
                    got = landing[land : land + region[1]]
                    packed[0, at(region)] = add_low(packed[0, at(region)], got)

                shards, land = (0,), land + region[1]
            else:
                size = region[1] // 2

                def parts(region=region, land=land, source=source, shards=shards, size=size, op=op):
                    return [
                        (
                            source.at[shard, away(region, op)],
                            landing.at[pl.ds(land + i * size, size)],
                            by_grp(op),
                        )
                        for i, shard in enumerate(shards)
                    ]

                region = kept(region, op)

                def take(region=region, land=land, shards=shards, size=size):
                    for i, shard in enumerate(shards):
                        got = landing[land + i * size : land + (i + 1) * size]
                        packed[shard, at(region)] = add_low(packed[shard, at(region)], got)

                land += size * len(shards)
                areas.append((op, region))
            chain.append((parts, take))
        last = chain[-1][1]

        def own():
            last()
            for i, bit in enumerate(extra):
                first, size = land + i * region[1], region[1]
                number = numbers.setdefault((name, "extra", i), len(numbers))
                one_step(number, packed.at[0, at(region)], landing.at[pl.ds(first, size)], by_grp(bit))
                packed[0, at(region)] = add_low(packed[0, at(region)], landing[first : first + size])
            packed_out[at(region)] = packed[0, at(region)]

        chain[-1] = (chain[-1][0], own)
        for bit, area in reversed(areas):
            chain.append(
                (
                    lambda bit=bit, area=area: [
                        (packed_out.at[at(area)], packed_out.at[at(area)], by_grp(bit))
                    ],
                    nothing,
                )
            )
        chains[name] = chain
        return land + len(extra) * region[1]

    def heads_chain(name, pair, number, lanes, order):
        chain, areas, region = [], [], (0, 256)
        for bit in order:
            size = region[1] // 2
            land = slice(256 - region[1], 256 - size)

            def parts(region=region, bit=bit, land=land):
                return [
                    (
                        dw.at[pair, :, away(region, bit), lanes],
                        summed_q.at[pair, :, pl.ds(land.start, land.stop - land.start), lanes],
                        by_grp(bit),
                    )
                ]

            region = kept(region, bit)

            def take(region=region, land=land):
                mine = at(region)
                dw[pair, :, mine, lanes] = add_low(
                    dw[pair, :, mine, lanes], summed_q[pair, :, land, lanes]
                )

            areas.append((bit, region))
            chain.append((parts, take))
        last, part = chain[-1][1], region

        def own():
            last()
            for i, bit in enumerate(extra):
                slot = 4 * (pair * len(extra) + i)
                count = numbers.setdefault((name, "extra", i), len(numbers))
                one_step(
                    count, dw.at[pair, :, at(part), lanes], q_extra.at[pl.ds(slot, 4), :, lanes],
                    by_grp(bit),
                )
                dw[pair, :, at(part), lanes] = add_low(
                    dw[pair, :, at(part), lanes], q_extra[slot : slot + 4, :, lanes]
                )
            q_out[pair][0, at(part), lanes] = dw[pair, my_row, at(part), lanes]

        chain[-1] = (chain[-1][0], own)
        chain.append(
            (
                lambda: [
                    (
                        dw.at[pair, my_row ^ j, at(part), lanes],
                        q_out[pair].at[j, at(part), lanes],
                        by_row(j),
                    )
                    for j in (1, 2, 3)
                ],
                nothing,
            )
        )
        for bit, area in reversed(areas):
            spot = lambda area=area: q_out[pair].at[:, at(area), lanes]
            chain.append((lambda bit=bit, spot=spot: [(spot(), spot(), by_grp(bit))], nothing))
        chains[name] = chain

    def gather_chain(name, got, out, finish):
        def first():
            out[0] = finish((got[0] + got[1]) + (got[2] + got[3]))

        chain = [(lambda: [(got.at[my_row], got.at[my_row], by_row(j)) for j in (1, 2, 3)], first)]
        for i, bit in enumerate(bits):
            chain.append(
                (
                    lambda i=i, bit=bit: [
                        (out.at[pl.ds(0, 1 << i)], out.at[pl.ds(1 << i, 1 << i)], by_grp(bit))
                    ],
                    nothing,
                )
            )
        chains[name] = chain

    def fold(sums):
        width = sums.shape[1] // 2
        return jnp.concatenate([sums[:, :width], sums[:, width:]], 0).astype(BF)

    loads = [
        pltpu.make_async_copy(src, dst, load_sem.at[i])
        for i, (src, dst) in enumerate(
            (
                (packed_hbm, packed),
                (mixed_hbm, mixed),
                (wq_hbm, mixed.at[pl.ds(0, D)]),
                (wk_hbm, mixed.at[pl.ds(D, D)]),
                (wv_hbm, weights),
                (frames_hbm, frames),
                (middle_hbm, middle),
            )
        )
    ]
    for load in loads[:1] + loads[4:]:
        load.start()

    barrier = pltpu.get_barrier_semaphore()
    for device in [by_row(j) for j in (1, 2, 3)] + [by_grp(bit) for bit in bits]:
        pl.semaphore_signal(barrier, inc=1, device_id=device, device_id_type=MESH)
    pl.semaphore_wait(barrier, 3 + len(bits))

    gather_chain("e", early_got, early_out, fold)
    early_got[my_row] = early_in[...]
    start("e")
    land, first_row = 0, 0
    for number, (count, order) in enumerate(FEED_PIECES):
        land = feed_chain(f"f{number}", (first_row, count), order, land)
        first_row += count
        start(f"f{number}")

    lanes_of = slice(0, 256)
    for j in range(4):
        mixed[pl.ds(pl.multiple_of((my_row ^ j) * block, block), block), lanes_of] = grads_in[j]
    ahead = roll_matrix(place[1])

    def turn(i, carry):
        cols = pl.ds(pl.multiple_of(i * TILE, TILE), TILE)
        after = pl.ds(pl.multiple_of((i + 1) % steps * TILE, TILE), TILE)
        part = matdot(ahead[:, :TILE], mixed[cols, lanes_of], 1, 0)
        part = (part + matdot(ahead[:, TILE:], mixed[after, lanes_of], 1, 0)).T
        grad_t[:, cols] = part.astype(BF)
        for head in range(4):
            mine = slice((head % 2) * HEAD_DIM, (head % 2 + 1) * HEAD_DIM)
            crossed = part[head * HEAD_DIM : (head + 1) * HEAD_DIM] * (ot0, ot1)[head // 2][
                mine, cols
            ].astype(F32)
            row_dots[head : head + 1, cols] = jnp.sum(crossed, axis=0, keepdims=True)
        return carry

    lax.fori_loop(0, steps, turn, 0)
    loads[1].start()
    loads[0].wait()

    def run(pair, here, spans, allowed):
        lanes = slice(pair * 128, (pair + 1) * 128)
        lse = (lse0, lse1)[pair]
        for head in range(2):
            mine = slice(head * HEAD_DIM, (head + 1) * HEAD_DIM)
            wide = slice(pair * 128 + head * HEAD_DIM, pair * 128 + (head + 1) * HEAD_DIM)
            dots = slice(2 * pair + head, 2 * pair + head + 1)
            grad_query = None
            for first, count in spans:
                keys = pl.ds(first, count)
                scores = matdot(k[keys, lanes], one_head(qt[lanes, here], head), 1, 0)
                if allowed is not None:
                    scores = jnp.where(allowed, scores, -1e30)
                probs = jnp.exp(scores - lse[head : head + 1, here])
                grad_probs = matdot(v[keys, lanes], one_head(grad_t[lanes, here], head), 1, 0)
                grad_scores = (probs * (grad_probs - row_dots[dots, here])).astype(BF)
                part = matdot(kt[wide, keys], grad_scores, 1, 0)
                grad_query = part if grad_query is None else grad_query + part
                dkt[mine, keys] += matdot(qt[wide, here], grad_scores, 1, 1)
                dvt[mine, keys] += matdot(grad_t[wide, here], probs.astype(BF), 1, 1)
            dqt[mine, here] = grad_query * HEAD_DIM**-0.5

    def finish(pair):
        def part(i, sums):
            cols = pl.ds(pl.multiple_of(i * TILE, TILE), TILE)
            cosine, sine = cos_t[:, cols], sin_t[:, cols]

            def turned(ref):
                parts = []
                for at_row in range(0, 128, HEAD_DIM):
                    first = ref[at_row : at_row + half, cols]
                    second = ref[at_row + half : at_row + HEAD_DIM, cols]
                    parts.append(first * cosine + second * sine)
                    parts.append(second * cosine - first * sine)
                return jnp.concatenate(parts, 0)

            columns = jnp.concatenate([turned(dqt), turned(dkt), dvt[:, cols]], 0)
            nat_ref[:, pl.ds(pl.multiple_of(TILE + i * TILE, TILE), TILE)] = columns.astype(BF)
            low = columns.T.astype(BF)
            rolled[cols, :] = low
            return sums + jnp.sum(low.astype(F32), axis=0, keepdims=True)

        sums = lax.fori_loop(0, steps, part, jnp.zeros((1, 384), F32))
        if pair == 1:
            for copy in copies_of("d0", 0):
                copy.wait_send()
        unroll(
            [got_d.at[my_row, pair]] + [send_d.at[j] for j in range(3)], nat_ref, my_row, place[1], block
        )
        chains[f"d{pair}"] = [
            (
                lambda: [(send_d.at[j - 1], got_d.at[my_row, pair], by_row(j)) for j in (1, 2, 3)],
                nothing,
            )
        ]
        start(f"d{pair}")
        run_hook(("fin", pair, 0))
        if pair == 0:
            loads[1].wait()
        for shard in range(4):
            columns = mixed[:, shard * 256 : (shard + 1) * 256]
            dw[pair, shard] = contract_rows(columns, rolled[...]).astype(BF)
        lane = 0
        for number, (count, order) in enumerate(HEAD_PIECES[pair]):
            heads_chain(f"q{pair}{number}", pair, number, pl.ds(lane, count), order)
            start(f"q{pair}{number}")
            lane += count
        return sums

    bias_sums = []
    for pair in range(2):
        dkt[...] = jnp.zeros_like(dkt)
        dvt[...] = jnp.zeros_like(dvt)

        def tile(i, carry):
            run(pair, pl.ds(pl.multiple_of(i * TILE, TILE), TILE), BACK_SPANS, None)
            for when in range(steps - 1):
                if ("tile", pair, when) in HOOKS:
                    pl.when(i == when)(functools.partial(run_hook, ("tile", pair, when)))
            return carry

        lax.fori_loop(0, steps - 1, tile, 0)
        tail = total - LONGEST
        run(pair, pl.ds(LONGEST, tail), [(LONGEST, tail)], seg_col[...] == seg_row[...])
        run_hook(("tile", pair, steps - 1))
        bias_sums.append(finish(pair))
        if pair == 1:
            for load in loads[2:4]:
                load.start()
        run_hook(("fin", pair, 1))

    for pair in range(2):
        advance(f"d{pair}", 0)
    for load in loads[2:]:
        load.wait()
    late = [jnp.zeros((1, 2 * D), F32) for _ in range(4)]
    for part in range(block // TILE):
        rows = slice(part * TILE, (part + 1) * TILE)
        grad = jnp.zeros((TILE, D), F32)
        for kind in range(3):
            pieces = [
                got_d[owner, pair, rows, kind * 128 : (kind + 1) * 128]
                for owner in range(4)
                for pair in range(2)
            ]
            weight = weights[...] if kind == 2 else mixed[kind * D : (kind + 1) * D]
            grad = grad + against(jnp.concatenate(pieces, 1), weight)
        normed, factor = normalize(frames[rows, :].astype(F32))
        scale = jnp.ones((TILE, D), F32)
        for u in range(scale_rows.shape[0]):
            scale = scale + member[rows, u : u + 1] * scale_rows[u : u + 1, :]
        back = normalize_back(grad * scale, normed, factor)
        frames_grad[rows, :] = (middle[rows, :] + back).astype(BF)
        for u in range(4):
            mark = member[rows, u : u + 1]
            late[u] += jnp.concatenate(
                [jnp.sum(t * mark, axis=0, keepdims=True) for t in (grad, grad * normed)], 1
            )
        if part == 0:
            run_hook(("epi", 0, 0))

    widths = [slice(kind * 128, (kind + 1) * 128) for kind in range(3)]
    bias_row = jnp.concatenate(
        [bias_sums[pair][:, w] for w in widths for pair in range(2)]
        + [jnp.zeros((1, 2 * D - 768), F32)],
        1,
    )
    index = lax.broadcasted_iota(jnp.int32, (8, 2 * D), 0)
    gather_chain(
        "l", late_got, late_out, lambda sums: fold(jnp.where(index == 4, bias_row, sums))
    )
    late_got[my_row] = jnp.concatenate(late + [jnp.zeros((4, 2 * D), F32)], 0)
    start("l")
    run_hook(("epi", 1, 0))
    for number in range(3, len(bits)):
        advance("e", number + 1)
        advance("l", number + 1)
    for name, step in started:
        if name != "d0":
            for copy in copies_of(name, step):
                copy.wait_send()


def attend_back(
    n_grp, place, qt, k, kt, v, heads_t, lse, seg_col, seg_row, cos_t, sin_t, early, member,
    scale_rows, grads, mixed, packed, weights, frames, middle,
):
    total = k.shape[0]
    block = total // 4
    rows = packed.shape[1]
    extra = max(0, len(bits_of(n_grp)) - 3)
    inputs = [
        qt, k, kt, v, *heads_t, *lse, seg_col, seg_row, cos_t, sin_t, early, member, scale_rows, grads,
    ]
    far = [mixed, packed, *weights, frames, middle]
    copies = 120
    return pl.pallas_call(
        functools.partial(back_kernel, n_grp),
        out_shape=[
            jax.ShapeDtypeStruct((block, D), BF),
            jax.ShapeDtypeStruct((rows, D), BF),
            jax.ShapeDtypeStruct((4, 256, 384), BF),
            jax.ShapeDtypeStruct((4, 256, 384), BF),
            jax.ShapeDtypeStruct((n_grp, 16, 2 * D), BF),
            jax.ShapeDtypeStruct((n_grp, 16, D), BF),
        ],
        in_specs=[pl.BlockSpec(memory_space=SMEM)]
        + [pl.BlockSpec(memory_space=VMEM)] * len(inputs)
        + [pl.BlockSpec(memory_space=pl.ANY)] * len(far),
        out_specs=[pl.BlockSpec(memory_space=VMEM)] * 6,
        scratch_shapes=[
            VMEM((256, total), BF),
            VMEM((8, total), F32),
            VMEM((128, total), F32),
            VMEM((128, total), F32),
            VMEM((128, total), F32),
            VMEM((384, total + TILE), BF),
            VMEM((total, 384), BF),
            VMEM((total, D), BF),
            VMEM((2, rows, D), BF),
            VMEM((D, D), BF),
            VMEM((block, D), BF),
            VMEM((block, D), F32),
            VMEM((rows * (15 + extra) // 8, D), BF),
            VMEM((2, 4, 256, 384), BF),
            VMEM((3, block, 384), BF),
            VMEM((4, 2, block, 384), BF),
            VMEM((4, 8, 4 * D), F32),
            VMEM((4, 8, 2 * D), F32),
            VMEM((2, 4, 256, 384), BF),
            VMEM((max(1, 8 * extra), 32, 384), BF),
            pltpu.SemaphoreType.DMA((copies,)),
            pltpu.SemaphoreType.DMA((copies,)),
            pltpu.SemaphoreType.DMA((len(far),)),
        ],
        compiler_params=pltpu.CompilerParams(
            vmem_limit_bytes=62 << 20, collective_id=1, has_side_effects=True
        ),
        cost_estimate=pl.CostEstimate(
            flops=4 * 2 * 5 * total * LONGEST * 256,
            bytes_accessed=40 << 20,
            transcendentals=4 * total * LONGEST,
        ),
        name="attend_back",
    )(place, *inputs, *far)


def feed_kernel(
    o, frames, cot, mod, member, out_bias, up_bias, down_bias, out_hbm, up_hbm, down_hbm,
    output, middle_out, grads_out, packed, early_out,
    w_out, w_up, w_down, h_s, a_s, ez_s, eb_s, ea_s, send_o, send_w, got_w, load_sem, send_sem, recv_sem,
):
    my_row = lax.axis_index("row")
    by_row = lambda j: {"row": my_row ^ j}
    rows_all = frames.shape[0]
    width = D // 4
    loads = [
        pltpu.make_async_copy(
            out_hbm.at[pl.ds(pl.multiple_of((my_row ^ j) * width, width), width)],
            w_out.at[pl.ds(j * width, width)],
            load_sem.at[j],
        )
        for j in range(4)
    ] + [
        pltpu.make_async_copy(up_hbm, w_up, load_sem.at[4]),
        pltpu.make_async_copy(down_hbm, w_down, load_sem.at[5]),
    ]
    for load in loads:
        load.start()
    barrier = pltpu.get_barrier_semaphore()
    for j in (1, 2, 3):
        pl.semaphore_signal(barrier, inc=1, device_id=by_row(j), device_id_type=MESH)
    pl.semaphore_wait(barrier, 3)

    def remote(number, src, dst, j):
        return pltpu.make_async_remote_copy(
            src, dst, send_sem.at[number], recv_sem.at[number], device_id=by_row(j), device_id_type=MESH
        )

    copies = []
    coef = math.sqrt(2.0 / math.pi)
    sums = [[jnp.zeros((1, D), F32) for _ in range(4)] for _ in range(4)]
    bias_sums = [jnp.zeros((1, n), F32) for n in (D, 2 * D, D)]
    for tile in range(rows_all // TILE):
        rows = slice(tile * TILE, (tile + 1) * TILE)
        marks = [member[rows, u : u + 1] for u in range(4)]

        def per_row(block):
            total = marks[0] * mod[0:1, block * D : (block + 1) * D]
            for u in range(1, 4):
                total = total + marks[u] * mod[u : u + 1, block * D : (block + 1) * D]
            return total

        gate_a, shift_f, scale_f, gate_f = per_row(2), per_row(3), 1.0 + per_row(4), per_row(5)
        if tile == 0:
            for load in loads[:4]:
                load.wait()
        heads = jnp.concatenate([o[j, rows, :] for j in range(4)], 1)
        attended = matdot(heads, w_out[...], 1, 0) + out_bias[...]
        middle = frames[rows, :].astype(F32) + gate_a * attended
        normed, factor = normalize(middle)
        h = (normed * scale_f + shift_f).astype(BF)
        h_s[rows, :] = h
        if tile == 0:
            loads[4].wait()
        z = matdot(h, w_up[...], 1, 0) + up_bias[...]
        square = z * z
        curve = jnp.tanh(coef * (z * (1.0 + 0.044715 * square)))
        share = 0.5 * (1.0 + curve)
        a = (z * share).astype(BF)
        a_s[rows, :] = a
        slope = share + (0.5 * coef) * z * (1.0 - curve * curve) * (1.0 + (3 * 0.044715) * square)
        if tile == 0:
            loads[5].wait()
        branch = matdot(a, w_down[...], 1, 0) + down_bias[...]
        output[rows, :] = (middle + gate_f * branch).astype(BF)
        upstream = cot[rows, :].astype(F32)
        e_b = (upstream * gate_f).astype(BF)
        eb_s[rows, :] = e_b
        e_z = (against(e_b, w_down[...]) * slope).astype(BF)
        ez_s[rows, :] = e_z
        e_h = against(e_z, w_up[...])
        e_mid = upstream + normalize_back(e_h * scale_f, normed, factor)
        middle_out[rows, :] = e_mid
        e_att = (e_mid * gate_a).astype(BF)
        ea_s[rows, :] = e_att
        e_o = against(e_att, w_out[...]).astype(BF)
        grads_out[0, rows, :] = e_o[:, :width]
        for j in (1, 2, 3):
            send_o[j - 1, rows, :] = e_o[:, j * width : (j + 1) * width]
            copies.append(
                remote(
                    len(copies), send_o.at[j - 1, pl.ds(tile * TILE, TILE)],
                    grads_out.at[j, pl.ds(tile * TILE, TILE)], j,
                )
            )
            copies[-1].start()
        for block, part in enumerate((e_mid * attended, e_h, e_h * normed, upstream * branch)):
            for u in range(4):
                sums[u][block] += jnp.sum(part * marks[u], axis=0, keepdims=True)
        for number, part in enumerate((e_att, e_z, e_b)):
            bias_sums[number] += jnp.sum(part.astype(F32), axis=0, keepdims=True)

    early_out[...] = jnp.concatenate(
        [jnp.concatenate(row, 1) for row in sums + [bias_sums]] + [jnp.zeros((3, 4 * D), F32)], 0
    )

    def shard(j, store):
        owner = my_row ^ j
        columns = pl.ds(pl.multiple_of(owner * 2 * width, 2 * width), 2 * width)
        store(768, contract_rows(a_s[:, columns], eb_s[...]))
        columns = pl.ds(pl.multiple_of(owner * width, width), width)
        store(256, contract_rows(h_s[:, columns], ez_s[:, :D]))
        store(512, contract_rows(h_s[:, columns], ez_s[:, D:]))
        store(0, contract_rows(o[j], ea_s[...]))

    for slot, j in enumerate((1, 3)):

        def store(first, value):
            send_w[slot, first : first + value.shape[0], :] = value.astype(BF)

        shard(j, store)
        copies.append(remote(len(copies), send_w.at[slot], got_w.at[slot], 1))
        copies[-1].start()
    for slot, j in enumerate((0, 2)):

        def store(first, value):
            packed[slot, first : first + value.shape[0], :] = value.astype(BF)

        shard(j, store)
    for slot in range(2):
        copies[-2 + slot].wait_recv()
        packed[slot] = add_low(packed[slot], got_w[slot])
    for copy in copies[:-2]:
        copy.wait_recv()
    for copy in copies:
        copy.wait_send()


def feed(o, frames, cot, mod, member, biases, weights):
    rows = frames.shape[0]
    inputs = [o, frames, cot, mod, member, *[b[None] for b in biases]]
    return pl.pallas_call(
        feed_kernel,
        out_shape=[
            jax.ShapeDtypeStruct((rows, D), BF),
            jax.ShapeDtypeStruct((rows, D), F32),
            jax.ShapeDtypeStruct((4, rows, D // 4), BF),
            jax.ShapeDtypeStruct((2, 1280, D), BF),
            jax.ShapeDtypeStruct((8, 4 * D), F32),
        ],
        in_specs=[pl.BlockSpec(memory_space=VMEM)] * len(inputs)
        + [pl.BlockSpec(memory_space=pl.ANY)] * 3,
        out_specs=[pl.BlockSpec(memory_space=VMEM)] * 5,
        scratch_shapes=[
            VMEM((D, D), BF),
            VMEM((D, 2 * D), BF),
            VMEM((2 * D, D), BF),
            VMEM((rows, D), BF),
            VMEM((rows, 2 * D), BF),
            VMEM((rows, 2 * D), BF),
            VMEM((rows, D), BF),
            VMEM((rows, D), BF),
            VMEM((3, rows, D // 4), BF),
            VMEM((2, 1280, D), BF),
            VMEM((2, 1280, D), BF),
            pltpu.SemaphoreType.DMA((6,)),
            pltpu.SemaphoreType.DMA((3 * rows // TILE + 2,)),
            pltpu.SemaphoreType.DMA((3 * rows // TILE + 2,)),
        ],
        compiler_params=pltpu.CompilerParams(
            vmem_limit_bytes=LIMIT, collective_id=2, has_side_effects=True
        ),
        cost_estimate=pl.CostEstimate(
            flops=2 * rows * D * 15 * D, bytes_accessed=30 << 20, transcendentals=rows * 2 * D
        ),
        name="feed",
    )(*inputs, *weights)


def outputs_kernel(
    packed, heads_0, heads_1, early, late, act, embedding, mod_weight_hbm,
    out_w, up_w, down_w, query_w, key_w, value_w, mod_w, mod_b, embed, out_b, up_b, down_b, query_b, key_b, value_b,
    mod_weight, rows_ref, mod_ref, load_sem,
):
    my_row = lax.axis_index("row")
    width = D // 4
    load = pltpu.make_async_copy(mod_weight_hbm, mod_weight, load_sem)
    load.start()
    n_grp = early.shape[0]
    out_w[...] = packed[:width].astype(F32)
    up_w[:, :D] = packed[width : 2 * width].astype(F32)
    up_w[:, D:] = packed[2 * width : 3 * width].astype(F32)
    down_w[...] = packed[3 * width :].astype(F32)
    for pair, heads in enumerate((heads_0, heads_1)):
        for j in range(4):
            lanes = pl.ds(pl.multiple_of((my_row ^ j) * width + pair * 128, 128), 128)
            for kind, out in enumerate((query_w, key_w, value_w)):
                out[:, lanes] = heads[j, :, kind * 128 : (kind + 1) * 128].astype(F32)
    for first, source, count in ((0, late, D), (2 * D, early, 2 * D)):
        for part in range(2):
            rows = source[:, 8 * part : 8 * part + 8].astype(F32).reshape(n_grp * 8, count)
            mod_ref[:, first + part * count : first + (part + 1) * count] = rows
    number = lax.broadcasted_iota(jnp.int32, (n_grp * 8, 1), 0) % 8
    utterance, bias = (number < 4).astype(F32), (number == 4).astype(F32)
    for block in range(6):
        lanes = slice(block * D, (block + 1) * D)
        rows = mod_ref[:, lanes]
        mod_w[:, lanes] = contract_rows(
            act[:, pl.ds(pl.multiple_of(my_row * width, width), width)], rows.astype(BF)
        )
        sums = [jnp.sum(rows * mark, axis=0, keepdims=True) for mark in (utterance, bias)]
        rows_ref[:, lanes] = jnp.concatenate(sums + [jnp.zeros((6, D), F32)], 0)

    def own(row, first, size):
        lanes = pl.ds(pl.multiple_of(first + my_row * size, 128), size)
        return rows_ref[row : row + 1, lanes]

    mod_b[...] = own(0, 0, 6 * width)
    for i, out in enumerate((query_b, key_b, value_b)):
        out[...] = rows_ref[1:2, i * width : (i + 1) * width]
    out_b[...] = own(1, 2 * D, width)
    up_b[...] = own(1, 3 * D, 2 * width)
    down_b[...] = own(1, 5 * D, width)
    load.wait()
    grad = against(mod_ref[:8].astype(BF), mod_weight[...])[:4]
    gate = 1.0 / (1.0 + jnp.exp(-embedding[...]))
    embed[...] = grad * (gate * (1.0 + embedding[...] * (1.0 - gate)))


def outputs(packed, heads_0, heads_1, early, late, act, embedding, mod_weight):
    width = D // 4
    n_grp = early.shape[0]
    shapes = [(width, D), (width, 2 * D), (2 * width, D)] + [(width, D)] * 3 + [(width, 6 * D)]
    shapes += [(1, 6 * width), (4, D)] + [(1, n) for n in (width, 2 * width, width, width, width, width)]
    return pl.pallas_call(
        outputs_kernel,
        out_shape=[jax.ShapeDtypeStruct(shape, F32) for shape in shapes],
        in_specs=[pl.BlockSpec(memory_space=VMEM)] * 7 + [pl.BlockSpec(memory_space=pl.ANY)],
        out_specs=[pl.BlockSpec(memory_space=VMEM)] * len(shapes),
        scratch_shapes=[
            VMEM((D, 6 * D), BF),
            VMEM((8, 6 * D), F32),
            VMEM((n_grp * 8, 6 * D), F32),
            pltpu.SemaphoreType.DMA,
        ],
        compiler_params=pltpu.CompilerParams(vmem_limit_bytes=LIMIT),
        name="outputs",
    )(packed, heads_0, heads_1, early, late, act, embedding, mod_weight)


def local(
    frames, time_embed, lengths, mod_weight, mod_bias, query_weight, query_bias, key_weight, key_bias,
    value_weight, value_bias, out_weight, out_bias, up_weight, up_bias, down_weight, down_bias, cotangent,
):
    n_grp = lax.axis_size("grp")
    row_count = frames.shape[0]
    my_row = lax.axis_index("row")
    group_rows = row_count * lax.axis_size("row")
    width = D // 4

    from_core = exchange(frames, "row", 1)
    from_x = exchange(frames, "row", 2)
    from_both = exchange(from_x, "row", 1)

    utt_sizes = lengths[0]
    finish = jnp.cumsum(utt_sizes)
    starts = finish - utt_sizes
    longest = jnp.argmax(utt_sizes)
    offset = starts[longest]
    place = jnp.stack([my_row, offset]).astype(jnp.int32)
    utts = jnp.arange(utt_sizes.shape[0], dtype=jnp.int32)

    def layout(rows):
        segment = jnp.sum((rows[:, None] >= finish[None, :]).astype(jnp.int32), axis=1)
        is_member = segment[:, None] == utts[None, :]
        position = rows - jnp.sum(jnp.where(is_member, starts[None, :], 0), axis=1)
        return segment, is_member.astype(F32), position

    rolled_rows = (jnp.arange(group_rows, dtype=jnp.int32) + offset) % group_rows
    segment, member_rolled, position = layout(rolled_rows)
    half = HEAD_DIM // 2
    frequency = jnp.exp(jnp.arange(half, dtype=F32) * (-2.0 * math.log(10000.0) / HEAD_DIM))
    angles = frequency[:, None] * position.astype(F32)[None, :]
    cos_t, sin_t = jnp.cos(angles), jnp.sin(angles)
    seg_tail = segment[LONGEST:]
    seg_col, seg_row = seg_tail[:, None], seg_tail[None, :]
    own_rows = my_row * row_count + jnp.arange(row_count, dtype=jnp.int32)
    _, member, _ = layout(own_rows)

    col_part = lambda w, j: lax.dynamic_slice_in_dim(w, (my_row ^ j) * width, width, 1)
    weight_t = jnp.concatenate(
        [col_part(w, 0).T for w in (query_weight, key_weight, value_weight)], 0
    )
    own_part = lambda b: lax.dynamic_slice_in_dim(b, my_row * width, width, 0)
    bias_t = jnp.concatenate([own_part(query_bias), own_part(key_bias), own_part(value_bias)])[:, None]
    embedding = time_embed[0]
    act_low = jax.nn.silu(embedding).astype(BF)
    modulation = jnp.dot(act_low, mod_weight, preferred_element_type=F32) + mod_bias
    mod_long = lax.dynamic_slice_in_dim(modulation[:, : 2 * D], longest, 1, 0)
    act_all = jnp.pad(act_low, ((0, 4), (0, 0)))
    for bit in bits_of(n_grp):
        act_all = jnp.concatenate([act_all, exchange(act_all, "grp", bit)], 0)

    mixed, qt, kt, vt, k_rows, v_rows = project(
        place, (frames, from_core, from_x, from_both), modulation[:, : 2 * D], mod_long,
        member_rolled[LONGEST:], weight_t, bias_t, cos_t, sin_t,
    )

    *heads_t, lse0, lse1, o_all = attend(place, qt, k_rows, vt, seg_col, seg_row)
    log_totals = [lse0, lse1]
    member_8 = jnp.pad(member, ((0, 0), (0, 4)))
    output, grad_middle, grad_pieces, packed, early = feed(
        o_all, frames, cotangent, modulation, member_8, (out_bias, up_bias, down_bias),
        (out_weight, up_weight, down_weight),
    )
    grad_frames, packed_total, heads_0, heads_1, early_all, late_all = attend_back(
        n_grp, place, qt, k_rows, kt, v_rows, heads_t, log_totals, seg_col, seg_row, cos_t, sin_t,
        early, member_8, modulation[:, D : 2 * D], grad_pieces, mixed, packed,
        (query_weight, key_weight, value_weight), frames, grad_middle,
    )

    grads = outputs(
        packed_total, heads_0, heads_1, early_all, late_all, act_all, embedding, mod_weight
    )
    out_grad, up_grad, down_grad, query_grad, key_grad, value_grad, mod_weight_grad = grads[:7]
    mod_bias_grad, grad_embedding = grads[7][0], grads[8]
    out_b, up_b, down_b, query_b, key_b, value_b = (b[0] for b in grads[9:])
    return (
        output,
        grad_frames,
        grad_embedding[None],
        mod_weight_grad,
        mod_bias_grad,
        query_grad,
        query_b,
        key_grad,
        key_b,
        value_grad,
        value_b,
        out_grad,
        out_b,
        up_grad,
        up_b,
        down_grad,
        down_b,
    )


def solution(mesh):
    placed = (
        (P(("grp", "row"), None), P("grp", None, None), P("grp", None))
        + (P(),) * 14
        + (P(("grp", "row"), None),)
    )
    return jax.shard_map(
        local,
        mesh=mesh,
        in_specs=placed,
        out_specs=(
            P(("grp", "row"), None),
            P(("grp", "row"), None),
            P("grp", None, None),
        )
        + (P("row", None), P("row")) * 7,
        check_vma=False,
    )
```

```python
import functools
import math

import jax
import jax.numpy as jnp
import numpy as np
from jax import lax
from jax.experimental import pallas as pl
from jax.experimental.pallas import tpu as pltpu
from jax.sharding import PartitionSpec as P

D = 1024
HEADS = 16
HEAD_DIM = 64
LONGEST = 1792
TILE = 256
BF = jnp.bfloat16
F32 = jnp.float32

highest = lax.Precision.HIGHEST
VMEM = pltpu.VMEM
SMEM = pltpu.SMEM
LIMIT = 60 << 20
MESH = pl.DeviceIdType.MESH
BACK_SPANS = [(0, 896), (896, 896)]


def matdot(left, right, left_dim, right_dim):
    return lax.dot_general(
        left, right, (((left_dim,), (right_dim,)), ((), ())), preferred_element_type=F32
    )


def contract_rows(left, right):
    return matdot(left, right, 0, 0)


def against(left, weight):
    return matdot(left, weight, 1, 1)


def column_sum(tensor):
    return jnp.sum(tensor.astype(F32), axis=0)


def normalize(tensor):
    centred = tensor - jnp.mean(tensor, axis=-1, keepdims=True)
    factor = lax.rsqrt(jnp.mean(centred * centred, axis=-1, keepdims=True) + 1e-06)
    return (centred * factor, factor)


def normalize_back(grad_normed, normed, factor):
    mean_grad = jnp.mean(grad_normed, axis=-1, keepdims=True)
    mean_cross = jnp.mean(grad_normed * normed, axis=-1, keepdims=True)
    return (grad_normed - mean_grad - normed * mean_cross) * factor


def exchange(tensor, axis, bit):
    size = lax.axis_size(axis)
    return lax.ppermute(tensor, axis, [(i, i ^ bit) for i in range(size)])


def add_low(left, right):
    return (left.astype(F32) + right.astype(F32)).astype(BF)


def bits_of(count):
    return [1 << i for i in range(count.bit_length() - 1)]


def roll_matrix(offset):
    row = lax.broadcasted_iota(jnp.int32, (TILE, 2 * TILE), 0)
    col = lax.broadcasted_iota(jnp.int32, (TILE, 2 * TILE), 1)
    return (col == row + offset).astype(F32).astype(BF)


def layout_of(lengths):
    sizes = [lengths[u] for u in range(4)]
    starts, finish, at = [], [], 0
    for size in sizes:
        starts.append(at)
        at = at + size
        finish.append(at)
    offset = 0
    for size, first in zip(sizes, starts):
        offset = offset + jnp.where(size == LONGEST, first, 0)
    return sizes, starts, finish, offset


def marks_of(rows, starts, finish):
    return [
        jnp.logical_and(rows >= first, rows < end).astype(F32) for first, end in zip(starts, finish)
    ]


def tail_allowed(finish, offset, total):
    count = total - LONGEST

    def segment(shape, dim):
        rows = LONGEST + offset + lax.broadcasted_iota(jnp.int32, shape, dim)
        rows = jnp.where(rows >= total, rows - total, rows)
        return sum((rows >= end).astype(jnp.int32) for end in finish)

    return segment((count, 1), 0) == segment((1, count), 1)


def project_kernel(
    lengths, embedding, mod_bias, q_bias, k_bias, v_bias, frequency,
    frames_hbm, mod_weight_hbm, wq_hbm, wk_hbm, wv_hbm,
    mixed_out, qt_out, kt_out, vt_out, k_out, v_out, cos_out, sin_out, mod_out, act_out,
    rows_ref, roll_ref, mod_weight, weight, weight_t, bias_t, send_sem, recv_sem, load_sem,
):
    my_row = lax.axis_index("row")
    block = frames_hbm.shape[0]
    total = 4 * block
    steps = total // TILE
    width = qt_out.shape[0]
    by_row = lambda j: {"row": my_row ^ j}
    sizes, starts, finish, offset = layout_of(lengths)

    def place(j, part=0, count=None):
        first = pl.multiple_of((my_row ^ j) * block + part * TILE, TILE)
        return pl.ds(first, count or TILE)

    def remote(number, src, dst, j):
        return pltpu.make_async_remote_copy(
            src, dst, send_sem.at[number], recv_sem.at[number], device_id=by_row(j), device_id_type=MESH
        )

    parts = block // TILE
    barrier = pltpu.get_barrier_semaphore()
    for j in (1, 2):
        pl.semaphore_signal(barrier, inc=1, device_id=by_row(j), device_id_type=MESH)
    pl.semaphore_wait(barrier, 2)
    to_x = [
        remote(i, frames_hbm.at[pl.ds(i * TILE, TILE)], rows_ref.at[place(0, i)], 2) for i in range(parts)
    ]
    to_core = remote(parts, frames_hbm, rows_ref.at[place(0, 0, block)], 1)
    onward = [
        remote(parts + 1 + i, rows_ref.at[place(2, i)], rows_ref.at[place(2, i)], 1) for i in range(parts)
    ]
    for copy in to_x + [to_core]:
        copy.start()
    columns = pl.ds(pl.multiple_of(my_row * width, width), width)
    loads = [
        pltpu.make_async_copy(src, dst, load_sem.at[i])
        for i, (src, dst) in enumerate(
            [(frames_hbm, rows_ref.at[place(0, 0, block)])]
            + [
                (w.at[:, columns], weight.at[:, pl.ds(i * width, width)])
                for i, w in enumerate((wq_hbm, wk_hbm, wv_hbm))
            ]
            + [
                (mod_weight_hbm.at[:, pl.ds(i * 2 * D, 2 * D)], mod_weight.at[i]) for i in range(3)
            ]
        )
    ]
    for load in loads:
        load.start()

    rows = lax.broadcasted_iota(jnp.int32, (1, total), 1) + offset
    rows = jnp.where(rows >= total, rows - total, rows)
    position = rows
    for first, end in zip(starts, finish):
        inside = jnp.logical_and(rows >= first, rows < end)
        position = jnp.where(inside, rows - first, position)
    angles = frequency[...] * position.astype(F32)
    cos_out[...] = jnp.cos(angles)
    sin_out[...] = jnp.sin(angles)
    roll_ref[...] = roll_matrix(offset)
    for i, bias in enumerate((q_bias, k_bias, v_bias)):
        bias_t[i : i + 1, :] = bias[0:1, columns]

    act = (embedding[...] / (1.0 + jnp.exp(-embedding[...]))).astype(BF).astype(F32)
    act_out[...] = jnp.concatenate([act[u : u + 1] for u in range(4)], 1)
    act_low = jnp.concatenate([act, jnp.zeros_like(act)], 0).astype(BF)
    for i in range(3):
        lanes = slice(i * 2 * D, (i + 1) * 2 * D)
        loads[4 + i].wait()
        mod_out[:, lanes] = matdot(act_low, mod_weight[i], 1, 0) + mod_bias[:, lanes]
    for load in loads[:4]:
        load.wait()
    for i in range(3):
        lanes = slice(i * width, (i + 1) * width)
        weight_t[lanes, :] = weight[:, lanes].T
    biases = jnp.concatenate([bias_t[i : i + 1, :] for i in range(3)], 1)
    biases = jnp.broadcast_to(biases, (8, 3 * width)).T[:, 0:1]

    mod_long = jnp.zeros((1, 2 * D), F32)
    for u in range(4):
        mod_long = mod_long + jnp.where(sizes[u] == LONGEST, 1.0, 0.0) * mod_out[u : u + 1, : 2 * D]
    half = HEAD_DIM // 2

    def tile(step):
        here = pl.ds(pl.multiple_of(step * TILE, TILE), TILE)
        after = pl.ds(pl.multiple_of((step + 1) % steps * TILE, TILE), TILE)
        moved = matdot(roll_ref[:, :TILE], rows_ref[here, :], 1, 0)
        normed, _ = normalize(moved + matdot(roll_ref[:, TILE:], rows_ref[after, :], 1, 0))

        @pl.when(step != steps - 1)
        def _():
            mixed_out[here, :] = (normed * (1.0 + mod_long[:, D:]) + mod_long[:, :D]).astype(BF)

        @pl.when(step == steps - 1)
        def _():
            spots = LONGEST + offset + lax.broadcasted_iota(jnp.int32, (TILE, 1), 0)
            spots = jnp.where(spots >= total, spots - total, spots)
            per_row = jnp.zeros((TILE, 2 * D), F32)
            for u, mark in enumerate(marks_of(spots, starts, finish)):
                per_row = per_row + mark * mod_out[u : u + 1, : 2 * D]
            mixed_out[here, :] = (normed * (1.0 + per_row[:, D:]) + per_row[:, :D]).astype(BF)

        wide = matdot(weight_t[...], mixed_out[here, :], 1, 1) + biases
        cosine, sine = cos_out[:, here], sin_out[:, here]

        def turned(base):
            out = []
            for at in range(base, base + width, HEAD_DIM):
                first, second = wide[at : at + half], wide[at + half : at + HEAD_DIM]
                out.append(first * cosine - second * sine)
                out.append(second * cosine + first * sine)
            return jnp.concatenate(out, 0)

        keys = turned(width)
        values = wide[2 * width :]
        qt_out[:, here] = turned(0).astype(BF) * jnp.asarray(HEAD_DIM**-0.5, BF)
        kt_out[:, here] = keys.astype(BF)
        vt_out[:, here] = values.astype(BF)
        k_out[here, :] = keys.T.astype(BF)
        v_out[here, :] = values.T.astype(BF)

    to_core.wait_recv()
    chip = my_row // 2 * (steps // 2)

    def near(i, carry):
        tile(chip + i)
        return carry

    def far(i, carry):
        tile((chip + i) % steps)
        return carry

    lax.fori_loop(0, steps // 2 - 1, near, 0)
    for arrived, copy in zip(to_x, onward):
        arrived.wait_recv()
        copy.start()
    for copy in onward:
        copy.wait_recv()
    lax.fori_loop(steps // 2 - 1, steps, far, 0)
    for copy in to_x + [to_core] + onward:
        copy.wait_send()


def project(lengths, frames, embedding, mod_weight, mod_bias, weights, biases):
    block = frames.shape[0]
    total = 4 * block
    width = D // 4
    half = HEAD_DIM // 2
    frequency = np.exp(np.arange(half) * (-2.0 * math.log(10000.0) / HEAD_DIM)).astype(np.float32)
    inputs = [embedding, mod_bias[None], *[b[None] for b in biases], jnp.asarray(frequency)[:, None]]
    far = [frames, mod_weight, *weights]
    copies = 1 + 2 * (block // TILE)
    return pl.pallas_call(
        project_kernel,
        out_shape=[
            jax.ShapeDtypeStruct((total, D), BF),
            jax.ShapeDtypeStruct((width, total), BF),
            jax.ShapeDtypeStruct((width, total), BF),
            jax.ShapeDtypeStruct((width, total), BF),
            jax.ShapeDtypeStruct((total, width), BF),
            jax.ShapeDtypeStruct((total, width), BF),
            jax.ShapeDtypeStruct((half, total), F32),
            jax.ShapeDtypeStruct((half, total), F32),
            jax.ShapeDtypeStruct((8, 6 * D), F32),
            jax.ShapeDtypeStruct((1, 4 * D), F32),
        ],
        in_specs=[pl.BlockSpec(memory_space=SMEM)]
        + [pl.BlockSpec(memory_space=VMEM)] * len(inputs)
        + [pl.BlockSpec(memory_space=pl.ANY)] * len(far),
        out_specs=[pl.BlockSpec(memory_space=VMEM)] * 10,
        scratch_shapes=[
            VMEM((total, D), BF),
            VMEM((TILE, 2 * TILE), BF),
            VMEM((3, D, 2 * D), BF),
            VMEM((D, 3 * width), BF),
            VMEM((3 * width, D), BF),
            VMEM((8, width), F32),
            pltpu.SemaphoreType.DMA((copies,)),
            pltpu.SemaphoreType.DMA((copies,)),
            pltpu.SemaphoreType.DMA((7,)),
        ],
        compiler_params=pltpu.CompilerParams(
            vmem_limit_bytes=LIMIT, collective_id=4, has_side_effects=True
        ),
        cost_estimate=pl.CostEstimate(
            flops=2 * total * D * 3 * width, bytes_accessed=40 << 20, transcendentals=total
        ),
        name="project",
    )(lengths, *inputs, *far)


def one_head(pair, head):
    part = pair[head * HEAD_DIM : (head + 1) * HEAD_DIM]
    empty = jnp.zeros_like(part)
    return jnp.concatenate([part, empty] if head == 0 else [empty, part], 0)


def unroll(outs, rolled_ref, my_row, offset, block):
    total = 4 * block
    rolled_ref[:, pl.ds(0, TILE)] = rolled_ref[:, pl.ds(total, TILE)]
    back = roll_matrix(TILE - offset)
    for j, out in enumerate(outs):
        for part in range(block // TILE):
            at = pl.multiple_of((my_row ^ j) * block + part * TILE, TILE)
            rows = matdot(back, rolled_ref[:, pl.ds(at, 2 * TILE)], 1, 1)
            out[part * TILE : (part + 1) * TILE, :] = rows.astype(BF)


def attend_kernel(
    lengths, qt, k, vt, ot0, ot1, lse0, lse1, o_all,
    rolled_ref, send_o, send_sem, recv_sem,
):
    my_row = lax.axis_index("row")
    total = k.shape[0]
    block = total // 4
    tail = total - LONGEST
    _, _, finish, offset = layout_of(lengths)
    barrier = pltpu.get_barrier_semaphore()
    for j in (1, 2, 3):
        pl.semaphore_signal(barrier, inc=1, device_id={"row": my_row ^ j}, device_id_type=MESH)
    pl.semaphore_wait(barrier, 3)

    def run(pair, here, first, count, allowed):
        outs, tops = [], []
        lanes = slice(pair * 128, (pair + 1) * 128)

        def scores_of(head):
            scores = matdot(k[first : first + count, lanes], one_head(qt[lanes, here], head), 1, 0)
            return scores if allowed is None else jnp.where(allowed, scores, -1e30)

        for head in range(2):
            tops.append(jnp.max(scores_of(head), axis=0, keepdims=True))
        for head in range(2):
            wide = slice(pair * 128 + head * HEAD_DIM, pair * 128 + (head + 1) * HEAD_DIM)
            weights = jnp.exp(scores_of(head) - tops[head]).astype(BF)
            values = jnp.concatenate([vt[wide, first : first + count], jnp.ones((16, count), BF)], 0)
            mixed = matdot(values, weights, 1, 0)
            exp_sum = mixed[HEAD_DIM : HEAD_DIM + 1]
            outs.append(mixed[:HEAD_DIM] / exp_sum)
            tops[head] = tops[head] + jnp.log(exp_sum)
        low = jnp.concatenate(outs, 0).astype(BF)
        (ot0, ot1)[pair][:, here] = low
        (lse0, lse1)[pair][:, here] = jnp.concatenate(tops * 4, 0)
        return low

    copies = []
    for pair in range(2):

        def tile(i, carry):
            low = run(pair, pl.ds(pl.multiple_of(i * TILE, TILE), TILE), 0, LONGEST, None)
            rolled_ref[:, pl.ds(pl.multiple_of(TILE + i * TILE, TILE), TILE)] = low
            return carry

        lax.fori_loop(0, LONGEST // TILE, tile, 0)
        low = run(pair, pl.ds(LONGEST, tail), LONGEST, tail, tail_allowed(finish, offset, total))
        rolled_ref[:, pl.ds(total, TILE)] = low
        lanes = pl.ds(pair * 128, 128)
        outs = [o_all.at[0, :, lanes]] + [send_o.at[3 * pair + j] for j in range(3)]
        unroll(outs, rolled_ref, my_row, offset, block)
        for j in (1, 2, 3):
            number = 3 * pair + j - 1
            copies.append(
                pltpu.make_async_remote_copy(
                    send_o.at[number], o_all.at[j, :, lanes], send_sem.at[number], recv_sem.at[number],
                    device_id={"row": my_row ^ j}, device_id_type=MESH,
                )
            )
            copies[-1].start()
    for copy in copies:
        copy.wait()


def attend(lengths, qt, k, vt):
    total = k.shape[0]
    block = total // 4
    return pl.pallas_call(
        attend_kernel,
        out_shape=[jax.ShapeDtypeStruct((128, total), BF)] * 2
        + [jax.ShapeDtypeStruct((8, total), F32)] * 2
        + [jax.ShapeDtypeStruct((4, block, 256), BF)],
        in_specs=[pl.BlockSpec(memory_space=SMEM)] + [pl.BlockSpec(memory_space=VMEM)] * 3,
        out_specs=[pl.BlockSpec(memory_space=VMEM)] * 5,
        scratch_shapes=[
            VMEM((128, total + TILE), BF),
            VMEM((6, block, 128), BF),
            pltpu.SemaphoreType.DMA((6,)),
            pltpu.SemaphoreType.DMA((6,)),
        ],
        compiler_params=pltpu.CompilerParams(
            vmem_limit_bytes=LIMIT, collective_id=3, has_side_effects=True
        ),
        cost_estimate=pl.CostEstimate(
            flops=2 * 2 * 4 * total * LONGEST * 256,
            bytes_accessed=8 << 20,
            transcendentals=4 * total * LONGEST,
        ),
        name="attend",
    )(lengths, qt, k, vt)


FEED_PIECES = ((384, ("x", 1, 2, 4)), (384, (2, 1, "x", 4)), (256, (1, 2, 4, "x")), (256, ("x", 1, 2, 4)),)
HEAD_PIECES = (
    ((384, (1, 2, 4)),),
    ((128, (1, 2, 4)), (128, (1, 2, 4)), (128, (1, 2, 4)),),
)
HOOKS = {
    ("tile", 0, 1): [("e", 0)],
    ("tile", 0, 2): [("f2", 0)],
    ("tile", 0, 3): [("e", 1)],
    ("tile", 0, 4): [("f1", 0)],
    ("tile", 0, 5): [("f0", 0), ("f2", 1)],
    ("tile", 0, 6): [("e", 2)],
    ("tile", 0, 7): [("f1", 1)],
    ("fin", 0, 0): [("f2", 2), ("f3", 0)],
    ("fin", 0, 1): [("f1", 2)],
    ("tile", 1, 0): [("f0", 1)],
    ("tile", 1, 1): [("e", 3), ("f3", 1)],
    ("tile", 1, 2): [("f1", 3)],
    ("tile", 1, 3): [("f0", 2), ("q00", 0)],
    ("tile", 1, 4): [("f2", 3), ("f3", 2)],
    ("tile", 1, 5): [("f1", 4)],
    ("tile", 1, 6): [("f0", 3)],
    ("tile", 1, 7): [("f1", 5), ("q00", 1)],
    ("fin", 1, 0): [("f2", 4), ("f3", 3)],
    ("fin", 1, 1): [("f0", 4), ("q10", 0), ("q11", 0), ("f1", 6), ("q12", 0), ("q00", 2)],
    ("epi", 0, 0): [("f2", 5), ("f3", 4), ("q00", 3)],
    ("epi", 1, 0): [("f0", 5), ("q10", 1), ("q11", 1), ("q12", 1), ("f2", 6), ("f3", 5), ("l", 0), ("q00", 4), ("q10", 2), ("f0", 6), ("q11", 2), ("q10", 3), ("q12", 2), ("q11", 3), ("q12", 3), ("f3", 6), ("l", 1), ("q00", 5), ("q10", 4), ("q11", 4), ("q12", 4), ("l", 2), ("q10", 5), ("q11", 5), ("q12", 5), ("q00", 6), ("q10", 6), ("l", 3), ("q11", 6), ("q12", 6)],
}


def back_kernel(
    n_grp, lengths, qt, k, kt, v, ot0, ot1, lse0, lse1, cos_t, sin_t, early_in, scale_rows,
    grads_in, mixed_hbm, packed_hbm, wq_hbm, wk_hbm, wv_hbm, frames_hbm, middle_hbm, mod_hbm,
    frames_grad, packed_out, qg0, qg1, early_out, late_out, embed_out,
    grad_t, row_dots, dqt, dkt, dvt, nat_ref, rolled, mixed, packed, weights, frames, middle,
    landing, dw, send_d, got_d, early_got, late_got, summed_q, q_extra,
    send_sem, recv_sem, load_sem,
):
    my_row, my_grp = lax.axis_index("row"), lax.axis_index("grp")
    total = k.shape[0]
    block = total // 4
    steps = total // TILE
    half = HEAD_DIM // 2
    _, starts, ends, offset = layout_of(lengths)
    bits = bits_of(n_grp)
    extra = bits[3:]
    side = lambda bit: (my_grp // bit) % 2
    by_row = lambda j: {"row": my_row ^ j}
    by_grp = lambda bit: {"grp": my_grp ^ bit}
    q_out = (qg0, qg1)

    chains, numbers, started = {}, {}, []

    def copies_of(name, step):
        out = []
        for index, (src, dst, device) in enumerate(chains[name][step][0]()):
            number = numbers.setdefault((name, step, index), len(numbers))
            out.append(
                pltpu.make_async_remote_copy(
                    src, dst, send_sem.at[number], recv_sem.at[number],
                    device_id=device, device_id_type=MESH,
                )
            )
        return out

    def start(name, step=0):
        started.append((name, step))
        for copy in copies_of(name, step):
            copy.start()

    def advance(name, step):
        for copy in copies_of(name, step):
            copy.wait_recv()
        chains[name][step][1]()
        if step + 1 < len(chains[name]):
            start(name, step + 1)

    def run_hook(mark):
        for name, step in HOOKS.get(mark, ()):
            advance(name, step)

    def one_step(number, src, dst, device):
        copy = pltpu.make_async_remote_copy(
            src, dst, send_sem.at[number], recv_sem.at[number], device_id=device, device_id_type=MESH
        )
        copy.start()
        copy.wait()

    def away(region, bit):
        offset, size = region
        return pl.ds(pl.multiple_of(offset + (1 - side(bit)) * (size // 2), 16), size // 2)

    def kept(region, bit):
        offset, size = region
        return (offset + side(bit) * (size // 2), size // 2)

    def at(region):
        return pl.ds(pl.multiple_of(region[0], 16), region[1])

    nothing = lambda: None

    def feed_chain(name, region, order, land):
        chain, areas, shards = [], [], (1, 0)
        for op in order:
            source = packed if chain else packed_hbm
            if op == "x":

                def parts(region=region, land=land, source=source):
                    return [(source.at[1, at(region)], landing.at[pl.ds(land, region[1])], by_row(2))]

                def take(region=region, land=land):
                    got = landing[land : land + region[1]]
                    packed[0, at(region)] = add_low(packed[0, at(region)], got)

                shards, land = (0,), land + region[1]
            else:
                size = region[1] // 2

                def parts(region=region, land=land, source=source, shards=shards, size=size, op=op):
                    return [
                        (
                            source.at[shard, away(region, op)],
                            landing.at[pl.ds(land + i * size, size)],
                            by_grp(op),
                        )
                        for i, shard in enumerate(shards)
                    ]

                region = kept(region, op)

                def take(region=region, land=land, shards=shards, size=size):
                    for i, shard in enumerate(shards):
                        got = landing[land + i * size : land + (i + 1) * size]
                        packed[shard, at(region)] = add_low(packed[shard, at(region)], got)

                land += size * len(shards)
                areas.append((op, region))
            chain.append((parts, take))
        last = chain[-1][1]

        def own():
            last()
            for i, bit in enumerate(extra):
                first, size = land + i * region[1], region[1]
                number = numbers.setdefault((name, "extra", i), len(numbers))
                one_step(number, packed.at[0, at(region)], landing.at[pl.ds(first, size)], by_grp(bit))
                packed[0, at(region)] = add_low(packed[0, at(region)], landing[first : first + size])
            packed_out[at(region)] = packed[0, at(region)]

        chain[-1] = (chain[-1][0], own)
        for bit, area in reversed(areas):
            chain.append(
                (
                    lambda bit=bit, area=area: [
                        (packed_out.at[at(area)], packed_out.at[at(area)], by_grp(bit))
                    ],
                    nothing,
                )
            )
        chains[name] = chain
        return land + len(extra) * region[1]

    def heads_chain(name, pair, number, lanes, order):
        chain, areas, region = [], [], (0, 256)
        for bit in order:
            size = region[1] // 2
            land = slice(256 - region[1], 256 - size)

            def parts(region=region, bit=bit, land=land):
                return [
                    (
                        dw.at[pair, :, away(region, bit), lanes],
                        summed_q.at[pair, :, pl.ds(land.start, land.stop - land.start), lanes],
                        by_grp(bit),
                    )
                ]

            region = kept(region, bit)

            def take(region=region, land=land):
                mine = at(region)
                dw[pair, :, mine, lanes] = add_low(
                    dw[pair, :, mine, lanes], summed_q[pair, :, land, lanes]
                )

            areas.append((bit, region))
            chain.append((parts, take))
        last, part = chain[-1][1], region

        def own():
            last()
            for i, bit in enumerate(extra):
                slot = 4 * (pair * len(extra) + i)
                count = numbers.setdefault((name, "extra", i), len(numbers))
                one_step(
                    count, dw.at[pair, :, at(part), lanes], q_extra.at[pl.ds(slot, 4), :, lanes],
                    by_grp(bit),
                )
                dw[pair, :, at(part), lanes] = add_low(
                    dw[pair, :, at(part), lanes], q_extra[slot : slot + 4, :, lanes]
                )
            q_out[pair][0, at(part), lanes] = dw[pair, my_row, at(part), lanes]

        chain[-1] = (chain[-1][0], own)
        chain.append(
            (
                lambda: [
                    (
                        dw.at[pair, my_row ^ j, at(part), lanes],
                        q_out[pair].at[j, at(part), lanes],
                        by_row(j),
                    )
                    for j in (1, 2, 3)
                ],
                nothing,
            )
        )
        for bit, area in reversed(areas):
            spot = lambda area=area: q_out[pair].at[:, at(area), lanes]
            chain.append((lambda bit=bit, spot=spot: [(spot(), spot(), by_grp(bit))], nothing))
        chains[name] = chain

    def gather_chain(name, got, out, finish):
        def first():
            out[0] = finish((got[0] + got[1]) + (got[2] + got[3]))

        chain = [(lambda: [(got.at[my_row], got.at[my_row], by_row(j)) for j in (1, 2, 3)], first)]
        for i, bit in enumerate(bits):
            chain.append(
                (
                    lambda i=i, bit=bit: [
                        (out.at[pl.ds(0, 1 << i)], out.at[pl.ds(1 << i, 1 << i)], by_grp(bit))
                    ],
                    nothing,
                )
            )
        chains[name] = chain

    def fold(sums):
        width = sums.shape[1] // 2
        return jnp.concatenate([sums[:, :width], sums[:, width:]], 0).astype(BF)

    loads = [
        pltpu.make_async_copy(src, dst, load_sem.at[i])
        for i, (src, dst) in enumerate(
            (
                (packed_hbm, packed),
                (mixed_hbm, mixed),
                (wq_hbm, mixed.at[pl.ds(0, D)]),
                (wk_hbm, mixed.at[pl.ds(D, D)]),
                (wv_hbm, weights),
                (frames_hbm, frames),
                (middle_hbm, middle),
            )
        )
    ]
    for load in loads[:1] + loads[4:]:
        load.start()

    barrier = pltpu.get_barrier_semaphore()
    for device in [by_row(j) for j in (1, 2, 3)] + [by_grp(bit) for bit in bits]:
        pl.semaphore_signal(barrier, inc=1, device_id=device, device_id_type=MESH)
    pl.semaphore_wait(barrier, 3 + len(bits))

    gather_chain("e", early_got, early_out, fold)
    early_got[my_row] = early_in[...]
    start("e")
    land, first_row = 0, 0
    for number, (count, order) in enumerate(FEED_PIECES):
        land = feed_chain(f"f{number}", (first_row, count), order, land)
        first_row += count
        start(f"f{number}")

    lanes_of = slice(0, 256)
    for j in range(4):
        mixed[pl.ds(pl.multiple_of((my_row ^ j) * block, block), block), lanes_of] = grads_in[j]
    ahead = roll_matrix(offset)

    def turn(i, carry):
        cols = pl.ds(pl.multiple_of(i * TILE, TILE), TILE)
        after = pl.ds(pl.multiple_of((i + 1) % steps * TILE, TILE), TILE)
        part = matdot(ahead[:, :TILE], mixed[cols, lanes_of], 1, 0)
        part = (part + matdot(ahead[:, TILE:], mixed[after, lanes_of], 1, 0)).T
        grad_t[:, cols] = part.astype(BF)
        for head in range(4):
            mine = slice((head % 2) * HEAD_DIM, (head % 2 + 1) * HEAD_DIM)
            crossed = part[head * HEAD_DIM : (head + 1) * HEAD_DIM] * (ot0, ot1)[head // 2][
                mine, cols
            ].astype(F32)
            row_dots[head : head + 1, cols] = jnp.sum(crossed, axis=0, keepdims=True)
        return carry

    lax.fori_loop(0, steps, turn, 0)
    loads[1].start()
    loads[0].wait()

    def run(pair, here, spans, allowed):
        lanes = slice(pair * 128, (pair + 1) * 128)
        lse = (lse0, lse1)[pair]
        for head in range(2):
            mine = slice(head * HEAD_DIM, (head + 1) * HEAD_DIM)
            wide = slice(pair * 128 + head * HEAD_DIM, pair * 128 + (head + 1) * HEAD_DIM)
            dots = slice(2 * pair + head, 2 * pair + head + 1)
            grad_query = None
            for first, count in spans:
                keys = pl.ds(first, count)
                scores = matdot(k[keys, lanes], one_head(qt[lanes, here], head), 1, 0)
                if allowed is not None:
                    scores = jnp.where(allowed, scores, -1e30)
                probs = jnp.exp(scores - lse[head : head + 1, here])
                grad_probs = matdot(v[keys, lanes], one_head(grad_t[lanes, here], head), 1, 0)
                grad_scores = (probs * (grad_probs - row_dots[dots, here])).astype(BF)
                part = matdot(kt[wide, keys], grad_scores, 1, 0)
                grad_query = part if grad_query is None else grad_query + part
                dkt[mine, keys] += matdot(qt[wide, here], grad_scores, 1, 1)
                dvt[mine, keys] += matdot(grad_t[wide, here], probs.astype(BF), 1, 1)
            dqt[mine, here] = grad_query * HEAD_DIM**-0.5

    def finish(pair):
        def part(i, sums):
            cols = pl.ds(pl.multiple_of(i * TILE, TILE), TILE)
            cosine, sine = cos_t[:, cols], sin_t[:, cols]

            def turned(ref):
                parts = []
                for at_row in range(0, 128, HEAD_DIM):
                    first = ref[at_row : at_row + half, cols]
                    second = ref[at_row + half : at_row + HEAD_DIM, cols]
                    parts.append(first * cosine + second * sine)
                    parts.append(second * cosine - first * sine)
                return jnp.concatenate(parts, 0)

            columns = jnp.concatenate([turned(dqt), turned(dkt), dvt[:, cols]], 0)
            nat_ref[:, pl.ds(pl.multiple_of(TILE + i * TILE, TILE), TILE)] = columns.astype(BF)
            low = columns.T.astype(BF)
            rolled[cols, :] = low
            return sums + jnp.sum(low.astype(F32), axis=0, keepdims=True)

        sums = lax.fori_loop(0, steps, part, jnp.zeros((1, 384), F32))
        if pair == 1:
            for copy in copies_of("d0", 0):
                copy.wait_send()
        unroll(
            [got_d.at[my_row, pair]] + [send_d.at[j] for j in range(3)], nat_ref, my_row, offset, block
        )
        chains[f"d{pair}"] = [
            (
                lambda: [(send_d.at[j - 1], got_d.at[my_row, pair], by_row(j)) for j in (1, 2, 3)],
                nothing,
            )
        ]
        start(f"d{pair}")
        run_hook(("fin", pair, 0))
        if pair == 0:
            loads[1].wait()
        for shard in range(4):
            columns = mixed[:, shard * 256 : (shard + 1) * 256]
            dw[pair, shard] = contract_rows(columns, rolled[...]).astype(BF)
        lane = 0
        for number, (count, order) in enumerate(HEAD_PIECES[pair]):
            heads_chain(f"q{pair}{number}", pair, number, pl.ds(lane, count), order)
            start(f"q{pair}{number}")
            lane += count
        return sums

    bias_sums = []
    for pair in range(2):
        dkt[...] = jnp.zeros_like(dkt)
        dvt[...] = jnp.zeros_like(dvt)

        def tile(i, carry):
            run(pair, pl.ds(pl.multiple_of(i * TILE, TILE), TILE), BACK_SPANS, None)
            for when in range(steps - 1):
                if ("tile", pair, when) in HOOKS:
                    pl.when(i == when)(functools.partial(run_hook, ("tile", pair, when)))
            return carry

        lax.fori_loop(0, steps - 1, tile, 0)
        tail = total - LONGEST
        run(pair, pl.ds(LONGEST, tail), [(LONGEST, tail)], tail_allowed(ends, offset, total))
        run_hook(("tile", pair, steps - 1))
        bias_sums.append(finish(pair))
        if pair == 1:
            for load in loads[2:4]:
                load.start()
        run_hook(("fin", pair, 1))

    for pair in range(2):
        advance(f"d{pair}", 0)
    for load in loads[2:]:
        load.wait()
    late = [jnp.zeros((1, 2 * D), F32) for _ in range(4)]
    for part in range(block // TILE):
        rows = slice(part * TILE, (part + 1) * TILE)
        grad = jnp.zeros((TILE, D), F32)
        for kind in range(3):
            pieces = [
                got_d[owner, pair, rows, kind * 128 : (kind + 1) * 128]
                for owner in range(4)
                for pair in range(2)
            ]
            weight = weights[...] if kind == 2 else mixed[kind * D : (kind + 1) * D]
            grad = grad + against(jnp.concatenate(pieces, 1), weight)
        normed, factor = normalize(frames[rows, :].astype(F32))
        spots = my_row * block + part * TILE + lax.broadcasted_iota(jnp.int32, (TILE, 1), 0)
        marks = marks_of(spots, starts, ends)
        scale = jnp.ones((TILE, D), F32)
        for u in range(4):
            scale = scale + marks[u] * scale_rows[u : u + 1, D : 2 * D]
        back = normalize_back(grad * scale, normed, factor)
        frames_grad[rows, :] = (middle[rows, :] + back).astype(BF)
        for u in range(4):
            mark = marks[u]
            late[u] += jnp.concatenate(
                [jnp.sum(t * mark, axis=0, keepdims=True) for t in (grad, grad * normed)], 1
            )
        if part == 0:
            run_hook(("epi", 0, 0))

    widths = [slice(kind * 128, (kind + 1) * 128) for kind in range(3)]
    bias_row = jnp.concatenate(
        [bias_sums[pair][:, w] for w in widths for pair in range(2)]
        + [jnp.zeros((1, 2 * D - 768), F32)],
        1,
    )
    index = lax.broadcasted_iota(jnp.int32, (8, 2 * D), 0)
    gather_chain(
        "l", late_got, late_out, lambda sums: fold(jnp.where(index == 4, bias_row, sums))
    )
    late_got[my_row] = jnp.concatenate(late + [jnp.zeros((4, 2 * D), F32)], 0)
    start("l")

    slots = [mixed.at[pl.ds(0, D)], mixed.at[pl.ds(D, D)], weights]
    blocks = [2, 3, 4, 5, 0, 1]
    fetches = [
        pltpu.make_async_copy(
            mod_hbm.at[:, pl.ds(block * D, D)], slots[i % 3], load_sem.at[len(loads) + i % 3]
        )
        for i, block in enumerate(blocks)
    ]
    for fetch in fetches[:3]:
        fetch.start()
    embed_out[...] = jnp.zeros_like(embed_out)

    def embed_step(i):
        block = blocks[i]
        fetches[i].wait()
        if block < 2:
            rows = late_out[0].astype(F32)[8 * block : 8 * block + 8]
        else:
            part, lane = divmod(block - 2, 2)
            rows = early_out[0, :, lane * D : (lane + 1) * D].astype(F32)[8 * part : 8 * part + 8]
        embed_out[...] += against(rows.astype(BF), slots[i % 3][...])
        if i + 3 < len(blocks):
            fetches[i + 3].start()

    done, late_ready = 0, False
    for number, (name, step) in enumerate(HOOKS[("epi", 1, 0)]):
        advance(name, step)
        late_ready = late_ready or (name, step) == ("l", 0)
        if number % 3 == 2 and done < (6 if late_ready else 4):
            embed_step(done)
            done += 1
    for i in range(done, 6):
        embed_step(i)
    for number in range(3, len(bits)):
        advance("e", number + 1)
        advance("l", number + 1)
    for name, step in started:
        if name != "d0":
            for copy in copies_of(name, step):
                copy.wait_send()


def attend_back(
    n_grp, lengths, qt, k, kt, v, heads_t, lse, cos_t, sin_t, early, scale_rows, grads, mixed, packed, weights, frames, middle, mod_weight,
):
    total = k.shape[0]
    block = total // 4
    rows = packed.shape[1]
    extra = max(0, len(bits_of(n_grp)) - 3)
    inputs = [
        qt, k, kt, v, *heads_t, *lse, cos_t, sin_t, early, scale_rows, grads,
    ]
    far = [mixed, packed, *weights, frames, middle, mod_weight]
    copies = 160
    return pl.pallas_call(
        functools.partial(back_kernel, n_grp),
        out_shape=[
            jax.ShapeDtypeStruct((block, D), BF),
            jax.ShapeDtypeStruct((rows, D), BF),
            jax.ShapeDtypeStruct((4, 256, 384), BF),
            jax.ShapeDtypeStruct((4, 256, 384), BF),
            jax.ShapeDtypeStruct((n_grp, 16, 2 * D), BF),
            jax.ShapeDtypeStruct((n_grp, 16, D), BF),
            jax.ShapeDtypeStruct((8, D), F32),
        ],
        in_specs=[pl.BlockSpec(memory_space=SMEM)]
        + [pl.BlockSpec(memory_space=VMEM)] * len(inputs)
        + [pl.BlockSpec(memory_space=pl.ANY)] * len(far),
        out_specs=[pl.BlockSpec(memory_space=VMEM)] * 7,
        scratch_shapes=[
            VMEM((256, total), BF),
            VMEM((8, total), F32),
            VMEM((128, total), F32),
            VMEM((128, total), F32),
            VMEM((128, total), F32),
            VMEM((384, total + TILE), BF),
            VMEM((total, 384), BF),
            VMEM((total, D), BF),
            VMEM((2, rows, D), BF),
            VMEM((D, D), BF),
            VMEM((block, D), BF),
            VMEM((block, D), F32),
            VMEM((rows * (15 + extra) // 8, D), BF),
            VMEM((2, 4, 256, 384), BF),
            VMEM((3, block, 384), BF),
            VMEM((4, 2, block, 384), BF),
            VMEM((4, 8, 4 * D), F32),
            VMEM((4, 8, 2 * D), F32),
            VMEM((2, 4, 256, 384), BF),
            VMEM((max(1, 8 * extra), 32, 384), BF),
            pltpu.SemaphoreType.DMA((copies,)),
            pltpu.SemaphoreType.DMA((copies,)),
            pltpu.SemaphoreType.DMA((len(far) + 3,)),
        ],
        compiler_params=pltpu.CompilerParams(
            vmem_limit_bytes=62 << 20, collective_id=1, has_side_effects=True
        ),
        cost_estimate=pl.CostEstimate(
            flops=4 * 2 * 5 * total * LONGEST * 256,
            bytes_accessed=40 << 20,
            transcendentals=4 * total * LONGEST,
        ),
        name="attend_back",
    )(lengths, *inputs, *far)


def feed_kernel(
    lengths, o, frames, cot, mod, act, out_bias, up_bias, down_bias, out_hbm, up_hbm, down_hbm,
    output, middle_out, grads_out, packed, early_out,
    w_out, w_up, w_down, h_s, a_s, ez_s, eb_s, ea_s, send_o, send_w, got_w, load_sem, send_sem, recv_sem,
):
    my_row = lax.axis_index("row")
    by_row = lambda j: {"row": my_row ^ j}
    rows_all = frames.shape[0]
    _, starts, ends, _ = layout_of(lengths)
    width = D // 4
    loads = [
        pltpu.make_async_copy(
            out_hbm.at[pl.ds(pl.multiple_of((my_row ^ j) * width, width), width)],
            w_out.at[pl.ds(j * width, width)],
            load_sem.at[j],
        )
        for j in range(4)
    ] + [
        pltpu.make_async_copy(up_hbm, w_up, load_sem.at[4]),
        pltpu.make_async_copy(down_hbm, w_down, load_sem.at[5]),
    ]
    for load in loads:
        load.start()
    barrier = pltpu.get_barrier_semaphore()
    for j in (1, 2, 3):
        pl.semaphore_signal(barrier, inc=1, device_id=by_row(j), device_id_type=MESH)
    pl.semaphore_wait(barrier, 3)

    def remote(number, src, dst, j):
        return pltpu.make_async_remote_copy(
            src, dst, send_sem.at[number], recv_sem.at[number], device_id=by_row(j), device_id_type=MESH
        )

    copies = []
    coef = math.sqrt(2.0 / math.pi)
    sums = [[jnp.zeros((1, D), F32) for _ in range(4)] for _ in range(4)]
    bias_sums = [jnp.zeros((1, n), F32) for n in (D, 2 * D, D)]
    for tile in range(rows_all // TILE):
        rows = slice(tile * TILE, (tile + 1) * TILE)
        spots = my_row * rows_all + tile * TILE + lax.broadcasted_iota(jnp.int32, (TILE, 1), 0)
        marks = marks_of(spots, starts, ends)

        def per_row(block):
            total = marks[0] * mod[0:1, block * D : (block + 1) * D]
            for u in range(1, 4):
                total = total + marks[u] * mod[u : u + 1, block * D : (block + 1) * D]
            return total

        gate_a, shift_f, scale_f, gate_f = per_row(2), per_row(3), 1.0 + per_row(4), per_row(5)
        if tile == 0:
            for load in loads[:4]:
                load.wait()
        heads = jnp.concatenate([o[j, rows, :] for j in range(4)], 1)
        attended = matdot(heads, w_out[...], 1, 0) + out_bias[...]
        middle = frames[rows, :].astype(F32) + gate_a * attended
        normed, factor = normalize(middle)
        h = (normed * scale_f + shift_f).astype(BF)
        h_s[rows, :] = h
        if tile == 0:
            loads[4].wait()
        z = matdot(h, w_up[...], 1, 0) + up_bias[...]
        square = z * z
        curve = jnp.tanh(coef * (z * (1.0 + 0.044715 * square)))
        share = 0.5 * (1.0 + curve)
        a = (z * share).astype(BF)
        a_s[rows, :] = a
        slope = share + (0.5 * coef) * z * (1.0 - curve * curve) * (1.0 + (3 * 0.044715) * square)
        if tile == 0:
            loads[5].wait()
        branch = matdot(a, w_down[...], 1, 0) + down_bias[...]
        output[rows, :] = (middle + gate_f * branch).astype(BF)
        upstream = cot[rows, :].astype(F32)
        e_b = (upstream * gate_f).astype(BF)
        eb_s[rows, :] = e_b
        e_z = (against(e_b, w_down[...]) * slope).astype(BF)
        ez_s[rows, :] = e_z
        e_h = against(e_z, w_up[...])
        e_mid = upstream + normalize_back(e_h * scale_f, normed, factor)
        middle_out[rows, :] = e_mid
        e_att = (e_mid * gate_a).astype(BF)
        ea_s[rows, :] = e_att
        e_o = against(e_att, w_out[...]).astype(BF)
        grads_out[0, rows, :] = e_o[:, :width]
        for j in (1, 2, 3):
            send_o[j - 1, rows, :] = e_o[:, j * width : (j + 1) * width]
            copies.append(
                remote(
                    len(copies), send_o.at[j - 1, pl.ds(tile * TILE, TILE)],
                    grads_out.at[j, pl.ds(tile * TILE, TILE)], j,
                )
            )
            copies[-1].start()
        for block, part in enumerate((e_mid * attended, e_h, e_h * normed, upstream * branch)):
            for u in range(4):
                sums[u][block] += jnp.sum(part * marks[u], axis=0, keepdims=True)
        for number, part in enumerate((e_att, e_z, e_b)):
            bias_sums[number] += jnp.sum(part.astype(F32), axis=0, keepdims=True)

    early_out[...] = jnp.concatenate(
        [jnp.concatenate(row, 1) for row in sums + [bias_sums]]
        + [act[...] * 0.25, jnp.zeros((2, 4 * D), F32)],
        0,
    )

    def shard(j, store):
        owner = my_row ^ j
        columns = pl.ds(pl.multiple_of(owner * 2 * width, 2 * width), 2 * width)
        store(768, contract_rows(a_s[:, columns], eb_s[...]))
        columns = pl.ds(pl.multiple_of(owner * width, width), width)
        store(256, contract_rows(h_s[:, columns], ez_s[:, :D]))
        store(512, contract_rows(h_s[:, columns], ez_s[:, D:]))
        store(0, contract_rows(o[j], ea_s[...]))

    for slot, j in enumerate((1, 3)):

        def store(first, value):
            send_w[slot, first : first + value.shape[0], :] = value.astype(BF)

        shard(j, store)
        copies.append(remote(len(copies), send_w.at[slot], got_w.at[slot], 1))
        copies[-1].start()
    for slot, j in enumerate((0, 2)):

        def store(first, value):
            packed[slot, first : first + value.shape[0], :] = value.astype(BF)

        shard(j, store)
    for slot in range(2):
        copies[-2 + slot].wait_recv()
        packed[slot] = add_low(packed[slot], got_w[slot])
    for copy in copies[:-2]:
        copy.wait_recv()
    for copy in copies:
        copy.wait_send()


def feed(lengths, o, frames, cot, mod, act, biases, weights):
    rows = frames.shape[0]
    inputs = [o, frames, cot, mod, act, *[b[None] for b in biases]]
    return pl.pallas_call(
        feed_kernel,
        out_shape=[
            jax.ShapeDtypeStruct((rows, D), BF),
            jax.ShapeDtypeStruct((rows, D), F32),
            jax.ShapeDtypeStruct((4, rows, D // 4), BF),
            jax.ShapeDtypeStruct((2, 1280, D), BF),
            jax.ShapeDtypeStruct((8, 4 * D), F32),
        ],
        in_specs=[pl.BlockSpec(memory_space=SMEM)]
        + [pl.BlockSpec(memory_space=VMEM)] * len(inputs)
        + [pl.BlockSpec(memory_space=pl.ANY)] * 3,
        out_specs=[pl.BlockSpec(memory_space=VMEM)] * 5,
        scratch_shapes=[
            VMEM((D, D), BF),
            VMEM((D, 2 * D), BF),
            VMEM((2 * D, D), BF),
            VMEM((rows, D), BF),
            VMEM((rows, 2 * D), BF),
            VMEM((rows, 2 * D), BF),
            VMEM((rows, D), BF),
            VMEM((rows, D), BF),
            VMEM((3, rows, D // 4), BF),
            VMEM((2, 1280, D), BF),
            VMEM((2, 1280, D), BF),
            pltpu.SemaphoreType.DMA((6,)),
            pltpu.SemaphoreType.DMA((3 * rows // TILE + 2,)),
            pltpu.SemaphoreType.DMA((3 * rows // TILE + 2,)),
        ],
        compiler_params=pltpu.CompilerParams(
            vmem_limit_bytes=LIMIT, collective_id=2, has_side_effects=True
        ),
        cost_estimate=pl.CostEstimate(
            flops=2 * rows * D * 15 * D, bytes_accessed=30 << 20, transcendentals=rows * 2 * D
        ),
        name="feed",
    )(lengths, *inputs, *weights)


def outputs_kernel(
    packed, heads_0, heads_1, early, late, embedding, embed_in,
    out_far, up_far, down_far, query_far, key_far, value_far, mod_far,
    mod_b, embed, out_b, up_b, down_b, query_b, key_b, value_b,
    out_w, up_w, down_w, query_w, key_w, value_w, mod_w, rows_ref, mod_ref, store_sem,
):
    my_row = lax.axis_index("row")
    width = D // 4
    stores = []

    def store(src, dst):
        stores.append(pltpu.make_async_copy(src, dst, store_sem.at[len(stores)]))
        stores[-1].start()

    n_grp = early.shape[0]
    out_w[...] = packed[:width].astype(F32)
    up_w[:, :D] = packed[width : 2 * width].astype(F32)
    up_w[:, D:] = packed[2 * width : 3 * width].astype(F32)
    store(out_w, out_far)
    store(up_w, up_far)
    down_w[...] = packed[3 * width :].astype(F32)
    store(down_w, down_far)
    for pair, heads in enumerate((heads_0, heads_1)):
        for j in range(4):
            lanes = pl.ds(pl.multiple_of((my_row ^ j) * width + pair * 128, 128), 128)
            for kind, out in enumerate((query_w, key_w, value_w)):
                out[:, lanes] = heads[j, :, kind * 128 : (kind + 1) * 128].astype(F32)
    store(query_w, query_far)
    store(key_w, key_far)
    store(value_w, value_far)
    for first, source, count in ((0, late, D), (2 * D, early, 2 * D)):
        for part in range(2):
            rows = source[:, 8 * part : 8 * part + 8].astype(F32).reshape(n_grp * 8, count)
            mod_ref[:, first + part * count : first + (part + 1) * count] = rows
    number = lax.broadcasted_iota(jnp.int32, (n_grp * 8, 1), 0) % 8
    utterance, bias = (number < 4).astype(F32), (number == 4).astype(F32)
    act = jnp.zeros((n_grp * 8, width), F32)
    for u in range(4):
        lanes = pl.ds(pl.multiple_of((2 + u) * D + my_row * width, width), width)
        moved = pltpu.roll(mod_ref[:, lanes], (u - 5) % (n_grp * 8), 0)
        act = jnp.where(number == u, moved, act)
    act = act.astype(BF)
    for block in range(6):
        lanes = slice(block * D, (block + 1) * D)
        rows = mod_ref[:, lanes]
        mod_w[:, lanes] = contract_rows(act, rows.astype(BF))
        store(mod_w.at[:, pl.ds(block * D, D)], mod_far.at[:, pl.ds(block * D, D)])
        sums = [jnp.sum(rows * mark, axis=0, keepdims=True) for mark in (utterance, bias)]
        rows_ref[:, lanes] = jnp.concatenate(sums + [jnp.zeros((6, D), F32)], 0)

    def own(row, first, size):
        lanes = pl.ds(pl.multiple_of(first + my_row * size, 128), size)
        return rows_ref[row : row + 1, lanes]

    mod_b[...] = own(0, 0, 6 * width)
    for i, out in enumerate((query_b, key_b, value_b)):
        out[...] = rows_ref[1:2, i * width : (i + 1) * width]
    out_b[...] = own(1, 2 * D, width)
    up_b[...] = own(1, 3 * D, 2 * width)
    down_b[...] = own(1, 5 * D, width)
    gate = 1.0 / (1.0 + jnp.exp(-embedding[...]))
    embed[...] = embed_in[:4] * (gate * (1.0 + embedding[...] * (1.0 - gate)))
    for copy in stores:
        copy.wait()


def outputs(packed, heads_0, heads_1, early, late, embedding, embed_in):
    width = D // 4
    n_grp = early.shape[0]
    shapes = [(width, D), (width, 2 * D), (2 * width, D)] + [(width, D)] * 3 + [(width, 6 * D)]
    shapes += [(1, 6 * width), (4, D)] + [(1, n) for n in (width, 2 * width, width, width, width, width)]
    return pl.pallas_call(
        outputs_kernel,
        out_shape=[jax.ShapeDtypeStruct(shape, F32) for shape in shapes],
        in_specs=[pl.BlockSpec(memory_space=VMEM)] * 7,
        out_specs=[pl.BlockSpec(memory_space=pl.ANY)] * 7
        + [pl.BlockSpec(memory_space=VMEM)] * (len(shapes) - 7),
        scratch_shapes=[VMEM(shape, F32) for shape in shapes[:7]]
        + [
            VMEM((8, 6 * D), F32),
            VMEM((n_grp * 8, 6 * D), F32),
            pltpu.SemaphoreType.DMA((12,)),
        ],
        compiler_params=pltpu.CompilerParams(vmem_limit_bytes=LIMIT),
        name="outputs",
    )(packed, heads_0, heads_1, early, late, embedding, embed_in)


def local(
    frames, time_embed, lengths, mod_weight, mod_bias, query_weight, query_bias, key_weight, key_bias,
    value_weight, value_bias, out_weight, out_bias, up_weight, up_bias, down_weight, down_bias, cotangent,
):
    n_grp = lax.axis_size("grp")
    lengths, embedding = lengths[0], time_embed[0]
    weights = (query_weight, key_weight, value_weight)
    mixed, qt, kt, vt, k_rows, v_rows, cos_t, sin_t, modulation, act = project(
        lengths, frames, embedding, mod_weight, mod_bias, weights, (query_bias, key_bias, value_bias)
    )
    *heads_t, lse_0, lse_1, o_all = attend(lengths, qt, k_rows, vt)
    output, grad_middle, grad_pieces, packed, early = feed(
        lengths, o_all, frames, cotangent, modulation, act, (out_bias, up_bias, down_bias),
        (out_weight, up_weight, down_weight),
    )
    grad_frames, packed_total, heads_0, heads_1, early_all, late_all, embed_part = attend_back(
        n_grp, lengths, qt, k_rows, kt, v_rows, heads_t, (lse_0, lse_1), cos_t, sin_t, early,
        modulation, grad_pieces, mixed, packed, weights, frames, grad_middle, mod_weight,
    )
    grads = outputs(packed_total, heads_0, heads_1, early_all, late_all, embedding, embed_part)
    out_grad, up_grad, down_grad, query_grad, key_grad, value_grad, mod_weight_grad = grads[:7]
    mod_bias_grad, grad_embedding = grads[7][0], grads[8]
    out_b, up_b, down_b, query_b, key_b, value_b = (b[0] for b in grads[9:])
    return (
        output,
        grad_frames,
        grad_embedding[None],
        mod_weight_grad,
        mod_bias_grad,
        query_grad,
        query_b,
        key_grad,
        key_b,
        value_grad,
        value_b,
        out_grad,
        out_b,
        up_grad,
        up_b,
        down_grad,
        down_b,
    )


def solution(mesh):
    placed = (
        (P(("grp", "row"), None), P("grp", None, None), P("grp", None))
        + (P(),) * 14
        + (P(("grp", "row"), None),)
    )
    return jax.shard_map(
        local,
        mesh=mesh,
        in_specs=placed,
        out_specs=(
            P(("grp", "row"), None),
            P(("grp", "row"), None),
            P("grp", None, None),
        )
        + (P("row", None), P("row")) * 7,
        check_vma=False,
    )
```

```python
import functools
import math

import jax
import jax.numpy as jnp
import numpy as np
from jax import lax
from jax.experimental import pallas as pl
from jax.experimental.pallas import tpu as pltpu
from jax.sharding import PartitionSpec as P

D = 1024
HEADS = 16
HEAD_DIM = 64
LONGEST = 1792
TILE = 256
BF = jnp.bfloat16
F32 = jnp.float32

highest = lax.Precision.HIGHEST
VMEM = pltpu.VMEM
SMEM = pltpu.SMEM
LIMIT = 60 << 20
MESH = pl.DeviceIdType.MESH
BACK_SPANS = [(0, 896), (896, 896)]


def matdot(left, right, left_dim, right_dim):
    return lax.dot_general(
        left, right, (((left_dim,), (right_dim,)), ((), ())), preferred_element_type=F32
    )


def contract_rows(left, right):
    return matdot(left, right, 0, 0)


def against(left, weight):
    return matdot(left, weight, 1, 1)


def column_sum(tensor):
    return jnp.sum(tensor.astype(F32), axis=0)


def normalize(tensor):
    centred = tensor - jnp.mean(tensor, axis=-1, keepdims=True)
    factor = lax.rsqrt(jnp.mean(centred * centred, axis=-1, keepdims=True) + 1e-06)
    return (centred * factor, factor)


def normalize_back(grad_normed, normed, factor):
    mean_grad = jnp.mean(grad_normed, axis=-1, keepdims=True)
    mean_cross = jnp.mean(grad_normed * normed, axis=-1, keepdims=True)
    return (grad_normed - mean_grad - normed * mean_cross) * factor


def exchange(tensor, axis, bit):
    size = lax.axis_size(axis)
    return lax.ppermute(tensor, axis, [(i, i ^ bit) for i in range(size)])


def add_low(left, right):
    return (left.astype(F32) + right.astype(F32)).astype(BF)


def bits_of(count):
    return [1 << i for i in range(count.bit_length() - 1)]


def roll_matrix(offset):
    row = lax.broadcasted_iota(jnp.int32, (TILE, 2 * TILE), 0)
    col = lax.broadcasted_iota(jnp.int32, (TILE, 2 * TILE), 1)
    return (col == row + offset).astype(F32).astype(BF)


def layout_of(lengths):
    sizes = [lengths[u] for u in range(4)]
    starts, finish, at = [], [], 0
    for size in sizes:
        starts.append(at)
        at = at + size
        finish.append(at)
    offset = 0
    for size, first in zip(sizes, starts):
        offset = offset + jnp.where(size == LONGEST, first, 0)
    return sizes, starts, finish, offset


def marks_of(rows, starts, finish):
    return [
        jnp.logical_and(rows >= first, rows < end).astype(F32) for first, end in zip(starts, finish)
    ]


def tail_allowed(finish, offset, total):
    count = total - LONGEST

    def segment(shape, dim):
        rows = LONGEST + offset + lax.broadcasted_iota(jnp.int32, shape, dim)
        rows = jnp.where(rows >= total, rows - total, rows)
        return sum((rows >= end).astype(jnp.int32) for end in finish)

    return segment((count, 1), 0) == segment((1, count), 1)


def front_kernel(
    lengths, embedding, mod_bias, q_bias, k_bias, v_bias, frequency,
    frames_hbm, mod_weight_hbm, wq_hbm, wk_hbm, wv_hbm,
    mixed_far, qt_far, kt_far, k_far, v_far, cos_out, sin_out, mod_out, act_out, ot0, ot1, lse0, lse1, o_all,
    mixed_out, qt_out, kt_out, vt_out, k_out, v_out,
    rows_ref, roll_ref, mod_weight, weight, weight_t, bias_t, rolled_ref, send_o,
    send_sem, recv_sem, load_sem, store_sem, send_o_sem, recv_o_sem,
):
    my_row = lax.axis_index("row")
    block = frames_hbm.shape[0]
    total = 4 * block
    steps = total // TILE
    width = qt_out.shape[0]
    by_row = lambda j: {"row": my_row ^ j}
    sizes, starts, finish, offset = layout_of(lengths)

    piece = TILE // 2

    def place(j, part=0, count=piece):
        first = pl.multiple_of((my_row ^ j) * block + part * piece, piece)
        return pl.ds(first, count)

    def remote(number, src, dst, j):
        return pltpu.make_async_remote_copy(
            src, dst, send_sem.at[number], recv_sem.at[number], device_id=by_row(j), device_id_type=MESH
        )

    parts = block // piece
    barrier = pltpu.get_barrier_semaphore()
    for j in (1, 2, 3):
        pl.semaphore_signal(barrier, inc=1, device_id=by_row(j), device_id_type=MESH)
    pl.semaphore_wait(barrier, 3)
    to_x = [
        remote(i, frames_hbm.at[pl.ds(i * piece, piece)], rows_ref.at[place(0, i)], 2)
        for i in range(parts)
    ]
    to_core = remote(parts, frames_hbm, rows_ref.at[place(0, 0, block)], 1)
    onward = [
        remote(parts + 1 + i, rows_ref.at[place(2, i)], rows_ref.at[place(2, i)], 1) for i in range(parts)
    ]
    for copy in to_x + [to_core]:
        copy.start()
    columns = pl.ds(pl.multiple_of(my_row * width, width), width)
    loads = [
        pltpu.make_async_copy(src, dst, load_sem.at[i])
        for i, (src, dst) in enumerate(
            [(frames_hbm, rows_ref.at[place(0, 0, block)])]
            + [
                (w.at[:, columns], weight.at[:, pl.ds(i * width, width)])
                for i, w in enumerate((wq_hbm, wk_hbm, wv_hbm))
            ]
            + [
                (mod_weight_hbm.at[:, pl.ds(i * 2 * D, 2 * D)], mod_weight.at[i]) for i in range(3)
            ]
        )
    ]
    for load in loads:
        load.start()

    rows = lax.broadcasted_iota(jnp.int32, (1, total), 1) + offset
    rows = jnp.where(rows >= total, rows - total, rows)
    position = rows
    for first, end in zip(starts, finish):
        inside = jnp.logical_and(rows >= first, rows < end)
        position = jnp.where(inside, rows - first, position)
    angles = frequency[...] * position.astype(F32)
    cos_out[...] = jnp.cos(angles)
    sin_out[...] = jnp.sin(angles)
    roll_ref[...] = roll_matrix(offset)
    for i, bias in enumerate((q_bias, k_bias, v_bias)):
        bias_t[i : i + 1, :] = bias[0:1, columns]

    act = (embedding[...] / (1.0 + jnp.exp(-embedding[...]))).astype(BF).astype(F32)
    act_out[...] = jnp.concatenate([act[u : u + 1] for u in range(4)], 1)
    act_low = jnp.concatenate([act, jnp.zeros_like(act)], 0).astype(BF)
    for i in range(3):
        lanes = slice(i * 2 * D, (i + 1) * 2 * D)
        loads[4 + i].wait()
        mod_out[:, lanes] = matdot(act_low, mod_weight[i], 1, 0) + mod_bias[:, lanes]
    for load in loads[:4]:
        load.wait()
    for i in range(3):
        lanes = slice(i * width, (i + 1) * width)
        weight_t[lanes, :] = weight[:, lanes].T
    biases = jnp.concatenate([bias_t[i : i + 1, :] for i in range(3)], 1)
    biases = jnp.broadcast_to(biases, (8, 3 * width)).T[:, 0:1]

    mod_long = jnp.zeros((1, 2 * D), F32)
    for u in range(4):
        mod_long = mod_long + jnp.where(sizes[u] == LONGEST, 1.0, 0.0) * mod_out[u : u + 1, : 2 * D]
    half = HEAD_DIM // 2

    def tile(step, tail=False):
        here = pl.ds(pl.multiple_of(step * TILE, TILE), TILE)
        if tail:
            moved = matdot(roll_ref[:, :TILE], rows_ref[here, :], 1, 0)
            normed, _ = normalize(moved + matdot(roll_ref[:, TILE:], rows_ref[:TILE, :], 1, 0))
            spots = LONGEST + offset + lax.broadcasted_iota(jnp.int32, (TILE, 1), 0)
            spots = jnp.where(spots >= total, spots - total, spots)
            per_row = jnp.zeros((TILE, 2 * D), F32)
            for u, mark in enumerate(marks_of(spots, starts, finish)):
                per_row = per_row + mark * mod_out[u : u + 1, : 2 * D]
        else:
            both = pl.ds(pl.multiple_of(step * TILE, TILE), 2 * TILE)
            normed, _ = normalize(matdot(roll_ref[...], rows_ref[both, :], 1, 0))
            per_row = mod_long
        mixed_out[here, :] = (normed * (1.0 + per_row[:, D:]) + per_row[:, :D]).astype(BF)
        wide = matdot(weight_t[...], mixed_out[here, :], 1, 1) + biases
        cosine, sine = cos_out[:, here], sin_out[:, here]

        def turned(base):
            out = []
            for at in range(base, base + width, HEAD_DIM):
                first, second = wide[at : at + half], wide[at + half : at + HEAD_DIM]
                out.append(first * cosine - second * sine)
                out.append(second * cosine + first * sine)
            return jnp.concatenate(out, 0)

        keys = turned(width)
        values = wide[2 * width :]
        qt_out[:, here] = turned(0).astype(BF) * jnp.asarray(HEAD_DIM**-0.5, BF)
        kt_out[:, here] = keys.astype(BF)
        vt_out[:, here] = values.astype(BF)
        k_out[here, :] = keys.T.astype(BF)
        v_out[here, :] = values.T.astype(BF)

    to_core.wait_recv()
    chip = my_row // 2
    for i in range(steps // 2 - 1):
        tile(chip * (steps // 2) + i)
    for arrived, copy in zip(to_x, onward):
        arrived.wait_recv()
        copy.start()
    for copy in onward:
        copy.wait_recv()
    for i in range(steps // 2):
        tile((1 - chip) * (steps // 2 - 1) + i)
    tile(steps - 1, True)
    stores = [
        pltpu.make_async_copy(src, dst, store_sem.at[i])
        for i, (src, dst) in enumerate(
            (
                (mixed_out, mixed_far),
                (qt_out, qt_far),
                (kt_out, kt_far),
                (k_out, k_far),
                (v_out, v_far),
            )
        )
    ]
    for copy in stores:
        copy.start()
    attend_part(
        finish, offset, qt_out, k_out, vt_out, ot0, ot1, lse0, lse1, o_all, rolled_ref, send_o,
        send_o_sem, recv_o_sem,
    )
    for copy in to_x + [to_core] + onward:
        copy.wait_send()
    for copy in stores:
        copy.wait()


def front(lengths, frames, embedding, mod_weight, mod_bias, weights, biases):
    block = frames.shape[0]
    total = 4 * block
    width = D // 4
    half = HEAD_DIM // 2
    frequency = np.exp(np.arange(half) * (-2.0 * math.log(10000.0) / HEAD_DIM)).astype(np.float32)
    inputs = [embedding, mod_bias[None], *[b[None] for b in biases], jnp.asarray(frequency)[:, None]]
    far = [frames, mod_weight, *weights]
    copies = 1 + 2 * (2 * block // TILE)
    wide, tall = (width, total), (total, width)
    stored = [(total, D), wide, wide, tall, tall]
    return pl.pallas_call(
        front_kernel,
        out_shape=[jax.ShapeDtypeStruct(shape, BF) for shape in stored]
        + [
            jax.ShapeDtypeStruct((half, total), F32),
            jax.ShapeDtypeStruct((half, total), F32),
            jax.ShapeDtypeStruct((8, 6 * D), F32),
            jax.ShapeDtypeStruct((1, 4 * D), F32),
        ]
        + [jax.ShapeDtypeStruct((128, total), BF)] * 2
        + [jax.ShapeDtypeStruct((8, total), F32)] * 2
        + [jax.ShapeDtypeStruct((4, block, 256), BF)],
        in_specs=[pl.BlockSpec(memory_space=SMEM)]
        + [pl.BlockSpec(memory_space=VMEM)] * len(inputs)
        + [pl.BlockSpec(memory_space=pl.ANY)] * len(far),
        out_specs=[pl.BlockSpec(memory_space=pl.ANY)] * 5 + [pl.BlockSpec(memory_space=VMEM)] * 9,
        scratch_shapes=[VMEM(shape, BF) for shape in [(total, D), wide, wide, wide, tall, tall]]
        + [
            VMEM((total, D), BF),
            VMEM((TILE, 2 * TILE), BF),
            VMEM((3, D, 2 * D), BF),
            VMEM((D, 3 * width), BF),
            VMEM((3 * width, D), BF),
            VMEM((8, width), F32),
            VMEM((128, total + TILE), BF),
            VMEM((6, block, 128), BF),
            pltpu.SemaphoreType.DMA((copies,)),
            pltpu.SemaphoreType.DMA((copies,)),
            pltpu.SemaphoreType.DMA((7,)),
            pltpu.SemaphoreType.DMA((5,)),
            pltpu.SemaphoreType.DMA((6,)),
            pltpu.SemaphoreType.DMA((6,)),
        ],
        compiler_params=pltpu.CompilerParams(
            vmem_limit_bytes=LIMIT, collective_id=4, has_side_effects=True
        ),
        cost_estimate=pl.CostEstimate(
            flops=2 * total * D * 3 * width + 2 * 2 * 6 * total * LONGEST * 256,
            bytes_accessed=40 << 20,
            transcendentals=4 * total * LONGEST,
        ),
        name="front",
    )(lengths, *inputs, *far)


def one_head(pair, head):
    part = pair[head * HEAD_DIM : (head + 1) * HEAD_DIM]
    empty = jnp.zeros_like(part)
    return jnp.concatenate([part, empty] if head == 0 else [empty, part], 0)


def unroll(outs, rolled_ref, my_row, offset, block):
    total = 4 * block
    rolled_ref[:, pl.ds(0, TILE)] = rolled_ref[:, pl.ds(total, TILE)]
    back = roll_matrix(TILE - offset)
    for j, out in enumerate(outs):
        for part in range(block // TILE):
            at = pl.multiple_of((my_row ^ j) * block + part * TILE, TILE)
            rows = matdot(back, rolled_ref[:, pl.ds(at, 2 * TILE)], 1, 1)
            out[part * TILE : (part + 1) * TILE, :] = rows.astype(BF)


def attend_part(
    finish, offset, qt, k, vt, ot0, ot1, lse0, lse1, o_all, rolled_ref, send_o, send_sem, recv_sem
):
    my_row = lax.axis_index("row")
    total = k.shape[0]
    block = total // 4
    tail = total - LONGEST

    def run(pair, here, first, count, allowed):
        outs, tops = [], []
        lanes = slice(pair * 128, (pair + 1) * 128)

        def scores_of(head):
            scores = matdot(k[first : first + count, lanes], one_head(qt[lanes, here], head), 1, 0)
            return scores if allowed is None else jnp.where(allowed, scores, -1e30)

        for head in range(2):
            tops.append(jnp.max(scores_of(head), axis=0, keepdims=True))
        for head in range(2):
            wide = slice(pair * 128 + head * HEAD_DIM, pair * 128 + (head + 1) * HEAD_DIM)
            weights = jnp.exp(scores_of(head) - tops[head]).astype(BF)
            values = jnp.concatenate([vt[wide, first : first + count], jnp.ones((16, count), BF)], 0)
            mixed = matdot(values, weights, 1, 0)
            exp_sum = mixed[HEAD_DIM : HEAD_DIM + 1]
            outs.append(mixed[:HEAD_DIM] / exp_sum)
            tops[head] = tops[head] + jnp.log(exp_sum)
        low = jnp.concatenate(outs, 0).astype(BF)
        (ot0, ot1)[pair][:, here] = low
        (lse0, lse1)[pair][:, here] = jnp.concatenate(tops * 4, 0)
        return low

    copies = []
    for pair in range(2):

        def tile(i, carry):
            low = run(pair, pl.ds(pl.multiple_of(i * TILE, TILE), TILE), 0, LONGEST, None)
            rolled_ref[:, pl.ds(pl.multiple_of(TILE + i * TILE, TILE), TILE)] = low
            return carry

        lax.fori_loop(0, LONGEST // TILE, tile, 0)
        low = run(pair, pl.ds(LONGEST, tail), LONGEST, tail, tail_allowed(finish, offset, total))
        rolled_ref[:, pl.ds(total, TILE)] = low
        lanes = pl.ds(pair * 128, 128)
        outs = [o_all.at[0, :, lanes]] + [send_o.at[3 * pair + j] for j in range(3)]
        unroll(outs, rolled_ref, my_row, offset, block)
        for j in (1, 2, 3):
            number = 3 * pair + j - 1
            copies.append(
                pltpu.make_async_remote_copy(
                    send_o.at[number], o_all.at[j, :, lanes], send_sem.at[number], recv_sem.at[number],
                    device_id={"row": my_row ^ j}, device_id_type=MESH,
                )
            )
            copies[-1].start()
    for copy in copies:
        copy.wait()


FEED_PIECES = ((384, ("x", 1, 2, 4)), (384, (2, 1, "x", 4)), (256, (1, 2, 4, "x")), (256, ("x", 1, 2, 4)),)
HEAD_PIECES = (
    ((384, (1, 2, 4)),),
    ((128, (1, 2, 4)), (128, (1, 2, 4)), (128, (1, 2, 4)),),
)
HOOKS = {
    ("tile", 0, 1): [("e", 0)],
    ("tile", 0, 2): [("f2", 0)],
    ("tile", 0, 3): [("e", 1)],
    ("tile", 0, 4): [("f1", 0)],
    ("tile", 0, 5): [("f0", 0), ("f2", 1)],
    ("tile", 0, 6): [("e", 2)],
    ("tile", 0, 7): [("f1", 1)],
    ("fin", 0, 0): [("f2", 2), ("f3", 0)],
    ("fin", 0, 1): [("f1", 2)],
    ("tile", 1, 0): [("f0", 1)],
    ("tile", 1, 1): [("e", 3), ("f3", 1)],
    ("tile", 1, 2): [("f1", 3)],
    ("tile", 1, 3): [("f0", 2), ("q00", 0)],
    ("tile", 1, 4): [("f2", 3), ("f3", 2)],
    ("tile", 1, 5): [("f1", 4)],
    ("tile", 1, 6): [("f0", 3)],
    ("tile", 1, 7): [("f1", 5), ("q00", 1)],
    ("fin", 1, 0): [("f2", 4), ("f3", 3)],
    ("fin", 1, 1): [("f0", 4), ("q10", 0), ("q11", 0), ("f1", 6), ("q12", 0), ("q00", 2)],
    ("epi", 0, 0): [("f2", 5), ("f3", 4), ("q00", 3)],
    ("epi", 1, 0): [("f0", 5), ("q10", 1), ("q11", 1), ("q12", 1), ("f2", 6), ("f3", 5), ("l", 0), ("q00", 4), ("q10", 2), ("f0", 6), ("q11", 2), ("q10", 3), ("q12", 2), ("q11", 3), ("q12", 3), ("f3", 6), ("l", 1), ("q00", 5), ("q10", 4), ("q11", 4), ("q12", 4), ("l", 2), ("q10", 5), ("q11", 5), ("q12", 5), ("q00", 6), ("q10", 6), ("l", 3), ("q11", 6), ("q12", 6)],
}


def back_kernel(
    n_grp, lengths, qt, k, kt, v, ot0, ot1, lse0, lse1, cos_t, sin_t, early_in, scale_rows,
    grads_in, mixed_hbm, packed_hbm, wq_hbm, wk_hbm, wv_hbm, frames_hbm, middle_hbm, mod_hbm,
    frames_grad, packed_out, qg0, qg1, early_out, late_out, embed_out,
    grad_t, row_dots, dqt, dkt, dvt, nat_ref, rolled, mixed, packed, weights, frames, middle,
    landing, dw, send_d, got_d, early_got, late_got, summed_q, q_extra,
    send_sem, recv_sem, load_sem,
):
    my_row, my_grp = lax.axis_index("row"), lax.axis_index("grp")
    total = k.shape[0]
    block = total // 4
    steps = total // TILE
    half = HEAD_DIM // 2
    _, starts, ends, offset = layout_of(lengths)
    bits = bits_of(n_grp)
    extra = bits[3:]
    side = lambda bit: (my_grp // bit) % 2
    by_row = lambda j: {"row": my_row ^ j}
    by_grp = lambda bit: {"grp": my_grp ^ bit}
    q_out = (qg0, qg1)

    chains, numbers, started = {}, {}, []

    def copies_of(name, step):
        out = []
        for index, (src, dst, device) in enumerate(chains[name][step][0]()):
            number = numbers.setdefault((name, step, index), len(numbers))
            out.append(
                pltpu.make_async_remote_copy(
                    src, dst, send_sem.at[number], recv_sem.at[number],
                    device_id=device, device_id_type=MESH,
                )
            )
        return out

    def start(name, step=0):
        started.append((name, step))
        for copy in copies_of(name, step):
            copy.start()

    def advance(name, step):
        for copy in copies_of(name, step):
            copy.wait_recv()
        chains[name][step][1]()
        if step + 1 < len(chains[name]):
            start(name, step + 1)

    def run_hook(mark):
        for name, step in HOOKS.get(mark, ()):
            advance(name, step)

    def one_step(number, src, dst, device):
        copy = pltpu.make_async_remote_copy(
            src, dst, send_sem.at[number], recv_sem.at[number], device_id=device, device_id_type=MESH
        )
        copy.start()
        copy.wait()

    def away(region, bit):
        offset, size = region
        return pl.ds(pl.multiple_of(offset + (1 - side(bit)) * (size // 2), 16), size // 2)

    def kept(region, bit):
        offset, size = region
        return (offset + side(bit) * (size // 2), size // 2)

    def at(region):
        return pl.ds(pl.multiple_of(region[0], 16), region[1])

    nothing = lambda: None

    def feed_chain(name, region, order, land):
        chain, areas, shards = [], [], (1, 0)
        for op in order:
            source = packed if chain else packed_hbm
            if op == "x":

                def parts(region=region, land=land, source=source):
                    return [(source.at[1, at(region)], landing.at[pl.ds(land, region[1])], by_row(2))]

                def take(region=region, land=land):
                    got = landing[land : land + region[1]]
                    packed[0, at(region)] = add_low(packed[0, at(region)], got)

                shards, land = (0,), land + region[1]
            else:
                size = region[1] // 2

                def parts(region=region, land=land, source=source, shards=shards, size=size, op=op):
                    return [
                        (
                            source.at[shard, away(region, op)],
                            landing.at[pl.ds(land + i * size, size)],
                            by_grp(op),
                        )
                        for i, shard in enumerate(shards)
                    ]

                region = kept(region, op)

                def take(region=region, land=land, shards=shards, size=size):
                    for i, shard in enumerate(shards):
                        got = landing[land + i * size : land + (i + 1) * size]
                        packed[shard, at(region)] = add_low(packed[shard, at(region)], got)

                land += size * len(shards)
                areas.append((op, region))
            chain.append((parts, take))
        last = chain[-1][1]

        def own():
            last()
            for i, bit in enumerate(extra):
                first, size = land + i * region[1], region[1]
                number = numbers.setdefault((name, "extra", i), len(numbers))
                one_step(number, packed.at[0, at(region)], landing.at[pl.ds(first, size)], by_grp(bit))
                packed[0, at(region)] = add_low(packed[0, at(region)], landing[first : first + size])
            packed_out[at(region)] = packed[0, at(region)]

        chain[-1] = (chain[-1][0], own)
        for bit, area in reversed(areas):
            chain.append(
                (
                    lambda bit=bit, area=area: [
                        (packed_out.at[at(area)], packed_out.at[at(area)], by_grp(bit))
                    ],
                    nothing,
                )
            )
        chains[name] = chain
        return land + len(extra) * region[1]

    def heads_chain(name, pair, number, lanes, order):
        chain, areas, region = [], [], (0, 256)
        for bit in order:
            size = region[1] // 2
            land = slice(256 - region[1], 256 - size)

            def parts(region=region, bit=bit, land=land):
                return [
                    (
                        dw.at[pair, :, away(region, bit), lanes],
                        summed_q.at[pair, :, pl.ds(land.start, land.stop - land.start), lanes],
                        by_grp(bit),
                    )
                ]

            region = kept(region, bit)

            def take(region=region, land=land):
                mine = at(region)
                dw[pair, :, mine, lanes] = add_low(
                    dw[pair, :, mine, lanes], summed_q[pair, :, land, lanes]
                )

            areas.append((bit, region))
            chain.append((parts, take))
        last, part = chain[-1][1], region

        def own():
            last()
            for i, bit in enumerate(extra):
                slot = 4 * (pair * len(extra) + i)
                count = numbers.setdefault((name, "extra", i), len(numbers))
                one_step(
                    count, dw.at[pair, :, at(part), lanes], q_extra.at[pl.ds(slot, 4), :, lanes],
                    by_grp(bit),
                )
                dw[pair, :, at(part), lanes] = add_low(
                    dw[pair, :, at(part), lanes], q_extra[slot : slot + 4, :, lanes]
                )
            q_out[pair][0, at(part), lanes] = dw[pair, my_row, at(part), lanes]

        chain[-1] = (chain[-1][0], own)
        chain.append(
            (
                lambda: [
                    (
                        dw.at[pair, my_row ^ j, at(part), lanes],
                        q_out[pair].at[j, at(part), lanes],
                        by_row(j),
                    )
                    for j in (1, 2, 3)
                ],
                nothing,
            )
        )
        for bit, area in reversed(areas):
            spot = lambda area=area: q_out[pair].at[:, at(area), lanes]
            chain.append((lambda bit=bit, spot=spot: [(spot(), spot(), by_grp(bit))], nothing))
        chains[name] = chain

    def gather_chain(name, got, out, finish):
        def first():
            out[0] = finish((got[0] + got[1]) + (got[2] + got[3]))

        chain = [(lambda: [(got.at[my_row], got.at[my_row], by_row(j)) for j in (1, 2, 3)], first)]
        for i, bit in enumerate(bits):
            chain.append(
                (
                    lambda i=i, bit=bit: [
                        (out.at[pl.ds(0, 1 << i)], out.at[pl.ds(1 << i, 1 << i)], by_grp(bit))
                    ],
                    nothing,
                )
            )
        chains[name] = chain

    def fold(sums):
        width = sums.shape[1] // 2
        return jnp.concatenate([sums[:, :width], sums[:, width:]], 0).astype(BF)

    loads = [
        pltpu.make_async_copy(src, dst, load_sem.at[i])
        for i, (src, dst) in enumerate(
            (
                (packed_hbm, packed),
                (mixed_hbm, mixed),
                (wq_hbm, mixed.at[pl.ds(0, D)]),
                (wk_hbm, mixed.at[pl.ds(D, D)]),
                (wv_hbm, weights),
                (frames_hbm, frames),
                (middle_hbm, middle),
            )
        )
    ]
    for load in loads[:1] + loads[4:]:
        load.start()

    barrier = pltpu.get_barrier_semaphore()
    for device in [by_row(j) for j in (1, 2, 3)] + [by_grp(bit) for bit in bits]:
        pl.semaphore_signal(barrier, inc=1, device_id=device, device_id_type=MESH)
    pl.semaphore_wait(barrier, 3 + len(bits))

    gather_chain("e", early_got, early_out, fold)
    early_got[my_row] = early_in[...]
    start("e")
    land, first_row = 0, 0
    for number, (count, order) in enumerate(FEED_PIECES):
        land = feed_chain(f"f{number}", (first_row, count), order, land)
        first_row += count
        start(f"f{number}")

    lanes_of = slice(0, 256)
    for j in range(4):
        mixed[pl.ds(pl.multiple_of((my_row ^ j) * block, block), block), lanes_of] = grads_in[j]
    ahead = roll_matrix(offset)

    def turn(i, carry):
        cols = pl.ds(pl.multiple_of(i * TILE, TILE), TILE)
        after = pl.ds(pl.multiple_of((i + 1) % steps * TILE, TILE), TILE)
        part = matdot(ahead[:, :TILE], mixed[cols, lanes_of], 1, 0)
        part = (part + matdot(ahead[:, TILE:], mixed[after, lanes_of], 1, 0)).T
        grad_t[:, cols] = part.astype(BF)
        for head in range(4):
            mine = slice((head % 2) * HEAD_DIM, (head % 2 + 1) * HEAD_DIM)
            crossed = part[head * HEAD_DIM : (head + 1) * HEAD_DIM] * (ot0, ot1)[head // 2][
                mine, cols
            ].astype(F32)
            row_dots[head : head + 1, cols] = jnp.sum(crossed, axis=0, keepdims=True)
        return carry

    lax.fori_loop(0, steps, turn, 0)
    loads[1].start()
    loads[0].wait()

    def run(pair, here, spans, allowed):
        lanes = slice(pair * 128, (pair + 1) * 128)
        lse = (lse0, lse1)[pair]
        for head in range(2):
            mine = slice(head * HEAD_DIM, (head + 1) * HEAD_DIM)
            wide = slice(pair * 128 + head * HEAD_DIM, pair * 128 + (head + 1) * HEAD_DIM)
            dots = slice(2 * pair + head, 2 * pair + head + 1)
            grad_query = None
            for first, count in spans:
                keys = pl.ds(first, count)
                scores = matdot(k[keys, lanes], one_head(qt[lanes, here], head), 1, 0)
                if allowed is not None:
                    scores = jnp.where(allowed, scores, -1e30)
                probs = jnp.exp(scores - lse[head : head + 1, here])
                grad_probs = matdot(v[keys, lanes], one_head(grad_t[lanes, here], head), 1, 0)
                grad_scores = (probs * (grad_probs - row_dots[dots, here])).astype(BF)
                part = matdot(kt[wide, keys], grad_scores, 1, 0)
                grad_query = part if grad_query is None else grad_query + part
                dkt[mine, keys] += matdot(qt[wide, here], grad_scores, 1, 1)
                dvt[mine, keys] += matdot(grad_t[wide, here], probs.astype(BF), 1, 1)
            dqt[mine, here] = grad_query * HEAD_DIM**-0.5

    def finish(pair):
        def part(i, sums):
            cols = pl.ds(pl.multiple_of(i * TILE, TILE), TILE)
            cosine, sine = cos_t[:, cols], sin_t[:, cols]

            def turned(ref):
                parts = []
                for at_row in range(0, 128, HEAD_DIM):
                    first = ref[at_row : at_row + half, cols]
                    second = ref[at_row + half : at_row + HEAD_DIM, cols]
                    parts.append(first * cosine + second * sine)
                    parts.append(second * cosine - first * sine)
                return jnp.concatenate(parts, 0)

            columns = jnp.concatenate([turned(dqt), turned(dkt), dvt[:, cols]], 0)
            nat_ref[:, pl.ds(pl.multiple_of(TILE + i * TILE, TILE), TILE)] = columns.astype(BF)
            low = columns.T.astype(BF)
            rolled[cols, :] = low
            return sums + jnp.sum(low.astype(F32), axis=0, keepdims=True)

        sums = lax.fori_loop(0, steps, part, jnp.zeros((1, 384), F32))
        if pair == 1:
            for copy in copies_of("d0", 0):
                copy.wait_send()
        unroll(
            [got_d.at[my_row, pair]] + [send_d.at[j] for j in range(3)], nat_ref, my_row, offset, block
        )
        chains[f"d{pair}"] = [
            (
                lambda: [(send_d.at[j - 1], got_d.at[my_row, pair], by_row(j)) for j in (1, 2, 3)],
                nothing,
            )
        ]
        start(f"d{pair}")
        run_hook(("fin", pair, 0))
        if pair == 0:
            loads[1].wait()
        for shard in range(4):
            columns = mixed[:, shard * 256 : (shard + 1) * 256]
            dw[pair, shard] = contract_rows(columns, rolled[...]).astype(BF)
        lane = 0
        for number, (count, order) in enumerate(HEAD_PIECES[pair]):
            heads_chain(f"q{pair}{number}", pair, number, pl.ds(lane, count), order)
            start(f"q{pair}{number}")
            lane += count
        return sums

    bias_sums = []
    for pair in range(2):
        dkt[...] = jnp.zeros_like(dkt)
        dvt[...] = jnp.zeros_like(dvt)

        def tile(i, carry):
            run(pair, pl.ds(pl.multiple_of(i * TILE, TILE), TILE), BACK_SPANS, None)
            for when in range(steps - 1):
                if ("tile", pair, when) in HOOKS:
                    pl.when(i == when)(functools.partial(run_hook, ("tile", pair, when)))
            return carry

        lax.fori_loop(0, steps - 1, tile, 0)
        tail = total - LONGEST
        run(pair, pl.ds(LONGEST, tail), [(LONGEST, tail)], tail_allowed(ends, offset, total))
        run_hook(("tile", pair, steps - 1))
        bias_sums.append(finish(pair))
        if pair == 1:
            for load in loads[2:4]:
                load.start()
        run_hook(("fin", pair, 1))

    for pair in range(2):
        advance(f"d{pair}", 0)
    for load in loads[2:]:
        load.wait()
    late = [jnp.zeros((1, 2 * D), F32) for _ in range(4)]
    for part in range(block // TILE):
        rows = slice(part * TILE, (part + 1) * TILE)
        grad = jnp.zeros((TILE, D), F32)
        for kind in range(3):
            pieces = [
                got_d[owner, pair, rows, kind * 128 : (kind + 1) * 128]
                for owner in range(4)
                for pair in range(2)
            ]
            weight = weights[...] if kind == 2 else mixed[kind * D : (kind + 1) * D]
            grad = grad + against(jnp.concatenate(pieces, 1), weight)
        normed, factor = normalize(frames[rows, :].astype(F32))
        spots = my_row * block + part * TILE + lax.broadcasted_iota(jnp.int32, (TILE, 1), 0)
        marks = marks_of(spots, starts, ends)
        scale = jnp.ones((TILE, D), F32)
        for u in range(4):
            scale = scale + marks[u] * scale_rows[u : u + 1, D : 2 * D]
        back = normalize_back(grad * scale, normed, factor)
        frames_grad[rows, :] = (middle[rows, :] + back).astype(BF)
        for u in range(4):
            mark = marks[u]
            late[u] += jnp.concatenate(
                [jnp.sum(t * mark, axis=0, keepdims=True) for t in (grad, grad * normed)], 1
            )
        if part == 0:
            run_hook(("epi", 0, 0))

    widths = [slice(kind * 128, (kind + 1) * 128) for kind in range(3)]
    bias_row = jnp.concatenate(
        [bias_sums[pair][:, w] for w in widths for pair in range(2)]
        + [jnp.zeros((1, 2 * D - 768), F32)],
        1,
    )
    index = lax.broadcasted_iota(jnp.int32, (8, 2 * D), 0)
    gather_chain(
        "l", late_got, late_out, lambda sums: fold(jnp.where(index == 4, bias_row, sums))
    )
    late_got[my_row] = jnp.concatenate(late + [jnp.zeros((4, 2 * D), F32)], 0)
    start("l")

    slots = [mixed.at[pl.ds(0, D)], mixed.at[pl.ds(D, D)], weights]
    blocks = [2, 3, 4, 5, 0, 1]
    fetches = [
        pltpu.make_async_copy(
            mod_hbm.at[:, pl.ds(block * D, D)], slots[i % 3], load_sem.at[len(loads) + i % 3]
        )
        for i, block in enumerate(blocks)
    ]
    for fetch in fetches[:3]:
        fetch.start()
    embed_out[...] = jnp.zeros_like(embed_out)

    def embed_step(i):
        block = blocks[i]
        fetches[i].wait()
        if block < 2:
            rows = late_out[0].astype(F32)[8 * block : 8 * block + 8]
        else:
            part, lane = divmod(block - 2, 2)
            rows = early_out[0, :, lane * D : (lane + 1) * D].astype(F32)[8 * part : 8 * part + 8]
        embed_out[...] += against(rows.astype(BF), slots[i % 3][...])
        if i + 3 < len(blocks):
            fetches[i + 3].start()

    done, late_ready = 0, False
    for number, (name, step) in enumerate(HOOKS[("epi", 1, 0)]):
        advance(name, step)
        late_ready = late_ready or (name, step) == ("l", 0)
        if number % 3 == 2 and done < (6 if late_ready else 4):
            embed_step(done)
            done += 1
    for i in range(done, 6):
        embed_step(i)
    for number in range(3, len(bits)):
        advance("e", number + 1)
        advance("l", number + 1)
    for name, step in started:
        if name != "d0":
            for copy in copies_of(name, step):
                copy.wait_send()


def attend_back(
    n_grp, lengths, qt, k, kt, v, heads_t, lse, cos_t, sin_t, early, scale_rows, grads, mixed, packed, weights, frames, middle, mod_weight,
):
    total = k.shape[0]
    block = total // 4
    rows = packed.shape[1]
    extra = max(0, len(bits_of(n_grp)) - 3)
    inputs = [
        qt, k, kt, v, *heads_t, *lse, cos_t, sin_t, early, scale_rows, grads,
    ]
    far = [mixed, packed, *weights, frames, middle, mod_weight]
    copies = 160
    return pl.pallas_call(
        functools.partial(back_kernel, n_grp),
        out_shape=[
            jax.ShapeDtypeStruct((block, D), BF),
            jax.ShapeDtypeStruct((rows, D), BF),
            jax.ShapeDtypeStruct((4, 256, 384), BF),
            jax.ShapeDtypeStruct((4, 256, 384), BF),
            jax.ShapeDtypeStruct((n_grp, 16, 2 * D), BF),
            jax.ShapeDtypeStruct((n_grp, 16, D), BF),
            jax.ShapeDtypeStruct((8, D), F32),
        ],
        in_specs=[pl.BlockSpec(memory_space=SMEM)]
        + [pl.BlockSpec(memory_space=VMEM)] * len(inputs)
        + [pl.BlockSpec(memory_space=pl.ANY)] * len(far),
        out_specs=[pl.BlockSpec(memory_space=VMEM)] * 7,
        scratch_shapes=[
            VMEM((256, total), BF),
            VMEM((8, total), F32),
            VMEM((128, total), F32),
            VMEM((128, total), F32),
            VMEM((128, total), F32),
            VMEM((384, total + TILE), BF),
            VMEM((total, 384), BF),
            VMEM((total, D), BF),
            VMEM((2, rows, D), BF),
            VMEM((D, D), BF),
            VMEM((block, D), BF),
            VMEM((block, D), F32),
            VMEM((rows * (15 + extra) // 8, D), BF),
            VMEM((2, 4, 256, 384), BF),
            VMEM((3, block, 384), BF),
            VMEM((4, 2, block, 384), BF),
            VMEM((4, 8, 4 * D), F32),
            VMEM((4, 8, 2 * D), F32),
            VMEM((2, 4, 256, 384), BF),
            VMEM((max(1, 8 * extra), 32, 384), BF),
            pltpu.SemaphoreType.DMA((copies,)),
            pltpu.SemaphoreType.DMA((copies,)),
            pltpu.SemaphoreType.DMA((len(far) + 3,)),
        ],
        compiler_params=pltpu.CompilerParams(
            vmem_limit_bytes=62 << 20, collective_id=1, has_side_effects=True
        ),
        cost_estimate=pl.CostEstimate(
            flops=4 * 2 * 5 * total * LONGEST * 256,
            bytes_accessed=40 << 20,
            transcendentals=4 * total * LONGEST,
        ),
        name="attend_back",
    )(lengths, *inputs, *far)


def feed_kernel(
    lengths, o, frames, cot, mod, act, out_bias, up_bias, down_bias, out_hbm, up_hbm, down_hbm,
    output, middle_out, grads_out, packed, early_out,
    w_out, w_up, w_down, h_s, a_s, ez_s, eb_s, ea_s, send_o, send_w, got_w, load_sem, send_sem, recv_sem,
):
    my_row = lax.axis_index("row")
    by_row = lambda j: {"row": my_row ^ j}
    rows_all = frames.shape[0]
    _, starts, ends, _ = layout_of(lengths)
    width = D // 4
    loads = [
        pltpu.make_async_copy(
            out_hbm.at[pl.ds(pl.multiple_of((my_row ^ j) * width, width), width)],
            w_out.at[pl.ds(j * width, width)],
            load_sem.at[j],
        )
        for j in range(4)
    ] + [
        pltpu.make_async_copy(up_hbm, w_up, load_sem.at[4]),
        pltpu.make_async_copy(down_hbm, w_down, load_sem.at[5]),
    ]
    for load in loads:
        load.start()
    barrier = pltpu.get_barrier_semaphore()
    for j in (1, 2, 3):
        pl.semaphore_signal(barrier, inc=1, device_id=by_row(j), device_id_type=MESH)
    pl.semaphore_wait(barrier, 3)

    def remote(number, src, dst, j):
        return pltpu.make_async_remote_copy(
            src, dst, send_sem.at[number], recv_sem.at[number], device_id=by_row(j), device_id_type=MESH
        )

    copies = []
    coef = math.sqrt(2.0 / math.pi)
    sums = [[jnp.zeros((1, D), F32) for _ in range(4)] for _ in range(4)]
    bias_sums = [jnp.zeros((1, n), F32) for n in (D, 2 * D, D)]
    for tile in range(rows_all // TILE):
        rows = slice(tile * TILE, (tile + 1) * TILE)
        spots = my_row * rows_all + tile * TILE + lax.broadcasted_iota(jnp.int32, (TILE, 1), 0)
        marks = marks_of(spots, starts, ends)

        def per_row(block):
            total = marks[0] * mod[0:1, block * D : (block + 1) * D]
            for u in range(1, 4):
                total = total + marks[u] * mod[u : u + 1, block * D : (block + 1) * D]
            return total

        gate_a, shift_f, scale_f, gate_f = per_row(2), per_row(3), 1.0 + per_row(4), per_row(5)
        if tile == 0:
            for load in loads[:4]:
                load.wait()
        heads = jnp.concatenate([o[j, rows, :] for j in range(4)], 1)
        attended = matdot(heads, w_out[...], 1, 0) + out_bias[...]
        middle = frames[rows, :].astype(F32) + gate_a * attended
        normed, factor = normalize(middle)
        h = (normed * scale_f + shift_f).astype(BF)
        h_s[rows, :] = h
        if tile == 0:
            loads[4].wait()
        z = matdot(h, w_up[...], 1, 0) + up_bias[...]
        square = z * z
        curve = jnp.tanh(coef * (z * (1.0 + 0.044715 * square)))
        share = 0.5 * (1.0 + curve)
        a = (z * share).astype(BF)
        a_s[rows, :] = a
        slope = share + (0.5 * coef) * z * (1.0 - curve * curve) * (1.0 + (3 * 0.044715) * square)
        if tile == 0:
            loads[5].wait()
        branch = matdot(a, w_down[...], 1, 0) + down_bias[...]
        output[rows, :] = (middle + gate_f * branch).astype(BF)
        upstream = cot[rows, :].astype(F32)
        e_b = (upstream * gate_f).astype(BF)
        eb_s[rows, :] = e_b
        e_z = (against(e_b, w_down[...]) * slope).astype(BF)
        ez_s[rows, :] = e_z
        e_h = against(e_z, w_up[...])
        e_mid = upstream + normalize_back(e_h * scale_f, normed, factor)
        middle_out[rows, :] = e_mid
        e_att = (e_mid * gate_a).astype(BF)
        ea_s[rows, :] = e_att
        e_o = against(e_att, w_out[...]).astype(BF)
        grads_out[0, rows, :] = e_o[:, :width]
        for j in (1, 2, 3):
            send_o[j - 1, rows, :] = e_o[:, j * width : (j + 1) * width]
            copies.append(
                remote(
                    len(copies), send_o.at[j - 1, pl.ds(tile * TILE, TILE)],
                    grads_out.at[j, pl.ds(tile * TILE, TILE)], j,
                )
            )
            copies[-1].start()
        for block, part in enumerate((e_mid * attended, e_h, e_h * normed, upstream * branch)):
            for u in range(4):
                sums[u][block] += jnp.sum(part * marks[u], axis=0, keepdims=True)
        for number, part in enumerate((e_att, e_z, e_b)):
            bias_sums[number] += jnp.sum(part.astype(F32), axis=0, keepdims=True)

    early_out[...] = jnp.concatenate(
        [jnp.concatenate(row, 1) for row in sums + [bias_sums]]
        + [act[...] * 0.25, jnp.zeros((2, 4 * D), F32)],
        0,
    )

    def shard(j, store):
        owner = my_row ^ j
        columns = pl.ds(pl.multiple_of(owner * 2 * width, 2 * width), 2 * width)
        store(768, contract_rows(a_s[:, columns], eb_s[...]))
        columns = pl.ds(pl.multiple_of(owner * width, width), width)
        store(256, contract_rows(h_s[:, columns], ez_s[:, :D]))
        store(512, contract_rows(h_s[:, columns], ez_s[:, D:]))
        store(0, contract_rows(o[j], ea_s[...]))

    for slot, j in enumerate((1, 3)):

        def store(first, value):
            send_w[slot, first : first + value.shape[0], :] = value.astype(BF)

        shard(j, store)
        copies.append(remote(len(copies), send_w.at[slot], got_w.at[slot], 1))
        copies[-1].start()
    for slot, j in enumerate((0, 2)):

        def store(first, value):
            packed[slot, first : first + value.shape[0], :] = value.astype(BF)

        shard(j, store)
    for slot in range(2):
        copies[-2 + slot].wait_recv()
        packed[slot] = add_low(packed[slot], got_w[slot])
    for copy in copies[:-2]:
        copy.wait_recv()
    for copy in copies:
        copy.wait_send()


def feed(lengths, o, frames, cot, mod, act, biases, weights):
    rows = frames.shape[0]
    inputs = [o, frames, cot, mod, act, *[b[None] for b in biases]]
    return pl.pallas_call(
        feed_kernel,
        out_shape=[
            jax.ShapeDtypeStruct((rows, D), BF),
            jax.ShapeDtypeStruct((rows, D), F32),
            jax.ShapeDtypeStruct((4, rows, D // 4), BF),
            jax.ShapeDtypeStruct((2, 1280, D), BF),
            jax.ShapeDtypeStruct((8, 4 * D), F32),
        ],
        in_specs=[pl.BlockSpec(memory_space=SMEM)]
        + [pl.BlockSpec(memory_space=VMEM)] * len(inputs)
        + [pl.BlockSpec(memory_space=pl.ANY)] * 3,
        out_specs=[pl.BlockSpec(memory_space=VMEM)] * 5,
        scratch_shapes=[
            VMEM((D, D), BF),
            VMEM((D, 2 * D), BF),
            VMEM((2 * D, D), BF),
            VMEM((rows, D), BF),
            VMEM((rows, 2 * D), BF),
            VMEM((rows, 2 * D), BF),
            VMEM((rows, D), BF),
            VMEM((rows, D), BF),
            VMEM((3, rows, D // 4), BF),
            VMEM((2, 1280, D), BF),
            VMEM((2, 1280, D), BF),
            pltpu.SemaphoreType.DMA((6,)),
            pltpu.SemaphoreType.DMA((3 * rows // TILE + 2,)),
            pltpu.SemaphoreType.DMA((3 * rows // TILE + 2,)),
        ],
        compiler_params=pltpu.CompilerParams(
            vmem_limit_bytes=LIMIT, collective_id=2, has_side_effects=True
        ),
        cost_estimate=pl.CostEstimate(
            flops=2 * rows * D * 15 * D, bytes_accessed=30 << 20, transcendentals=rows * 2 * D
        ),
        name="feed",
    )(lengths, *inputs, *weights)


def outputs_kernel(
    packed, heads_0, heads_1, early, late, embedding, embed_in,
    out_far, up_far, down_far, query_far, key_far, value_far, mod_far,
    mod_b, embed, out_b, up_b, down_b, query_b, key_b, value_b,
    out_w, up_w, down_w, query_w, key_w, value_w, mod_w, rows_ref, mod_ref, store_sem,
):
    my_row = lax.axis_index("row")
    width = D // 4
    stores = []

    def store(src, dst):
        stores.append(pltpu.make_async_copy(src, dst, store_sem.at[len(stores)]))
        stores[-1].start()

    n_grp = early.shape[0]
    out_w[...] = packed[:width].astype(F32)
    up_w[:, :D] = packed[width : 2 * width].astype(F32)
    up_w[:, D:] = packed[2 * width : 3 * width].astype(F32)
    store(out_w, out_far)
    store(up_w, up_far)
    down_w[...] = packed[3 * width :].astype(F32)
    store(down_w, down_far)
    for pair, heads in enumerate((heads_0, heads_1)):
        for j in range(4):
            lanes = pl.ds(pl.multiple_of((my_row ^ j) * width + pair * 128, 128), 128)
            for kind, out in enumerate((query_w, key_w, value_w)):
                out[:, lanes] = heads[j, :, kind * 128 : (kind + 1) * 128].astype(F32)
    store(query_w, query_far)
    store(key_w, key_far)
    store(value_w, value_far)
    for first, source, count in ((0, late, D), (2 * D, early, 2 * D)):
        for part in range(2):
            rows = source[:, 8 * part : 8 * part + 8].astype(F32).reshape(n_grp * 8, count)
            mod_ref[:, first + part * count : first + (part + 1) * count] = rows
    number = lax.broadcasted_iota(jnp.int32, (n_grp * 8, 1), 0) % 8
    utterance, bias = (number < 4).astype(F32), (number == 4).astype(F32)
    act = jnp.zeros((n_grp * 8, width), F32)
    for u in range(4):
        lanes = pl.ds(pl.multiple_of((2 + u) * D + my_row * width, width), width)
        moved = pltpu.roll(mod_ref[:, lanes], (u - 5) % (n_grp * 8), 0)
        act = jnp.where(number == u, moved, act)
    act = act.astype(BF)
    for block in range(6):
        lanes = slice(block * D, (block + 1) * D)
        rows = mod_ref[:, lanes]
        mod_w[:, lanes] = contract_rows(act, rows.astype(BF))
        store(mod_w.at[:, pl.ds(block * D, D)], mod_far.at[:, pl.ds(block * D, D)])
        sums = [jnp.sum(rows * mark, axis=0, keepdims=True) for mark in (utterance, bias)]
        rows_ref[:, lanes] = jnp.concatenate(sums + [jnp.zeros((6, D), F32)], 0)

    def own(row, first, size):
        lanes = pl.ds(pl.multiple_of(first + my_row * size, 128), size)
        return rows_ref[row : row + 1, lanes]

    mod_b[...] = own(0, 0, 6 * width)
    for i, out in enumerate((query_b, key_b, value_b)):
        out[...] = rows_ref[1:2, i * width : (i + 1) * width]
    out_b[...] = own(1, 2 * D, width)
    up_b[...] = own(1, 3 * D, 2 * width)
    down_b[...] = own(1, 5 * D, width)
    gate = 1.0 / (1.0 + jnp.exp(-embedding[...]))
    embed[...] = embed_in[:4] * (gate * (1.0 + embedding[...] * (1.0 - gate)))
    for copy in stores:
        copy.wait()


def outputs(packed, heads_0, heads_1, early, late, embedding, embed_in):
    width = D // 4
    n_grp = early.shape[0]
    shapes = [(width, D), (width, 2 * D), (2 * width, D)] + [(width, D)] * 3 + [(width, 6 * D)]
    shapes += [(1, 6 * width), (4, D)] + [(1, n) for n in (width, 2 * width, width, width, width, width)]
    return pl.pallas_call(
        outputs_kernel,
        out_shape=[jax.ShapeDtypeStruct(shape, F32) for shape in shapes],
        in_specs=[pl.BlockSpec(memory_space=VMEM)] * 7,
        out_specs=[pl.BlockSpec(memory_space=pl.ANY)] * 7
        + [pl.BlockSpec(memory_space=VMEM)] * (len(shapes) - 7),
        scratch_shapes=[VMEM(shape, F32) for shape in shapes[:7]]
        + [
            VMEM((8, 6 * D), F32),
            VMEM((n_grp * 8, 6 * D), F32),
            pltpu.SemaphoreType.DMA((12,)),
        ],
        compiler_params=pltpu.CompilerParams(vmem_limit_bytes=LIMIT),
        name="outputs",
    )(packed, heads_0, heads_1, early, late, embedding, embed_in)


def local(
    frames, time_embed, lengths, mod_weight, mod_bias, query_weight, query_bias, key_weight, key_bias,
    value_weight, value_bias, out_weight, out_bias, up_weight, up_bias, down_weight, down_bias, cotangent,
):
    n_grp = lax.axis_size("grp")
    lengths, embedding = lengths[0], time_embed[0]
    weights = (query_weight, key_weight, value_weight)
    mixed, qt, kt, k_rows, v_rows, cos_t, sin_t, modulation, act, *heads_t, lse_0, lse_1, o_all = front(
        lengths, frames, embedding, mod_weight, mod_bias, weights, (query_bias, key_bias, value_bias)
    )
    output, grad_middle, grad_pieces, packed, early = feed(
        lengths, o_all, frames, cotangent, modulation, act, (out_bias, up_bias, down_bias),
        (out_weight, up_weight, down_weight),
    )
    grad_frames, packed_total, heads_0, heads_1, early_all, late_all, embed_part = attend_back(
        n_grp, lengths, qt, k_rows, kt, v_rows, heads_t, (lse_0, lse_1), cos_t, sin_t, early,
        modulation, grad_pieces, mixed, packed, weights, frames, grad_middle, mod_weight,
    )
    grads = outputs(packed_total, heads_0, heads_1, early_all, late_all, embedding, embed_part)
    out_grad, up_grad, down_grad, query_grad, key_grad, value_grad, mod_weight_grad = grads[:7]
    mod_bias_grad, grad_embedding = grads[7][0], grads[8]
    out_b, up_b, down_b, query_b, key_b, value_b = (b[0] for b in grads[9:])
    return (
        output,
        grad_frames,
        grad_embedding[None],
        mod_weight_grad,
        mod_bias_grad,
        query_grad,
        query_b,
        key_grad,
        key_b,
        value_grad,
        value_b,
        out_grad,
        out_b,
        up_grad,
        up_b,
        down_grad,
        down_b,
    )


def solution(mesh):
    placed = (
        (P(("grp", "row"), None), P("grp", None, None), P("grp", None))
        + (P(),) * 14
        + (P(("grp", "row"), None),)
    )
    return jax.shard_map(
        local,
        mesh=mesh,
        in_specs=placed,
        out_specs=(
            P(("grp", "row"), None),
            P(("grp", "row"), None),
            P("grp", None, None),
        )
        + (P("row", None), P("row")) * 7,
        check_vma=False,
    )
```

```python
import functools
import math

import jax
import jax.numpy as jnp
import numpy as np
from jax import lax
from jax.experimental import pallas as pl
from jax.experimental.pallas import tpu as pltpu
from jax.sharding import PartitionSpec as P

D = 1024
HEADS = 16
HEAD_DIM = 64
LONGEST = 1792
TILE = 256
BF = jnp.bfloat16
F32 = jnp.float32

highest = lax.Precision.HIGHEST
VMEM = pltpu.VMEM
SMEM = pltpu.SMEM
LIMIT = 60 << 20
MESH = pl.DeviceIdType.MESH
BACK_SPANS = [(0, 896), (896, 896)]


def matdot(left, right, left_dim, right_dim):
    return lax.dot_general(
        left, right, (((left_dim,), (right_dim,)), ((), ())), preferred_element_type=F32
    )


def contract_rows(left, right):
    return matdot(left, right, 0, 0)


def against(left, weight):
    return matdot(left, weight, 1, 1)


def column_sum(tensor):
    return jnp.sum(tensor.astype(F32), axis=0)


def normalize(tensor):
    centred = tensor - jnp.mean(tensor, axis=-1, keepdims=True)
    factor = lax.rsqrt(jnp.mean(centred * centred, axis=-1, keepdims=True) + 1e-06)
    return (centred * factor, factor)


def normalize_back(grad_normed, normed, factor):
    mean_grad = jnp.mean(grad_normed, axis=-1, keepdims=True)
    mean_cross = jnp.mean(grad_normed * normed, axis=-1, keepdims=True)
    return (grad_normed - mean_grad - normed * mean_cross) * factor


def exchange(tensor, axis, bit):
    size = lax.axis_size(axis)
    return lax.ppermute(tensor, axis, [(i, i ^ bit) for i in range(size)])


def add_low(left, right):
    return (left.astype(F32) + right.astype(F32)).astype(BF)


def bits_of(count):
    return [1 << i for i in range(count.bit_length() - 1)]


def roll_matrix(offset):
    row = lax.broadcasted_iota(jnp.int32, (TILE, 2 * TILE), 0)
    col = lax.broadcasted_iota(jnp.int32, (TILE, 2 * TILE), 1)
    return (col == row + offset).astype(F32).astype(BF)


def layout_of(lengths):
    sizes = [lengths[u] for u in range(4)]
    starts, finish, at = [], [], 0
    for size in sizes:
        starts.append(at)
        at = at + size
        finish.append(at)
    offset = 0
    for size, first in zip(sizes, starts):
        offset = offset + jnp.where(size == LONGEST, first, 0)
    return sizes, starts, finish, offset


def marks_of(rows, starts, finish):
    return [
        jnp.logical_and(rows >= first, rows < end).astype(F32) for first, end in zip(starts, finish)
    ]


def tail_allowed(finish, offset, total):
    count = total - LONGEST

    def segment(shape, dim):
        rows = LONGEST + offset + lax.broadcasted_iota(jnp.int32, shape, dim)
        rows = jnp.where(rows >= total, rows - total, rows)
        return sum((rows >= end).astype(jnp.int32) for end in finish)

    return segment((count, 1), 0) == segment((1, count), 1)


def front_kernel(
    lengths, embedding, mod_bias, q_bias, k_bias, v_bias, frequency,
    frames_hbm, mod_weight_hbm, wq_hbm, wk_hbm, wv_hbm,
    mixed_far, qt_far, kt_far, k_far, v_far, cos_out, sin_out, mod_out, act_out, ot0, ot1, lse0, lse1, o_all,
    mixed_out, qt_out, kt_out, vt_out, k_out, v_out,
    rows_ref, roll_ref, mod_weight, weight, weight_t, bias_t, rolled_ref, send_o,
    send_sem, recv_sem, load_sem, store_sem, send_o_sem, recv_o_sem,
):
    my_row = lax.axis_index("row")
    block = frames_hbm.shape[0]
    total = 4 * block
    steps = total // TILE
    width = qt_out.shape[0]
    by_row = lambda j: {"row": my_row ^ j}
    sizes, starts, finish, offset = layout_of(lengths)

    piece = TILE

    def place(j, part=0, count=piece):
        first = pl.multiple_of((my_row ^ j) * block + part * piece, piece)
        return pl.ds(first, count)

    def remote(number, src, dst, j):
        return pltpu.make_async_remote_copy(
            src, dst, send_sem.at[number], recv_sem.at[number], device_id=by_row(j), device_id_type=MESH
        )

    parts = block // piece
    barrier = pltpu.get_barrier_semaphore()
    for j in (1, 2, 3):
        pl.semaphore_signal(barrier, inc=1, device_id=by_row(j), device_id_type=MESH)
    pl.semaphore_wait(barrier, 3)
    to_x = [
        remote(i, frames_hbm.at[pl.ds(i * piece, piece)], rows_ref.at[place(0, i)], 2)
        for i in range(parts)
    ]
    to_core = remote(parts, frames_hbm, rows_ref.at[place(0, 0, block)], 1)
    onward = [
        remote(parts + 1 + i, rows_ref.at[place(2, i)], rows_ref.at[place(2, i)], 1) for i in range(parts)
    ]
    for copy in [to_core] + to_x:
        copy.start()
    columns = pl.ds(pl.multiple_of(my_row * width, width), width)
    loads = [
        pltpu.make_async_copy(src, dst, load_sem.at[i])
        for i, (src, dst) in enumerate(
            [(frames_hbm, rows_ref.at[place(0, 0, block)])]
            + [
                (w.at[:, columns], weight.at[:, pl.ds(i * width, width)])
                for i, w in enumerate((wq_hbm, wk_hbm, wv_hbm))
            ]
            + [
                (mod_weight_hbm.at[:, pl.ds(i * 2 * D, 2 * D)], mod_weight.at[i]) for i in range(3)
            ]
        )
    ]
    for load in loads:
        load.start()

    rows = lax.broadcasted_iota(jnp.int32, (1, total), 1) + offset
    rows = jnp.where(rows >= total, rows - total, rows)
    position = rows
    for first, end in zip(starts, finish):
        inside = jnp.logical_and(rows >= first, rows < end)
        position = jnp.where(inside, rows - first, position)
    angles = frequency[...] * position.astype(F32)
    cos_out[...] = jnp.cos(angles)
    sin_out[...] = jnp.sin(angles)
    roll_ref[...] = roll_matrix(offset)
    for i, bias in enumerate((q_bias, k_bias, v_bias)):
        bias_t[i : i + 1, :] = bias[0:1, columns]

    act = (embedding[...] / (1.0 + jnp.exp(-embedding[...]))).astype(BF).astype(F32)
    act_out[...] = jnp.concatenate([act[u : u + 1] for u in range(4)], 1)
    act_low = jnp.concatenate([act, jnp.zeros_like(act)], 0).astype(BF)
    for i in range(3):
        lanes = slice(i * 2 * D, (i + 1) * 2 * D)
        loads[4 + i].wait()
        mod_out[:, lanes] = matdot(act_low, mod_weight[i], 1, 0) + mod_bias[:, lanes]
    for load in loads[:4]:
        load.wait()
    for i in range(3):
        lanes = slice(i * width, (i + 1) * width)
        weight_t[lanes, :] = weight[:, lanes].T
    biases = jnp.concatenate([bias_t[i : i + 1, :] for i in range(3)], 1)
    biases = jnp.broadcast_to(biases, (8, 3 * width)).T[:, 0:1]

    mod_long = jnp.zeros((1, 2 * D), F32)
    for u in range(4):
        mod_long = mod_long + jnp.where(sizes[u] == LONGEST, 1.0, 0.0) * mod_out[u : u + 1, : 2 * D]
    half = HEAD_DIM // 2

    def tile(step, tail=False):
        here = pl.ds(pl.multiple_of(step * TILE, TILE), TILE)
        if tail:
            moved = matdot(roll_ref[:, :TILE], rows_ref[here, :], 1, 0)
            normed, _ = normalize(moved + matdot(roll_ref[:, TILE:], rows_ref[:TILE, :], 1, 0))
            spots = LONGEST + offset + lax.broadcasted_iota(jnp.int32, (TILE, 1), 0)
            spots = jnp.where(spots >= total, spots - total, spots)
            per_row = jnp.zeros((TILE, 2 * D), F32)
            for u, mark in enumerate(marks_of(spots, starts, finish)):
                per_row = per_row + mark * mod_out[u : u + 1, : 2 * D]
        else:
            both = pl.ds(pl.multiple_of(step * TILE, TILE), 2 * TILE)
            normed, _ = normalize(matdot(roll_ref[...], rows_ref[both, :], 1, 0))
            per_row = mod_long
        mixed_out[here, :] = (normed * (1.0 + per_row[:, D:]) + per_row[:, :D]).astype(BF)
        wide = matdot(weight_t[...], mixed_out[here, :], 1, 1) + biases
        cosine, sine = cos_out[:, here], sin_out[:, here]

        def turned(base):
            out = []
            for at in range(base, base + width, HEAD_DIM):
                first, second = wide[at : at + half], wide[at + half : at + HEAD_DIM]
                out.append(first * cosine - second * sine)
                out.append(second * cosine + first * sine)
            return jnp.concatenate(out, 0)

        keys = turned(width)
        values = wide[2 * width :]
        qt_out[:, here] = turned(0).astype(BF) * jnp.asarray(HEAD_DIM**-0.5, BF)
        kt_out[:, here] = keys.astype(BF)
        vt_out[:, here] = values.astype(BF)
        k_out[here, :] = keys.T.astype(BF)
        v_out[here, :] = values.T.astype(BF)

    to_core.wait_recv()
    chip = my_row // 2

    def near(i, carry):
        tile(chip * (steps // 2) + i)
        return carry

    def far(i, carry):
        tile((1 - chip) * (steps // 2 - 1) + i)
        return carry

    lax.fori_loop(0, steps // 2 - 1, near, 0)
    for arrived, copy in zip(to_x, onward):
        arrived.wait_recv()
        copy.start()
    for copy in onward:
        copy.wait_recv()
    lax.fori_loop(0, steps // 2, far, 0)
    tile(steps - 1, True)
    stores = [
        pltpu.make_async_copy(src, dst, store_sem.at[i])
        for i, (src, dst) in enumerate(
            (
                (mixed_out, mixed_far),
                (qt_out, qt_far),
                (kt_out, kt_far),
                (k_out, k_far),
                (v_out, v_far),
            )
        )
    ]
    for copy in stores:
        copy.start()
    attend_part(
        finish, offset, qt_out, k_out, vt_out, ot0, ot1, lse0, lse1, o_all, rolled_ref, send_o,
        send_o_sem, recv_o_sem,
    )
    for copy in to_x + [to_core] + onward:
        copy.wait_send()
    for copy in stores:
        copy.wait()


def front(lengths, frames, embedding, mod_weight, mod_bias, weights, biases):
    block = frames.shape[0]
    total = 4 * block
    width = D // 4
    half = HEAD_DIM // 2
    frequency = np.exp(np.arange(half) * (-2.0 * math.log(10000.0) / HEAD_DIM)).astype(np.float32)
    inputs = [embedding, mod_bias[None], *[b[None] for b in biases], jnp.asarray(frequency)[:, None]]
    far = [frames, mod_weight, *weights]
    copies = 1 + 2 * (block // TILE)
    wide, tall = (width, total), (total, width)
    stored = [(total, D), wide, wide, tall, tall]
    return pl.pallas_call(
        front_kernel,
        out_shape=[jax.ShapeDtypeStruct(shape, BF) for shape in stored]
        + [
            jax.ShapeDtypeStruct((half, total), F32),
            jax.ShapeDtypeStruct((half, total), F32),
            jax.ShapeDtypeStruct((8, 6 * D), F32),
            jax.ShapeDtypeStruct((1, 4 * D), F32),
        ]
        + [jax.ShapeDtypeStruct((128, total), BF)] * 2
        + [jax.ShapeDtypeStruct((8, total), F32)] * 2
        + [jax.ShapeDtypeStruct((4, block, 256), BF)],
        in_specs=[pl.BlockSpec(memory_space=SMEM)]
        + [pl.BlockSpec(memory_space=VMEM)] * len(inputs)
        + [pl.BlockSpec(memory_space=pl.ANY)] * len(far),
        out_specs=[pl.BlockSpec(memory_space=pl.ANY)] * 5 + [pl.BlockSpec(memory_space=VMEM)] * 9,
        scratch_shapes=[VMEM(shape, BF) for shape in [(total, D), wide, wide, wide, tall, tall]]
        + [
            VMEM((total, D), BF),
            VMEM((TILE, 2 * TILE), BF),
            VMEM((3, D, 2 * D), BF),
            VMEM((D, 3 * width), BF),
            VMEM((3 * width, D), BF),
            VMEM((8, width), F32),
            VMEM((128, total + TILE), BF),
            VMEM((6, block, 128), BF),
            pltpu.SemaphoreType.DMA((copies,)),
            pltpu.SemaphoreType.DMA((copies,)),
            pltpu.SemaphoreType.DMA((7,)),
            pltpu.SemaphoreType.DMA((5,)),
            pltpu.SemaphoreType.DMA((6,)),
            pltpu.SemaphoreType.DMA((6,)),
        ],
        compiler_params=pltpu.CompilerParams(
            vmem_limit_bytes=LIMIT, collective_id=4, has_side_effects=True
        ),
        cost_estimate=pl.CostEstimate(
            flops=2 * total * D * 3 * width + 2 * 2 * 6 * total * LONGEST * 256,
            bytes_accessed=40 << 20,
            transcendentals=4 * total * LONGEST,
        ),
        name="front",
    )(lengths, *inputs, *far)


def one_head(pair, head):
    part = pair[head * HEAD_DIM : (head + 1) * HEAD_DIM]
    empty = jnp.zeros_like(part)
    return jnp.concatenate([part, empty] if head == 0 else [empty, part], 0)


def unroll(outs, rolled_ref, my_row, offset, block):
    total = 4 * block
    rolled_ref[:, pl.ds(0, TILE)] = rolled_ref[:, pl.ds(total, TILE)]
    back = roll_matrix(TILE - offset)
    for j, out in enumerate(outs):
        for part in range(block // TILE):
            at = pl.multiple_of((my_row ^ j) * block + part * TILE, TILE)
            rows = matdot(back, rolled_ref[:, pl.ds(at, 2 * TILE)], 1, 1)
            out[part * TILE : (part + 1) * TILE, :] = rows.astype(BF)


def attend_part(
    finish, offset, qt, k, vt, ot0, ot1, lse0, lse1, o_all, rolled_ref, send_o, send_sem, recv_sem
):
    my_row = lax.axis_index("row")
    total = k.shape[0]
    block = total // 4
    tail = total - LONGEST

    def run(pair, here, first, count, allowed):
        outs, tops = [], []
        lanes = slice(pair * 128, (pair + 1) * 128)

        def scores_of(head):
            scores = matdot(k[first : first + count, lanes], one_head(qt[lanes, here], head), 1, 0)
            return scores if allowed is None else jnp.where(allowed, scores, -1e30)

        for head in range(2):
            tops.append(jnp.max(scores_of(head), axis=0, keepdims=True))
        for head in range(2):
            wide = slice(pair * 128 + head * HEAD_DIM, pair * 128 + (head + 1) * HEAD_DIM)
            weights = jnp.exp(scores_of(head) - tops[head]).astype(BF)
            values = jnp.concatenate([vt[wide, first : first + count], jnp.ones((16, count), BF)], 0)
            mixed = matdot(values, weights, 1, 0)
            exp_sum = mixed[HEAD_DIM : HEAD_DIM + 1]
            outs.append(mixed[:HEAD_DIM] / exp_sum)
            tops[head] = tops[head] + jnp.log(exp_sum)
        low = jnp.concatenate(outs, 0).astype(BF)
        (ot0, ot1)[pair][:, here] = low
        (lse0, lse1)[pair][:, here] = jnp.concatenate(tops * 4, 0)
        return low

    copies = []
    for pair in range(2):

        def tile(i, carry):
            low = run(pair, pl.ds(pl.multiple_of(i * TILE, TILE), TILE), 0, LONGEST, None)
            rolled_ref[:, pl.ds(pl.multiple_of(TILE + i * TILE, TILE), TILE)] = low
            return carry

        lax.fori_loop(0, LONGEST // TILE, tile, 0)
        low = run(pair, pl.ds(LONGEST, tail), LONGEST, tail, tail_allowed(finish, offset, total))
        rolled_ref[:, pl.ds(total, TILE)] = low
        lanes = pl.ds(pair * 128, 128)
        outs = [o_all.at[0, :, lanes]] + [send_o.at[3 * pair + j] for j in range(3)]
        unroll(outs, rolled_ref, my_row, offset, block)
        for j in (1, 2, 3):
            number = 3 * pair + j - 1
            copies.append(
                pltpu.make_async_remote_copy(
                    send_o.at[number], o_all.at[j, :, lanes], send_sem.at[number], recv_sem.at[number],
                    device_id={"row": my_row ^ j}, device_id_type=MESH,
                )
            )
            copies[-1].start()
    for copy in copies:
        copy.wait()


FEED_PIECES = ((384, ("x", 1, 2, 4)), (384, (2, 1, "x", 4)), (256, (1, 2, 4, "x")), (256, ("x", 1, 2, 4)),)
HEAD_PIECES = (
    ((384, (1, 2, 4)),),
    ((128, (1, 2, 4)), (128, (1, 2, 4)), (128, (1, 2, 4)),),
)
HOOKS = {
    ("tile", 0, 1): [("e", 0)],
    ("tile", 0, 2): [("f2", 0)],
    ("tile", 0, 3): [("e", 1)],
    ("tile", 0, 4): [("f1", 0)],
    ("tile", 0, 5): [("f0", 0), ("f2", 1)],
    ("tile", 0, 6): [("e", 2)],
    ("tile", 0, 7): [("f1", 1)],
    ("fin", 0, 0): [("f2", 2), ("f3", 0)],
    ("fin", 0, 1): [("f1", 2)],
    ("tile", 1, 0): [("f0", 1)],
    ("tile", 1, 1): [("e", 3), ("f3", 1)],
    ("tile", 1, 2): [("f1", 3)],
    ("tile", 1, 3): [("f0", 2), ("q00", 0)],
    ("tile", 1, 4): [("f2", 3), ("f3", 2)],
    ("tile", 1, 5): [("f1", 4)],
    ("tile", 1, 6): [("f0", 3)],
    ("tile", 1, 7): [("f1", 5), ("q00", 1)],
    ("fin", 1, 0): [("f2", 4), ("f3", 3)],
    ("fin", 1, 1): [("f0", 4), ("q10", 0), ("q11", 0), ("f1", 6), ("q12", 0), ("q00", 2)],
    ("epi", 0, 0): [("f2", 5), ("f3", 4), ("q00", 3)],
    ("epi", 1, 0): [("f0", 5), ("q10", 1), ("q11", 1), ("q12", 1), ("f2", 6), ("f3", 5), ("l", 0), ("q00", 4), ("q10", 2), ("f0", 6), ("q11", 2), ("q10", 3), ("q12", 2), ("q11", 3), ("q12", 3), ("f3", 6), ("l", 1), ("q00", 5), ("q10", 4), ("q11", 4), ("q12", 4), ("l", 2), ("q10", 5), ("q11", 5), ("q12", 5), ("q00", 6), ("q10", 6), ("l", 3), ("q11", 6), ("q12", 6)],
}


def back_kernel(
    n_grp, lengths, qt, k, kt, v, ot0, ot1, lse0, lse1, cos_t, sin_t, early_in, scale_rows,
    grads_in, mixed_hbm, packed_hbm, wq_hbm, wk_hbm, wv_hbm, frames_hbm, middle_hbm, mod_hbm,
    frames_grad, packed_out, qg0, qg1, early_out, late_out, embed_out,
    grad_t, row_dots, dqt, dkt, dvt, nat_ref, rolled, mixed, packed, weights, frames, middle,
    landing, dw, send_d, got_d, early_got, late_got, summed_q, q_extra,
    send_sem, recv_sem, load_sem,
):
    my_row, my_grp = lax.axis_index("row"), lax.axis_index("grp")
    total = k.shape[0]
    block = total // 4
    steps = total // TILE
    half = HEAD_DIM // 2
    _, starts, ends, offset = layout_of(lengths)
    bits = bits_of(n_grp)
    extra = bits[3:]
    side = lambda bit: (my_grp // bit) % 2
    by_row = lambda j: {"row": my_row ^ j}
    by_grp = lambda bit: {"grp": my_grp ^ bit}
    q_out = (qg0, qg1)

    chains, numbers, started = {}, {}, []

    def copies_of(name, step):
        out = []
        for index, (src, dst, device) in enumerate(chains[name][step][0]()):
            number = numbers.setdefault((name, step, index), len(numbers))
            out.append(
                pltpu.make_async_remote_copy(
                    src, dst, send_sem.at[number], recv_sem.at[number],
                    device_id=device, device_id_type=MESH,
                )
            )
        return out

    def start(name, step=0):
        started.append((name, step))
        for copy in copies_of(name, step):
            copy.start()

    def advance(name, step):
        for copy in copies_of(name, step):
            copy.wait_recv()
        chains[name][step][1]()
        if step + 1 < len(chains[name]):
            start(name, step + 1)

    def run_hook(mark):
        for name, step in HOOKS.get(mark, ()):
            advance(name, step)

    def one_step(number, src, dst, device):
        copy = pltpu.make_async_remote_copy(
            src, dst, send_sem.at[number], recv_sem.at[number], device_id=device, device_id_type=MESH
        )
        copy.start()
        copy.wait()

    def away(region, bit):
        offset, size = region
        return pl.ds(pl.multiple_of(offset + (1 - side(bit)) * (size // 2), 16), size // 2)

    def kept(region, bit):
        offset, size = region
        return (offset + side(bit) * (size // 2), size // 2)

    def at(region):
        return pl.ds(pl.multiple_of(region[0], 16), region[1])

    nothing = lambda: None

    def feed_chain(name, region, order, land):
        chain, areas, shards = [], [], (1, 0)
        for op in order:
            source = packed if chain else packed_hbm
            if op == "x":

                def parts(region=region, land=land, source=source):
                    return [(source.at[1, at(region)], landing.at[pl.ds(land, region[1])], by_row(2))]

                def take(region=region, land=land):
                    got = landing[land : land + region[1]]
                    packed[0, at(region)] = add_low(packed[0, at(region)], got)

                shards, land = (0,), land + region[1]
            else:
                size = region[1] // 2

                def parts(region=region, land=land, source=source, shards=shards, size=size, op=op):
                    return [
                        (
                            source.at[shard, away(region, op)],
                            landing.at[pl.ds(land + i * size, size)],
                            by_grp(op),
                        )
                        for i, shard in enumerate(shards)
                    ]

                region = kept(region, op)

                def take(region=region, land=land, shards=shards, size=size):
                    for i, shard in enumerate(shards):
                        got = landing[land + i * size : land + (i + 1) * size]
                        packed[shard, at(region)] = add_low(packed[shard, at(region)], got)

                land += size * len(shards)
                areas.append((op, region))
            chain.append((parts, take))
        last = chain[-1][1]

        def own():
            last()
            for i, bit in enumerate(extra):
                first, size = land + i * region[1], region[1]
                number = numbers.setdefault((name, "extra", i), len(numbers))
                one_step(number, packed.at[0, at(region)], landing.at[pl.ds(first, size)], by_grp(bit))
                packed[0, at(region)] = add_low(packed[0, at(region)], landing[first : first + size])
            packed_out[at(region)] = packed[0, at(region)]

        chain[-1] = (chain[-1][0], own)
        for bit, area in reversed(areas):
            chain.append(
                (
                    lambda bit=bit, area=area: [
                        (packed_out.at[at(area)], packed_out.at[at(area)], by_grp(bit))
                    ],
                    nothing,
                )
            )
        chains[name] = chain
        return land + len(extra) * region[1]

    def heads_chain(name, pair, number, lanes, order):
        chain, areas, region = [], [], (0, 256)
        for bit in order:
            size = region[1] // 2
            land = slice(256 - region[1], 256 - size)

            def parts(region=region, bit=bit, land=land):
                return [
                    (
                        dw.at[pair, :, away(region, bit), lanes],
                        summed_q.at[pair, :, pl.ds(land.start, land.stop - land.start), lanes],
                        by_grp(bit),
                    )
                ]

            region = kept(region, bit)

            def take(region=region, land=land):
                mine = at(region)
                dw[pair, :, mine, lanes] = add_low(
                    dw[pair, :, mine, lanes], summed_q[pair, :, land, lanes]
                )

            areas.append((bit, region))
            chain.append((parts, take))
        last, part = chain[-1][1], region

        def own():
            last()
            for i, bit in enumerate(extra):
                slot = 4 * (pair * len(extra) + i)
                count = numbers.setdefault((name, "extra", i), len(numbers))
                one_step(
                    count, dw.at[pair, :, at(part), lanes], q_extra.at[pl.ds(slot, 4), :, lanes],
                    by_grp(bit),
                )
                dw[pair, :, at(part), lanes] = add_low(
                    dw[pair, :, at(part), lanes], q_extra[slot : slot + 4, :, lanes]
                )
            q_out[pair][0, at(part), lanes] = dw[pair, my_row, at(part), lanes]

        chain[-1] = (chain[-1][0], own)
        chain.append(
            (
                lambda: [
                    (
                        dw.at[pair, my_row ^ j, at(part), lanes],
                        q_out[pair].at[j, at(part), lanes],
                        by_row(j),
                    )
                    for j in (1, 2, 3)
                ],
                nothing,
            )
        )
        for bit, area in reversed(areas):
            spot = lambda area=area: q_out[pair].at[:, at(area), lanes]
            chain.append((lambda bit=bit, spot=spot: [(spot(), spot(), by_grp(bit))], nothing))
        chains[name] = chain

    def gather_chain(name, got, out, finish):
        def first():
            out[0] = finish((got[0] + got[1]) + (got[2] + got[3]))

        chain = [(lambda: [(got.at[my_row], got.at[my_row], by_row(j)) for j in (1, 2, 3)], first)]
        for i, bit in enumerate(bits):
            chain.append(
                (
                    lambda i=i, bit=bit: [
                        (out.at[pl.ds(0, 1 << i)], out.at[pl.ds(1 << i, 1 << i)], by_grp(bit))
                    ],
                    nothing,
                )
            )
        chains[name] = chain

    def fold(sums):
        width = sums.shape[1] // 2
        return jnp.concatenate([sums[:, :width], sums[:, width:]], 0).astype(BF)

    loads = [
        pltpu.make_async_copy(src, dst, load_sem.at[i])
        for i, (src, dst) in enumerate(
            (
                (packed_hbm, packed),
                (mixed_hbm, mixed),
                (wq_hbm, mixed.at[pl.ds(0, D)]),
                (wk_hbm, mixed.at[pl.ds(D, D)]),
                (wv_hbm, weights),
                (frames_hbm, frames),
                (middle_hbm, middle),
            )
        )
    ]
    for load in loads[:1] + loads[4:]:
        load.start()

    barrier = pltpu.get_barrier_semaphore()
    for device in [by_row(j) for j in (1, 2, 3)] + [by_grp(bit) for bit in bits]:
        pl.semaphore_signal(barrier, inc=1, device_id=device, device_id_type=MESH)
    pl.semaphore_wait(barrier, 3 + len(bits))

    gather_chain("e", early_got, early_out, fold)
    early_got[my_row] = early_in[...]
    start("e")
    land, first_row = 0, 0
    for number, (count, order) in enumerate(FEED_PIECES):
        land = feed_chain(f"f{number}", (first_row, count), order, land)
        first_row += count
        start(f"f{number}")

    lanes_of = slice(0, 256)
    for j in range(4):
        mixed[pl.ds(pl.multiple_of((my_row ^ j) * block, block), block), lanes_of] = grads_in[j]
    ahead = roll_matrix(offset)

    def turn(i, carry):
        cols = pl.ds(pl.multiple_of(i * TILE, TILE), TILE)
        after = pl.ds(pl.multiple_of((i + 1) % steps * TILE, TILE), TILE)
        part = matdot(ahead[:, :TILE], mixed[cols, lanes_of], 1, 0)
        part = (part + matdot(ahead[:, TILE:], mixed[after, lanes_of], 1, 0)).T
        grad_t[:, cols] = part.astype(BF)
        for head in range(4):
            mine = slice((head % 2) * HEAD_DIM, (head % 2 + 1) * HEAD_DIM)
            crossed = part[head * HEAD_DIM : (head + 1) * HEAD_DIM] * (ot0, ot1)[head // 2][
                mine, cols
            ].astype(F32)
            row_dots[head : head + 1, cols] = jnp.sum(crossed, axis=0, keepdims=True)
        return carry

    lax.fori_loop(0, steps, turn, 0)
    loads[1].start()
    loads[0].wait()

    def run(pair, here, spans, allowed):
        lanes = slice(pair * 128, (pair + 1) * 128)
        lse = (lse0, lse1)[pair]
        for head in range(2):
            mine = slice(head * HEAD_DIM, (head + 1) * HEAD_DIM)
            wide = slice(pair * 128 + head * HEAD_DIM, pair * 128 + (head + 1) * HEAD_DIM)
            dots = slice(2 * pair + head, 2 * pair + head + 1)
            grad_query = None
            for first, count in spans:
                keys = pl.ds(first, count)
                scores = matdot(k[keys, lanes], one_head(qt[lanes, here], head), 1, 0)
                if allowed is not None:
                    scores = jnp.where(allowed, scores, -1e30)
                probs = jnp.exp(scores - lse[head : head + 1, here])
                grad_probs = matdot(v[keys, lanes], one_head(grad_t[lanes, here], head), 1, 0)
                grad_scores = (probs * (grad_probs - row_dots[dots, here])).astype(BF)
                part = matdot(kt[wide, keys], grad_scores, 1, 0)
                grad_query = part if grad_query is None else grad_query + part
                dkt[mine, keys] += matdot(qt[wide, here], grad_scores, 1, 1)
                dvt[mine, keys] += matdot(grad_t[wide, here], probs.astype(BF), 1, 1)
            dqt[mine, here] = grad_query * HEAD_DIM**-0.5

    def finish(pair):
        def part(i, sums):
            cols = pl.ds(pl.multiple_of(i * TILE, TILE), TILE)
            cosine, sine = cos_t[:, cols], sin_t[:, cols]

            def turned(ref):
                parts = []
                for at_row in range(0, 128, HEAD_DIM):
                    first = ref[at_row : at_row + half, cols]
                    second = ref[at_row + half : at_row + HEAD_DIM, cols]
                    parts.append(first * cosine + second * sine)
                    parts.append(second * cosine - first * sine)
                return jnp.concatenate(parts, 0)

            columns = jnp.concatenate([turned(dqt), turned(dkt), dvt[:, cols]], 0)
            nat_ref[:, pl.ds(pl.multiple_of(TILE + i * TILE, TILE), TILE)] = columns.astype(BF)
            low = columns.T.astype(BF)
            rolled[cols, :] = low
            return sums + jnp.sum(low.astype(F32), axis=0, keepdims=True)

        sums = lax.fori_loop(0, steps, part, jnp.zeros((1, 384), F32))
        if pair == 1:
            for copy in copies_of("d0", 0):
                copy.wait_send()
        unroll(
            [got_d.at[my_row, pair]] + [send_d.at[j] for j in range(3)], nat_ref, my_row, offset, block
        )
        chains[f"d{pair}"] = [
            (
                lambda: [(send_d.at[j - 1], got_d.at[my_row, pair], by_row(j)) for j in (1, 2, 3)],
                nothing,
            )
        ]
        start(f"d{pair}")
        run_hook(("fin", pair, 0))
        if pair == 0:
            loads[1].wait()
        for shard in range(4):
            columns = mixed[:, shard * 256 : (shard + 1) * 256]
            dw[pair, shard] = contract_rows(columns, rolled[...]).astype(BF)
        lane = 0
        for number, (count, order) in enumerate(HEAD_PIECES[pair]):
            heads_chain(f"q{pair}{number}", pair, number, pl.ds(lane, count), order)
            start(f"q{pair}{number}")
            lane += count
        return sums

    bias_sums = []
    for pair in range(2):
        dkt[...] = jnp.zeros_like(dkt)
        dvt[...] = jnp.zeros_like(dvt)

        def tile(i, carry):
            run(pair, pl.ds(pl.multiple_of(i * TILE, TILE), TILE), BACK_SPANS, None)
            for when in range(steps - 1):
                if ("tile", pair, when) in HOOKS:
                    pl.when(i == when)(functools.partial(run_hook, ("tile", pair, when)))
            return carry

        lax.fori_loop(0, steps - 1, tile, 0)
        tail = total - LONGEST
        run(pair, pl.ds(LONGEST, tail), [(LONGEST, tail)], tail_allowed(ends, offset, total))
        run_hook(("tile", pair, steps - 1))
        bias_sums.append(finish(pair))
        if pair == 1:
            for load in loads[2:4]:
                load.start()
        run_hook(("fin", pair, 1))

    for pair in range(2):
        advance(f"d{pair}", 0)
    for load in loads[2:]:
        load.wait()
    late = [jnp.zeros((1, 2 * D), F32) for _ in range(4)]
    for part in range(block // TILE):
        rows = slice(part * TILE, (part + 1) * TILE)
        grad = jnp.zeros((TILE, D), F32)
        for kind in range(3):
            pieces = [
                got_d[owner, pair, rows, kind * 128 : (kind + 1) * 128]
                for owner in range(4)
                for pair in range(2)
            ]
            weight = weights[...] if kind == 2 else mixed[kind * D : (kind + 1) * D]
            grad = grad + against(jnp.concatenate(pieces, 1), weight)
        normed, factor = normalize(frames[rows, :].astype(F32))
        spots = my_row * block + part * TILE + lax.broadcasted_iota(jnp.int32, (TILE, 1), 0)
        marks = marks_of(spots, starts, ends)
        scale = jnp.ones((TILE, D), F32)
        for u in range(4):
            scale = scale + marks[u] * scale_rows[u : u + 1, D : 2 * D]
        back = normalize_back(grad * scale, normed, factor)
        frames_grad[rows, :] = (middle[rows, :] + back).astype(BF)
        for u in range(4):
            mark = marks[u]
            late[u] += jnp.concatenate(
                [jnp.sum(t * mark, axis=0, keepdims=True) for t in (grad, grad * normed)], 1
            )
        if part == 0:
            run_hook(("epi", 0, 0))

    widths = [slice(kind * 128, (kind + 1) * 128) for kind in range(3)]
    bias_row = jnp.concatenate(
        [bias_sums[pair][:, w] for w in widths for pair in range(2)]
        + [jnp.zeros((1, 2 * D - 768), F32)],
        1,
    )
    index = lax.broadcasted_iota(jnp.int32, (8, 2 * D), 0)
    gather_chain(
        "l", late_got, late_out, lambda sums: fold(jnp.where(index == 4, bias_row, sums))
    )
    late_got[my_row] = jnp.concatenate(late + [jnp.zeros((4, 2 * D), F32)], 0)
    start("l")

    slots = [mixed.at[pl.ds(0, D)], mixed.at[pl.ds(D, D)], weights]
    blocks = [2, 3, 4, 5, 0, 1]
    fetches = [
        pltpu.make_async_copy(
            mod_hbm.at[:, pl.ds(block * D, D)], slots[i % 3], load_sem.at[len(loads) + i % 3]
        )
        for i, block in enumerate(blocks)
    ]
    for fetch in fetches[:3]:
        fetch.start()
    embed_out[...] = jnp.zeros_like(embed_out)

    def embed_step(i):
        block = blocks[i]
        fetches[i].wait()
        if block < 2:
            rows = late_out[0].astype(F32)[8 * block : 8 * block + 8]
        else:
            part, lane = divmod(block - 2, 2)
            rows = early_out[0, :, lane * D : (lane + 1) * D].astype(F32)[8 * part : 8 * part + 8]
        embed_out[...] += against(rows.astype(BF), slots[i % 3][...])
        if i + 3 < len(blocks):
            fetches[i + 3].start()

    done, late_ready = 0, False
    for number, (name, step) in enumerate(HOOKS[("epi", 1, 0)]):
        advance(name, step)
        late_ready = late_ready or (name, step) == ("l", 0)
        if number % 3 == 2 and done < (6 if late_ready else 4):
            embed_step(done)
            done += 1
    for i in range(done, 6):
        embed_step(i)
    for number in range(3, len(bits)):
        advance("e", number + 1)
        advance("l", number + 1)
    for name, step in started:
        if name != "d0":
            for copy in copies_of(name, step):
                copy.wait_send()


def attend_back(
    n_grp, lengths, qt, k, kt, v, heads_t, lse, cos_t, sin_t, early, scale_rows, grads, mixed, packed, weights, frames, middle, mod_weight,
):
    total = k.shape[0]
    block = total // 4
    rows = packed.shape[1]
    extra = max(0, len(bits_of(n_grp)) - 3)
    inputs = [
        qt, k, kt, v, *heads_t, *lse, cos_t, sin_t, early, scale_rows, grads,
    ]
    far = [mixed, packed, *weights, frames, middle, mod_weight]
    copies = 160
    return pl.pallas_call(
        functools.partial(back_kernel, n_grp),
        out_shape=[
            jax.ShapeDtypeStruct((block, D), BF),
            jax.ShapeDtypeStruct((rows, D), BF),
            jax.ShapeDtypeStruct((4, 256, 384), BF),
            jax.ShapeDtypeStruct((4, 256, 384), BF),
            jax.ShapeDtypeStruct((n_grp, 16, 2 * D), BF),
            jax.ShapeDtypeStruct((n_grp, 16, D), BF),
            jax.ShapeDtypeStruct((8, D), F32),
        ],
        in_specs=[pl.BlockSpec(memory_space=SMEM)]
        + [pl.BlockSpec(memory_space=VMEM)] * len(inputs)
        + [pl.BlockSpec(memory_space=pl.ANY)] * len(far),
        out_specs=[pl.BlockSpec(memory_space=VMEM)] * 7,
        scratch_shapes=[
            VMEM((256, total), BF),
            VMEM((8, total), F32),
            VMEM((128, total), F32),
            VMEM((128, total), F32),
            VMEM((128, total), F32),
            VMEM((384, total + TILE), BF),
            VMEM((total, 384), BF),
            VMEM((total, D), BF),
            VMEM((2, rows, D), BF),
            VMEM((D, D), BF),
            VMEM((block, D), BF),
            VMEM((block, D), F32),
            VMEM((rows * (15 + extra) // 8, D), BF),
            VMEM((2, 4, 256, 384), BF),
            VMEM((3, block, 384), BF),
            VMEM((4, 2, block, 384), BF),
            VMEM((4, 8, 4 * D), F32),
            VMEM((4, 8, 2 * D), F32),
            VMEM((2, 4, 256, 384), BF),
            VMEM((max(1, 8 * extra), 32, 384), BF),
            pltpu.SemaphoreType.DMA((copies,)),
            pltpu.SemaphoreType.DMA((copies,)),
            pltpu.SemaphoreType.DMA((len(far) + 3,)),
        ],
        compiler_params=pltpu.CompilerParams(
            vmem_limit_bytes=62 << 20, collective_id=1, has_side_effects=True
        ),
        cost_estimate=pl.CostEstimate(
            flops=4 * 2 * 5 * total * LONGEST * 256,
            bytes_accessed=40 << 20,
            transcendentals=4 * total * LONGEST,
        ),
        name="attend_back",
    )(lengths, *inputs, *far)


def feed_kernel(
    lengths, o, frames, cot, mod, act, out_bias, up_bias, down_bias, out_hbm, up_hbm, down_hbm,
    output, middle_out, grads_out, packed, early_out,
    w_out, w_up, w_down, h_s, a_s, ez_s, eb_s, ea_s, send_o, send_w, got_w, load_sem, send_sem, recv_sem,
):
    my_row = lax.axis_index("row")
    by_row = lambda j: {"row": my_row ^ j}
    rows_all = frames.shape[0]
    _, starts, ends, _ = layout_of(lengths)
    width = D // 4
    loads = [
        pltpu.make_async_copy(
            out_hbm.at[pl.ds(pl.multiple_of((my_row ^ j) * width, width), width)],
            w_out.at[pl.ds(j * width, width)],
            load_sem.at[j],
        )
        for j in range(4)
    ] + [
        pltpu.make_async_copy(up_hbm, w_up, load_sem.at[4]),
        pltpu.make_async_copy(down_hbm, w_down, load_sem.at[5]),
    ]
    for load in loads:
        load.start()
    barrier = pltpu.get_barrier_semaphore()
    for j in (1, 2, 3):
        pl.semaphore_signal(barrier, inc=1, device_id=by_row(j), device_id_type=MESH)
    pl.semaphore_wait(barrier, 3)

    def remote(number, src, dst, j):
        return pltpu.make_async_remote_copy(
            src, dst, send_sem.at[number], recv_sem.at[number], device_id=by_row(j), device_id_type=MESH
        )

    copies = []
    coef = math.sqrt(2.0 / math.pi)
    sums = [[jnp.zeros((1, D), F32) for _ in range(4)] for _ in range(4)]
    bias_sums = [jnp.zeros((1, n), F32) for n in (D, 2 * D, D)]
    for tile in range(rows_all // TILE):
        rows = slice(tile * TILE, (tile + 1) * TILE)
        spots = my_row * rows_all + tile * TILE + lax.broadcasted_iota(jnp.int32, (TILE, 1), 0)
        marks = marks_of(spots, starts, ends)

        def per_row(block):
            total = marks[0] * mod[0:1, block * D : (block + 1) * D]
            for u in range(1, 4):
                total = total + marks[u] * mod[u : u + 1, block * D : (block + 1) * D]
            return total

        gate_a, shift_f, scale_f, gate_f = per_row(2), per_row(3), 1.0 + per_row(4), per_row(5)
        if tile == 0:
            for load in loads[:4]:
                load.wait()
        heads = jnp.concatenate([o[j, rows, :] for j in range(4)], 1)
        attended = matdot(heads, w_out[...], 1, 0) + out_bias[...]
        middle = frames[rows, :].astype(F32) + gate_a * attended
        normed, factor = normalize(middle)
        h = (normed * scale_f + shift_f).astype(BF)
        h_s[rows, :] = h
        if tile == 0:
            loads[4].wait()
        z = matdot(h, w_up[...], 1, 0) + up_bias[...]
        square = z * z
        curve = jnp.tanh(coef * (z * (1.0 + 0.044715 * square)))
        share = 0.5 * (1.0 + curve)
        a = (z * share).astype(BF)
        a_s[rows, :] = a
        slope = share + (0.5 * coef) * z * (1.0 - curve * curve) * (1.0 + (3 * 0.044715) * square)
        if tile == 0:
            loads[5].wait()
        branch = matdot(a, w_down[...], 1, 0) + down_bias[...]
        output[rows, :] = (middle + gate_f * branch).astype(BF)
        upstream = cot[rows, :].astype(F32)
        e_b = (upstream * gate_f).astype(BF)
        eb_s[rows, :] = e_b
        e_z = (against(e_b, w_down[...]) * slope).astype(BF)
        ez_s[rows, :] = e_z
        e_h = against(e_z, w_up[...])
        e_mid = upstream + normalize_back(e_h * scale_f, normed, factor)
        middle_out[rows, :] = e_mid
        e_att = (e_mid * gate_a).astype(BF)
        ea_s[rows, :] = e_att
        e_o = against(e_att, w_out[...]).astype(BF)
        grads_out[0, rows, :] = e_o[:, :width]
        for j in (1, 2, 3):
            send_o[j - 1, rows, :] = e_o[:, j * width : (j + 1) * width]
            copies.append(
                remote(
                    len(copies), send_o.at[j - 1, pl.ds(tile * TILE, TILE)],
                    grads_out.at[j, pl.ds(tile * TILE, TILE)], j,
                )
            )
            copies[-1].start()
        for block, part in enumerate((e_mid * attended, e_h, e_h * normed, upstream * branch)):
            for u in range(4):
                sums[u][block] += jnp.sum(part * marks[u], axis=0, keepdims=True)
        for number, part in enumerate((e_att, e_z, e_b)):
            bias_sums[number] += jnp.sum(part.astype(F32), axis=0, keepdims=True)

    early_out[...] = jnp.concatenate(
        [jnp.concatenate(row, 1) for row in sums + [bias_sums]]
        + [act[...] * 0.25, jnp.zeros((2, 4 * D), F32)],
        0,
    )

    def shard(j, store):
        owner = my_row ^ j
        columns = pl.ds(pl.multiple_of(owner * 2 * width, 2 * width), 2 * width)
        store(768, contract_rows(a_s[:, columns], eb_s[...]))
        columns = pl.ds(pl.multiple_of(owner * width, width), width)
        store(256, contract_rows(h_s[:, columns], ez_s[:, :D]))
        store(512, contract_rows(h_s[:, columns], ez_s[:, D:]))
        store(0, contract_rows(o[j], ea_s[...]))

    for slot, j in enumerate((1, 3)):

        def store(first, value):
            send_w[slot, first : first + value.shape[0], :] = value.astype(BF)

        shard(j, store)
        copies.append(remote(len(copies), send_w.at[slot], got_w.at[slot], 1))
        copies[-1].start()
    for slot, j in enumerate((0, 2)):

        def store(first, value):
            packed[slot, first : first + value.shape[0], :] = value.astype(BF)

        shard(j, store)
    for slot in range(2):
        copies[-2 + slot].wait_recv()
        packed[slot] = add_low(packed[slot], got_w[slot])
    for copy in copies[:-2]:
        copy.wait_recv()
    for copy in copies:
        copy.wait_send()


def feed(lengths, o, frames, cot, mod, act, biases, weights):
    rows = frames.shape[0]
    inputs = [o, frames, cot, mod, act, *[b[None] for b in biases]]
    return pl.pallas_call(
        feed_kernel,
        out_shape=[
            jax.ShapeDtypeStruct((rows, D), BF),
            jax.ShapeDtypeStruct((rows, D), F32),
            jax.ShapeDtypeStruct((4, rows, D // 4), BF),
            jax.ShapeDtypeStruct((2, 1280, D), BF),
            jax.ShapeDtypeStruct((8, 4 * D), F32),
        ],
        in_specs=[pl.BlockSpec(memory_space=SMEM)]
        + [pl.BlockSpec(memory_space=VMEM)] * len(inputs)
        + [pl.BlockSpec(memory_space=pl.ANY)] * 3,
        out_specs=[pl.BlockSpec(memory_space=VMEM)] * 5,
        scratch_shapes=[
            VMEM((D, D), BF),
            VMEM((D, 2 * D), BF),
            VMEM((2 * D, D), BF),
            VMEM((rows, D), BF),
            VMEM((rows, 2 * D), BF),
            VMEM((rows, 2 * D), BF),
            VMEM((rows, D), BF),
            VMEM((rows, D), BF),
            VMEM((3, rows, D // 4), BF),
            VMEM((2, 1280, D), BF),
            VMEM((2, 1280, D), BF),
            pltpu.SemaphoreType.DMA((6,)),
            pltpu.SemaphoreType.DMA((3 * rows // TILE + 2,)),
            pltpu.SemaphoreType.DMA((3 * rows // TILE + 2,)),
        ],
        compiler_params=pltpu.CompilerParams(
            vmem_limit_bytes=LIMIT, collective_id=2, has_side_effects=True
        ),
        cost_estimate=pl.CostEstimate(
            flops=2 * rows * D * 15 * D, bytes_accessed=30 << 20, transcendentals=rows * 2 * D
        ),
        name="feed",
    )(lengths, *inputs, *weights)


def outputs_kernel(
    packed, heads_0, heads_1, early, late, embedding, embed_in,
    out_far, up_far, down_far, query_far, key_far, value_far, mod_far,
    mod_b, embed, out_b, up_b, down_b, query_b, key_b, value_b,
    out_w, up_w, down_w, query_w, key_w, value_w, mod_w, rows_ref, mod_ref, store_sem,
):
    my_row = lax.axis_index("row")
    width = D // 4
    stores = []

    def store(src, dst):
        stores.append(pltpu.make_async_copy(src, dst, store_sem.at[len(stores)]))
        stores[-1].start()

    n_grp = early.shape[0]
    out_w[...] = packed[:width].astype(F32)
    up_w[:, :D] = packed[width : 2 * width].astype(F32)
    up_w[:, D:] = packed[2 * width : 3 * width].astype(F32)
    store(out_w, out_far)
    store(up_w, up_far)
    down_w[...] = packed[3 * width :].astype(F32)
    store(down_w, down_far)
    for pair, heads in enumerate((heads_0, heads_1)):
        for j in range(4):
            lanes = pl.ds(pl.multiple_of((my_row ^ j) * width + pair * 128, 128), 128)
            for kind, out in enumerate((query_w, key_w, value_w)):
                out[:, lanes] = heads[j, :, kind * 128 : (kind + 1) * 128].astype(F32)
    store(query_w, query_far)
    store(key_w, key_far)
    store(value_w, value_far)
    for first, source, count in ((0, late, D), (2 * D, early, 2 * D)):
        for part in range(2):
            rows = source[:, 8 * part : 8 * part + 8].astype(F32).reshape(n_grp * 8, count)
            mod_ref[:, first + part * count : first + (part + 1) * count] = rows
    number = lax.broadcasted_iota(jnp.int32, (n_grp * 8, 1), 0) % 8
    utterance, bias = (number < 4).astype(F32), (number == 4).astype(F32)
    act = jnp.zeros((n_grp * 8, width), F32)
    for u in range(4):
        lanes = pl.ds(pl.multiple_of((2 + u) * D + my_row * width, width), width)
        moved = pltpu.roll(mod_ref[:, lanes], (u - 5) % (n_grp * 8), 0)
        act = jnp.where(number == u, moved, act)
    act = act.astype(BF)
    for block in range(6):
        lanes = slice(block * D, (block + 1) * D)
        rows = mod_ref[:, lanes]
        mod_w[:, lanes] = contract_rows(act, rows.astype(BF))
        store(mod_w.at[:, pl.ds(block * D, D)], mod_far.at[:, pl.ds(block * D, D)])
        sums = [jnp.sum(rows * mark, axis=0, keepdims=True) for mark in (utterance, bias)]
        rows_ref[:, lanes] = jnp.concatenate(sums + [jnp.zeros((6, D), F32)], 0)

    def own(row, first, size):
        lanes = pl.ds(pl.multiple_of(first + my_row * size, 128), size)
        return rows_ref[row : row + 1, lanes]

    mod_b[...] = own(0, 0, 6 * width)
    for i, out in enumerate((query_b, key_b, value_b)):
        out[...] = rows_ref[1:2, i * width : (i + 1) * width]
    out_b[...] = own(1, 2 * D, width)
    up_b[...] = own(1, 3 * D, 2 * width)
    down_b[...] = own(1, 5 * D, width)
    gate = 1.0 / (1.0 + jnp.exp(-embedding[...]))
    embed[...] = embed_in[:4] * (gate * (1.0 + embedding[...] * (1.0 - gate)))
    for copy in stores:
        copy.wait()


def outputs(packed, heads_0, heads_1, early, late, embedding, embed_in):
    width = D // 4
    n_grp = early.shape[0]
    shapes = [(width, D), (width, 2 * D), (2 * width, D)] + [(width, D)] * 3 + [(width, 6 * D)]
    shapes += [(1, 6 * width), (4, D)] + [(1, n) for n in (width, 2 * width, width, width, width, width)]
    return pl.pallas_call(
        outputs_kernel,
        out_shape=[jax.ShapeDtypeStruct(shape, F32) for shape in shapes],
        in_specs=[pl.BlockSpec(memory_space=VMEM)] * 7,
        out_specs=[pl.BlockSpec(memory_space=pl.ANY)] * 7
        + [pl.BlockSpec(memory_space=VMEM)] * (len(shapes) - 7),
        scratch_shapes=[VMEM(shape, F32) for shape in shapes[:7]]
        + [
            VMEM((8, 6 * D), F32),
            VMEM((n_grp * 8, 6 * D), F32),
            pltpu.SemaphoreType.DMA((12,)),
        ],
        compiler_params=pltpu.CompilerParams(vmem_limit_bytes=LIMIT),
        name="outputs",
    )(packed, heads_0, heads_1, early, late, embedding, embed_in)


def local(
    frames, time_embed, lengths, mod_weight, mod_bias, query_weight, query_bias, key_weight, key_bias,
    value_weight, value_bias, out_weight, out_bias, up_weight, up_bias, down_weight, down_bias, cotangent,
):
    n_grp = lax.axis_size("grp")
    lengths, embedding = lengths[0], time_embed[0]
    weights = (query_weight, key_weight, value_weight)
    mixed, qt, kt, k_rows, v_rows, cos_t, sin_t, modulation, act, *heads_t, lse_0, lse_1, o_all = front(
        lengths, frames, embedding, mod_weight, mod_bias, weights, (query_bias, key_bias, value_bias)
    )
    output, grad_middle, grad_pieces, packed, early = feed(
        lengths, o_all, frames, cotangent, modulation, act, (out_bias, up_bias, down_bias),
        (out_weight, up_weight, down_weight),
    )
    grad_frames, packed_total, heads_0, heads_1, early_all, late_all, embed_part = attend_back(
        n_grp, lengths, qt, k_rows, kt, v_rows, heads_t, (lse_0, lse_1), cos_t, sin_t, early,
        modulation, grad_pieces, mixed, packed, weights, frames, grad_middle, mod_weight,
    )
    grads = outputs(packed_total, heads_0, heads_1, early_all, late_all, embedding, embed_part)
    out_grad, up_grad, down_grad, query_grad, key_grad, value_grad, mod_weight_grad = grads[:7]
    mod_bias_grad, grad_embedding = grads[7][0], grads[8]
    out_b, up_b, down_b, query_b, key_b, value_b = (b[0] for b in grads[9:])
    return (
        output,
        grad_frames,
        grad_embedding[None],
        mod_weight_grad,
        mod_bias_grad,
        query_grad,
        query_b,
        key_grad,
        key_b,
        value_grad,
        value_b,
        out_grad,
        out_b,
        up_grad,
        up_b,
        down_grad,
        down_b,
    )


def solution(mesh):
    placed = (
        (P(("grp", "row"), None), P("grp", None, None), P("grp", None))
        + (P(),) * 14
        + (P(("grp", "row"), None),)
    )
    return jax.shard_map(
        local,
        mesh=mesh,
        in_specs=placed,
        out_specs=(
            P(("grp", "row"), None),
            P(("grp", "row"), None),
            P("grp", None, None),
        )
        + (P("row", None), P("row")) * 7,
        check_vma=False,
    )
```

```python
import functools
import math

import jax
import jax.numpy as jnp
import numpy as np
from jax import lax
from jax.experimental import pallas as pl
from jax.experimental.pallas import tpu as pltpu
from jax.sharding import PartitionSpec as P

D = 1024
HEADS = 16
HEAD_DIM = 64
LONGEST = 1792
TILE = 256
BF = jnp.bfloat16
F32 = jnp.float32

highest = lax.Precision.HIGHEST
VMEM = pltpu.VMEM
SMEM = pltpu.SMEM
LIMIT = 60 << 20
MESH = pl.DeviceIdType.MESH
BACK_SPANS = [(0, 896), (896, 896)]


def matdot(left, right, left_dim, right_dim):
    return lax.dot_general(
        left, right, (((left_dim,), (right_dim,)), ((), ())), preferred_element_type=F32
    )


def contract_rows(left, right):
    return matdot(left, right, 0, 0)


def against(left, weight):
    return matdot(left, weight, 1, 1)


def column_sum(tensor):
    return jnp.sum(tensor.astype(F32), axis=0)


def normalize(tensor):
    centred = tensor - jnp.mean(tensor, axis=-1, keepdims=True)
    factor = lax.rsqrt(jnp.mean(centred * centred, axis=-1, keepdims=True) + 1e-06)
    return (centred * factor, factor)


def normalize_back(grad_normed, normed, factor):
    mean_grad = jnp.mean(grad_normed, axis=-1, keepdims=True)
    mean_cross = jnp.mean(grad_normed * normed, axis=-1, keepdims=True)
    return (grad_normed - mean_grad - normed * mean_cross) * factor


def exchange(tensor, axis, bit):
    size = lax.axis_size(axis)
    return lax.ppermute(tensor, axis, [(i, i ^ bit) for i in range(size)])


def add_low(left, right):
    return (left.astype(F32) + right.astype(F32)).astype(BF)


def bits_of(count):
    return [1 << i for i in range(count.bit_length() - 1)]


def roll_matrix(offset):
    row = lax.broadcasted_iota(jnp.int32, (TILE, 2 * TILE), 0)
    col = lax.broadcasted_iota(jnp.int32, (TILE, 2 * TILE), 1)
    return (col == row + offset).astype(F32).astype(BF)


def layout_of(lengths):
    sizes = [lengths[u] for u in range(4)]
    starts, finish, at = [], [], 0
    for size in sizes:
        starts.append(at)
        at = at + size
        finish.append(at)
    offset = 0
    for size, first in zip(sizes, starts):
        offset = offset + jnp.where(size == LONGEST, first, 0)
    return sizes, starts, finish, offset


def marks_of(rows, starts, finish):
    return [
        jnp.logical_and(rows >= first, rows < end).astype(F32) for first, end in zip(starts, finish)
    ]


def tail_allowed(finish, offset, total):
    count = total - LONGEST

    def segment(shape, dim):
        rows = LONGEST + offset + lax.broadcasted_iota(jnp.int32, shape, dim)
        rows = jnp.where(rows >= total, rows - total, rows)
        return sum((rows >= end).astype(jnp.int32) for end in finish)

    return segment((count, 1), 0) == segment((1, count), 1)


def front_kernel(
    lengths, embedding, mod_bias, q_bias, k_bias, v_bias, frequency,
    frames_hbm, mod_weight_hbm, wq_hbm, wk_hbm, wv_hbm,
    mixed_far, qt_far, kt_far, k_far, v_far, cos_out, sin_out, mod_out, act_out, ot0, ot1, lse0, lse1, o_all,
    mixed_out, qt_out, kt_out, vt_out, k_out, v_out,
    rows_ref, roll_ref, mod_weight, weight, weight_t, bias_t, rolled_ref, send_o,
    send_sem, recv_sem, load_sem, store_sem, send_o_sem, recv_o_sem,
):
    my_row = lax.axis_index("row")
    block = frames_hbm.shape[0]
    total = 4 * block
    steps = total // TILE
    width = qt_out.shape[0]
    by_row = lambda j: {"row": my_row ^ j}
    sizes, starts, finish, offset = layout_of(lengths)

    piece = TILE

    def place(j, part=0, count=piece):
        first = pl.multiple_of((my_row ^ j) * block + part * piece, piece)
        return pl.ds(first, count)

    def remote(number, src, dst, j):
        return pltpu.make_async_remote_copy(
            src, dst, send_sem.at[number], recv_sem.at[number], device_id=by_row(j), device_id_type=MESH
        )

    parts = block // piece
    barrier = pltpu.get_barrier_semaphore()
    for j in (1, 2, 3):
        pl.semaphore_signal(barrier, inc=1, device_id=by_row(j), device_id_type=MESH)
    pl.semaphore_wait(barrier, 3)
    to_x = [
        remote(i, frames_hbm.at[pl.ds(i * piece, piece)], rows_ref.at[place(0, i)], 2)
        for i in range(parts)
    ]
    to_core = remote(parts, frames_hbm, rows_ref.at[place(0, 0, block)], 1)
    onward = [
        remote(parts + 1 + i, rows_ref.at[place(2, i)], rows_ref.at[place(2, i)], 1) for i in range(parts)
    ]
    for copy in [to_core] + to_x:
        copy.start()
    columns = pl.ds(pl.multiple_of(my_row * width, width), width)
    loads = [
        pltpu.make_async_copy(src, dst, load_sem.at[i])
        for i, (src, dst) in enumerate(
            [(frames_hbm, rows_ref.at[place(0, 0, block)])]
            + [
                (w.at[:, columns], weight.at[:, pl.ds(i * width, width)])
                for i, w in enumerate((wq_hbm, wk_hbm, wv_hbm))
            ]
            + [
                (mod_weight_hbm.at[:, pl.ds(i * 2 * D, 2 * D)], mod_weight.at[i]) for i in range(3)
            ]
        )
    ]
    for load in loads:
        load.start()

    rows = lax.broadcasted_iota(jnp.int32, (1, total), 1) + offset
    rows = jnp.where(rows >= total, rows - total, rows)
    position = rows
    for first, end in zip(starts, finish):
        inside = jnp.logical_and(rows >= first, rows < end)
        position = jnp.where(inside, rows - first, position)
    angles = frequency[...] * position.astype(F32)
    cos_out[...] = jnp.cos(angles)
    sin_out[...] = jnp.sin(angles)
    roll_ref[...] = roll_matrix(offset)
    for i, bias in enumerate((q_bias, k_bias, v_bias)):
        bias_t[i : i + 1, :] = bias[0:1, columns]

    act = (embedding[...] / (1.0 + jnp.exp(-embedding[...]))).astype(BF).astype(F32)
    act_out[...] = jnp.concatenate([act[u : u + 1] for u in range(4)], 1)
    act_low = jnp.concatenate([act, jnp.zeros_like(act)], 0).astype(BF)
    for i in range(3):
        lanes = slice(i * 2 * D, (i + 1) * 2 * D)
        loads[4 + i].wait()
        mod_out[:, lanes] = matdot(act_low, mod_weight[i], 1, 0) + mod_bias[:, lanes]
    for load in loads[:4]:
        load.wait()
    for i in range(3):
        lanes = slice(i * width, (i + 1) * width)
        weight_t[lanes, :] = weight[:, lanes].T
    biases = jnp.concatenate([bias_t[i : i + 1, :] for i in range(3)], 1)
    biases = jnp.broadcast_to(biases, (8, 3 * width)).T[:, 0:1]

    mod_long = jnp.zeros((1, 2 * D), F32)
    for u in range(4):
        mod_long = mod_long + jnp.where(sizes[u] == LONGEST, 1.0, 0.0) * mod_out[u : u + 1, : 2 * D]
    half = HEAD_DIM // 2

    def tile(step, tail=False):
        here = pl.ds(pl.multiple_of(step * TILE, TILE), TILE)
        if tail:
            moved = matdot(roll_ref[:, :TILE], rows_ref[here, :], 1, 0)
            normed, _ = normalize(moved + matdot(roll_ref[:, TILE:], rows_ref[:TILE, :], 1, 0))
            spots = LONGEST + offset + lax.broadcasted_iota(jnp.int32, (TILE, 1), 0)
            spots = jnp.where(spots >= total, spots - total, spots)
            per_row = jnp.zeros((TILE, 2 * D), F32)
            for u, mark in enumerate(marks_of(spots, starts, finish)):
                per_row = per_row + mark * mod_out[u : u + 1, : 2 * D]
        else:
            both = pl.ds(pl.multiple_of(step * TILE, TILE), 2 * TILE)
            normed, _ = normalize(matdot(roll_ref[...], rows_ref[both, :], 1, 0))
            per_row = mod_long
        mixed_out[here, :] = (normed * (1.0 + per_row[:, D:]) + per_row[:, :D]).astype(BF)
        wide = matdot(weight_t[...], mixed_out[here, :], 1, 1) + biases
        cosine, sine = cos_out[:, here], sin_out[:, here]

        def turned(base):
            out = []
            for at in range(base, base + width, HEAD_DIM):
                first, second = wide[at : at + half], wide[at + half : at + HEAD_DIM]
                out.append(first * cosine - second * sine)
                out.append(second * cosine + first * sine)
            return jnp.concatenate(out, 0)

        keys = turned(width)
        values = wide[2 * width :]
        qt_out[:, here] = turned(0).astype(BF) * jnp.asarray(HEAD_DIM**-0.5, BF)
        kt_out[:, here] = keys.astype(BF)
        vt_out[:, here] = values.astype(BF)
        k_out[here, :] = keys.T.astype(BF)
        v_out[here, :] = values.T.astype(BF)

    to_core.wait_recv()
    chip = my_row // 2

    def near(i, carry):
        tile(chip * (steps // 2) + i)
        return carry

    def far(i, carry):
        tile((1 - chip) * (steps // 2 - 1) + i)
        return carry

    lax.fori_loop(0, steps // 2 - 1, near, 0)
    for arrived, copy in zip(to_x, onward):
        arrived.wait_recv()
        copy.start()
    for copy in onward:
        copy.wait_recv()
    lax.fori_loop(0, steps // 2, far, 0)
    tile(steps - 1, True)
    stores = [
        pltpu.make_async_copy(src, dst, store_sem.at[i])
        for i, (src, dst) in enumerate(
            (
                (mixed_out, mixed_far),
                (qt_out, qt_far),
                (kt_out, kt_far),
                (k_out, k_far),
                (v_out, v_far),
            )
        )
    ]
    for copy in stores:
        copy.start()
    attend_part(
        finish, offset, qt_out, k_out, vt_out, ot0, ot1, lse0, lse1, o_all, rolled_ref, send_o,
        send_o_sem, recv_o_sem,
    )
    for copy in to_x + [to_core] + onward:
        copy.wait_send()
    for copy in stores:
        copy.wait()


def front(lengths, frames, embedding, mod_weight, mod_bias, weights, biases):
    block = frames.shape[0]
    total = 4 * block
    width = D // 4
    half = HEAD_DIM // 2
    frequency = np.exp(np.arange(half) * (-2.0 * math.log(10000.0) / HEAD_DIM)).astype(np.float32)
    inputs = [embedding, mod_bias[None], *[b[None] for b in biases], jnp.asarray(frequency)[:, None]]
    far = [frames, mod_weight, *weights]
    copies = 1 + 2 * (block // TILE)
    wide, tall = (width, total), (total, width)
    stored = [(total, D), wide, wide, tall, tall]
    return pl.pallas_call(
        front_kernel,
        out_shape=[jax.ShapeDtypeStruct(shape, BF) for shape in stored]
        + [
            jax.ShapeDtypeStruct((half, total), F32),
            jax.ShapeDtypeStruct((half, total), F32),
            jax.ShapeDtypeStruct((8, 6 * D), F32),
            jax.ShapeDtypeStruct((1, 4 * D), F32),
        ]
        + [jax.ShapeDtypeStruct((128, total), BF)] * 2
        + [jax.ShapeDtypeStruct((8, total), F32)] * 2
        + [jax.ShapeDtypeStruct((4, block, 256), BF)],
        in_specs=[pl.BlockSpec(memory_space=SMEM)]
        + [pl.BlockSpec(memory_space=VMEM)] * len(inputs)
        + [pl.BlockSpec(memory_space=pl.ANY)] * len(far),
        out_specs=[pl.BlockSpec(memory_space=pl.ANY)] * 5 + [pl.BlockSpec(memory_space=VMEM)] * 9,
        scratch_shapes=[VMEM(shape, BF) for shape in [(total, D), wide, wide, wide, tall, tall]]
        + [
            VMEM((total, D), BF),
            VMEM((TILE, 2 * TILE), BF),
            VMEM((3, D, 2 * D), BF),
            VMEM((D, 3 * width), BF),
            VMEM((3 * width, D), BF),
            VMEM((8, width), F32),
            VMEM((128, total + TILE), BF),
            VMEM((6, block, 128), BF),
            pltpu.SemaphoreType.DMA((copies,)),
            pltpu.SemaphoreType.DMA((copies,)),
            pltpu.SemaphoreType.DMA((7,)),
            pltpu.SemaphoreType.DMA((5,)),
            pltpu.SemaphoreType.DMA((6,)),
            pltpu.SemaphoreType.DMA((6,)),
        ],
        compiler_params=pltpu.CompilerParams(
            vmem_limit_bytes=LIMIT, collective_id=4, has_side_effects=True
        ),
        cost_estimate=pl.CostEstimate(
            flops=2 * total * D * 3 * width + 2 * 2 * 6 * total * LONGEST * 256,
            bytes_accessed=40 << 20,
            transcendentals=4 * total * LONGEST,
        ),
        name="front",
    )(lengths, *inputs, *far)


def one_head(pair, head):
    part = pair[head * HEAD_DIM : (head + 1) * HEAD_DIM]
    empty = jnp.zeros_like(part)
    return jnp.concatenate([part, empty] if head == 0 else [empty, part], 0)


def unroll(outs, rolled_ref, my_row, offset, block):
    total = 4 * block
    rolled_ref[:, pl.ds(0, TILE)] = rolled_ref[:, pl.ds(total, TILE)]
    back = roll_matrix(TILE - offset)
    for j, out in enumerate(outs):
        for part in range(block // TILE):
            at = pl.multiple_of((my_row ^ j) * block + part * TILE, TILE)
            rows = matdot(back, rolled_ref[:, pl.ds(at, 2 * TILE)], 1, 1)
            out[part * TILE : (part + 1) * TILE, :] = rows.astype(BF)


def attend_part(
    finish, offset, qt, k, vt, ot0, ot1, lse0, lse1, o_all, rolled_ref, send_o, send_sem, recv_sem
):
    my_row = lax.axis_index("row")
    total = k.shape[0]
    block = total // 4
    tail = total - LONGEST

    def run(pair, here, first, count, allowed):
        outs, tops = [], []
        lanes = slice(pair * 128, (pair + 1) * 128)

        def scores_of(head):
            scores = matdot(k[first : first + count, lanes], one_head(qt[lanes, here], head), 1, 0)
            return scores if allowed is None else jnp.where(allowed, scores, -1e30)

        for head in range(2):
            tops.append(jnp.max(scores_of(head), axis=0, keepdims=True))
        for head in range(2):
            wide = slice(pair * 128 + head * HEAD_DIM, pair * 128 + (head + 1) * HEAD_DIM)
            weights = jnp.exp(scores_of(head) - tops[head]).astype(BF)
            values = jnp.concatenate([vt[wide, first : first + count], jnp.ones((16, count), BF)], 0)
            mixed = matdot(values, weights, 1, 0)
            exp_sum = mixed[HEAD_DIM : HEAD_DIM + 1]
            outs.append(mixed[:HEAD_DIM] / exp_sum)
            tops[head] = tops[head] + jnp.log(exp_sum)
        low = jnp.concatenate(outs, 0).astype(BF)
        (ot0, ot1)[pair][:, here] = low
        (lse0, lse1)[pair][:, here] = jnp.concatenate(tops * 4, 0)
        return low

    copies = []
    for pair in range(2):

        def tile(i, carry):
            low = run(pair, pl.ds(pl.multiple_of(i * TILE, TILE), TILE), 0, LONGEST, None)
            rolled_ref[:, pl.ds(pl.multiple_of(TILE + i * TILE, TILE), TILE)] = low
            return carry

        lax.fori_loop(0, LONGEST // TILE, tile, 0)
        low = run(pair, pl.ds(LONGEST, tail), LONGEST, tail, tail_allowed(finish, offset, total))
        rolled_ref[:, pl.ds(total, TILE)] = low
        lanes = pl.ds(pair * 128, 128)
        outs = [o_all.at[0, :, lanes]] + [send_o.at[3 * pair + j] for j in range(3)]
        unroll(outs, rolled_ref, my_row, offset, block)
        for j in (1, 2, 3):
            number = 3 * pair + j - 1
            copies.append(
                pltpu.make_async_remote_copy(
                    send_o.at[number], o_all.at[j, :, lanes], send_sem.at[number], recv_sem.at[number],
                    device_id={"row": my_row ^ j}, device_id_type=MESH,
                )
            )
            copies[-1].start()
    for copy in copies:
        copy.wait()


FEED_PIECES = ((384, ("x", 1, 2, 4)), (384, (2, 1, "x", 4)), (256, (1, 2, 4, "x")), (256, ("x", 1, 2, 4)),)
HEAD_PIECES = (
    ((384, (1, 2, 4)),),
    ((128, (1, 2, 4)), (128, (1, 2, 4)), (128, (1, 2, 4)),),
)
HOOKS = {
    ("tile", 0, 1): [("e", 0)],
    ("tile", 0, 2): [("f2", 0)],
    ("tile", 0, 3): [("e", 1)],
    ("tile", 0, 4): [("f1", 0)],
    ("tile", 0, 5): [("f0", 0), ("f2", 1)],
    ("tile", 0, 6): [("e", 2)],
    ("tile", 0, 7): [("f1", 1)],
    ("fin", 0, 0): [("f2", 2), ("f3", 0)],
    ("fin", 0, 1): [("f1", 2)],
    ("tile", 1, 0): [("f0", 1)],
    ("tile", 1, 1): [("e", 3), ("f3", 1)],
    ("tile", 1, 2): [("f1", 3)],
    ("tile", 1, 3): [("f0", 2), ("q00", 0)],
    ("tile", 1, 4): [("f2", 3), ("f3", 2)],
    ("tile", 1, 5): [("f1", 4)],
    ("tile", 1, 6): [("f0", 3)],
    ("tile", 1, 7): [("f1", 5), ("q00", 1)],
    ("fin", 1, 0): [("f2", 4), ("f3", 3)],
    ("fin", 1, 1): [("f0", 4), ("q10", 0), ("q11", 0), ("f1", 6), ("q12", 0), ("q00", 2)],
    ("epi", 0, 0): [("f2", 5), ("f3", 4), ("q00", 3)],
    ("epi", 1, 0): [("f0", 5), ("q10", 1), ("q11", 1), ("q12", 1), ("f2", 6), ("f3", 5), ("l", 0), ("q00", 4), ("q10", 2), ("f0", 6), ("q11", 2), ("q10", 3), ("q12", 2), ("q11", 3), ("q12", 3), ("f3", 6), ("l", 1), ("q00", 5), ("q10", 4), ("q11", 4), ("q12", 4), ("l", 2), ("q10", 5), ("q11", 5), ("q12", 5), ("q00", 6), ("q10", 6), ("l", 3), ("q11", 6), ("q12", 6)],
}


def back_kernel(
    n_grp, lengths, qt, k, kt, v, ot0, ot1, lse0, lse1, cos_t, sin_t, early_in, scale_rows,
    grads_in, mixed_hbm, packed_hbm, wq_hbm, wk_hbm, wv_hbm, frames_hbm, middle_hbm, mod_hbm,
    frames_grad, packed_out, qg0, qg1, early_out, late_out, embed_out,
    grad_t, row_dots, dqt, dkt, dvt, nat_ref, rolled, mixed, packed, weights, frames, middle,
    landing, dw, send_d, got_d, early_got, late_got, summed_q, q_extra,
    send_sem, recv_sem, load_sem,
):
    my_row, my_grp = lax.axis_index("row"), lax.axis_index("grp")
    total = k.shape[0]
    block = total // 4
    steps = total // TILE
    half = HEAD_DIM // 2
    _, starts, ends, offset = layout_of(lengths)
    bits = bits_of(n_grp)
    extra = bits[3:]
    side = lambda bit: (my_grp // bit) % 2
    by_row = lambda j: {"row": my_row ^ j}
    by_grp = lambda bit: {"grp": my_grp ^ bit}
    q_out = (qg0, qg1)

    chains, numbers, started = {}, {}, []

    def copies_of(name, step):
        out = []
        for index, (src, dst, device) in enumerate(chains[name][step][0]()):
            number = numbers.setdefault((name, step, index), len(numbers))
            out.append(
                pltpu.make_async_remote_copy(
                    src, dst, send_sem.at[number], recv_sem.at[number],
                    device_id=device, device_id_type=MESH,
                )
            )
        return out

    def start(name, step=0):
        started.append((name, step))
        for copy in copies_of(name, step):
            copy.start()

    def advance(name, step):
        for copy in copies_of(name, step):
            copy.wait_recv()
        chains[name][step][1]()
        if step + 1 < len(chains[name]):
            start(name, step + 1)

    def run_hook(mark):
        for name, step in HOOKS.get(mark, ()):
            advance(name, step)

    def one_step(number, src, dst, device):
        copy = pltpu.make_async_remote_copy(
            src, dst, send_sem.at[number], recv_sem.at[number], device_id=device, device_id_type=MESH
        )
        copy.start()
        copy.wait()

    def away(region, bit):
        offset, size = region
        return pl.ds(pl.multiple_of(offset + (1 - side(bit)) * (size // 2), 16), size // 2)

    def kept(region, bit):
        offset, size = region
        return (offset + side(bit) * (size // 2), size // 2)

    def at(region):
        return pl.ds(pl.multiple_of(region[0], 16), region[1])

    nothing = lambda: None

    def feed_chain(name, region, order, land):
        chain, areas, shards = [], [], (1, 0)
        for op in order:
            source = packed if chain else packed_hbm
            if op == "x":

                def parts(region=region, land=land, source=source):
                    return [(source.at[1, at(region)], landing.at[pl.ds(land, region[1])], by_row(2))]

                def take(region=region, land=land):
                    got = landing[land : land + region[1]]
                    packed[0, at(region)] = add_low(packed[0, at(region)], got)

                shards, land = (0,), land + region[1]
            else:
                size = region[1] // 2

                def parts(region=region, land=land, source=source, shards=shards, size=size, op=op):
                    return [
                        (
                            source.at[shard, away(region, op)],
                            landing.at[pl.ds(land + i * size, size)],
                            by_grp(op),
                        )
                        for i, shard in enumerate(shards)
                    ]

                region = kept(region, op)

                def take(region=region, land=land, shards=shards, size=size):
                    for i, shard in enumerate(shards):
                        got = landing[land + i * size : land + (i + 1) * size]
                        packed[shard, at(region)] = add_low(packed[shard, at(region)], got)

                land += size * len(shards)
                areas.append((op, region))
            chain.append((parts, take))
        last = chain[-1][1]

        def own():
            last()
            for i, bit in enumerate(extra):
                first, size = land + i * region[1], region[1]
                number = numbers.setdefault((name, "extra", i), len(numbers))
                one_step(number, packed.at[0, at(region)], landing.at[pl.ds(first, size)], by_grp(bit))
                packed[0, at(region)] = add_low(packed[0, at(region)], landing[first : first + size])
            packed_out[at(region)] = packed[0, at(region)]

        chain[-1] = (chain[-1][0], own)
        for bit, area in reversed(areas):
            chain.append(
                (
                    lambda bit=bit, area=area: [
                        (packed_out.at[at(area)], packed_out.at[at(area)], by_grp(bit))
                    ],
                    nothing,
                )
            )
        chains[name] = chain
        return land + len(extra) * region[1]

    def heads_chain(name, pair, number, lanes, order):
        chain, areas, region = [], [], (0, 256)
        for bit in order:
            size = region[1] // 2
            land = slice(256 - region[1], 256 - size)

            def parts(region=region, bit=bit, land=land):
                return [
                    (
                        dw.at[pair, :, away(region, bit), lanes],
                        summed_q.at[pair, :, pl.ds(land.start, land.stop - land.start), lanes],
                        by_grp(bit),
                    )
                ]

            region = kept(region, bit)

            def take(region=region, land=land):
                mine = at(region)
                dw[pair, :, mine, lanes] = add_low(
                    dw[pair, :, mine, lanes], summed_q[pair, :, land, lanes]
                )

            areas.append((bit, region))
            chain.append((parts, take))
        last, part = chain[-1][1], region

        def own():
            last()
            for i, bit in enumerate(extra):
                slot = 4 * (pair * len(extra) + i)
                count = numbers.setdefault((name, "extra", i), len(numbers))
                one_step(
                    count, dw.at[pair, :, at(part), lanes], q_extra.at[pl.ds(slot, 4), :, lanes],
                    by_grp(bit),
                )
                dw[pair, :, at(part), lanes] = add_low(
                    dw[pair, :, at(part), lanes], q_extra[slot : slot + 4, :, lanes]
                )
            q_out[pair][0, at(part), lanes] = dw[pair, my_row, at(part), lanes]

        chain[-1] = (chain[-1][0], own)
        chain.append(
            (
                lambda: [
                    (
                        dw.at[pair, my_row ^ j, at(part), lanes],
                        q_out[pair].at[j, at(part), lanes],
                        by_row(j),
                    )
                    for j in (1, 2, 3)
                ],
                nothing,
            )
        )
        for bit, area in reversed(areas):
            spot = lambda area=area: q_out[pair].at[:, at(area), lanes]
            chain.append((lambda bit=bit, spot=spot: [(spot(), spot(), by_grp(bit))], nothing))
        chains[name] = chain

    def gather_chain(name, got, out, finish):
        def first():
            out[0] = finish((got[0] + got[1]) + (got[2] + got[3]))

        chain = [(lambda: [(got.at[my_row], got.at[my_row], by_row(j)) for j in (1, 2, 3)], first)]
        for i, bit in enumerate(bits):
            chain.append(
                (
                    lambda i=i, bit=bit: [
                        (out.at[pl.ds(0, 1 << i)], out.at[pl.ds(1 << i, 1 << i)], by_grp(bit))
                    ],
                    nothing,
                )
            )
        chains[name] = chain

    def fold(sums):
        width = sums.shape[1] // 2
        return jnp.concatenate([sums[:, :width], sums[:, width:]], 0).astype(BF)

    loads = [
        pltpu.make_async_copy(src, dst, load_sem.at[i])
        for i, (src, dst) in enumerate(
            (
                (packed_hbm, packed),
                (mixed_hbm, mixed),
                (wq_hbm, mixed.at[pl.ds(0, D)]),
                (wk_hbm, mixed.at[pl.ds(D, D)]),
                (wv_hbm, weights),
                (frames_hbm, frames),
                (middle_hbm, middle),
            )
        )
    ]
    for load in loads[:1] + loads[4:]:
        load.start()

    barrier = pltpu.get_barrier_semaphore()
    for device in [by_row(j) for j in (1, 2, 3)] + [by_grp(bit) for bit in bits]:
        pl.semaphore_signal(barrier, inc=1, device_id=device, device_id_type=MESH)
    pl.semaphore_wait(barrier, 3 + len(bits))

    gather_chain("e", early_got, early_out, fold)
    early_got[my_row] = early_in[...]
    start("e")
    land, first_row = 0, 0
    for number, (count, order) in enumerate(FEED_PIECES):
        land = feed_chain(f"f{number}", (first_row, count), order, land)
        first_row += count
        start(f"f{number}")

    lanes_of = slice(0, 256)
    for j in range(4):
        mixed[pl.ds(pl.multiple_of((my_row ^ j) * block, block), block), lanes_of] = grads_in[j]
    ahead = roll_matrix(offset)

    def turn(i, carry):
        cols = pl.ds(pl.multiple_of(i * TILE, TILE), TILE)
        after = pl.ds(pl.multiple_of((i + 1) % steps * TILE, TILE), TILE)
        part = matdot(ahead[:, :TILE], mixed[cols, lanes_of], 1, 0)
        part = (part + matdot(ahead[:, TILE:], mixed[after, lanes_of], 1, 0)).T
        grad_t[:, cols] = part.astype(BF)
        for head in range(4):
            mine = slice((head % 2) * HEAD_DIM, (head % 2 + 1) * HEAD_DIM)
            crossed = part[head * HEAD_DIM : (head + 1) * HEAD_DIM] * (ot0, ot1)[head // 2][
                mine, cols
            ].astype(F32)
            row_dots[head : head + 1, cols] = jnp.sum(crossed, axis=0, keepdims=True)
        return carry

    lax.fori_loop(0, steps, turn, 0)
    loads[1].start()
    loads[0].wait()

    def run(pair, here, spans, allowed):
        lanes = slice(pair * 128, (pair + 1) * 128)
        lse = (lse0, lse1)[pair]
        for head in range(2):
            mine = slice(head * HEAD_DIM, (head + 1) * HEAD_DIM)
            wide = slice(pair * 128 + head * HEAD_DIM, pair * 128 + (head + 1) * HEAD_DIM)
            dots = slice(2 * pair + head, 2 * pair + head + 1)
            grad_query = None
            for first, count in spans:
                keys = pl.ds(first, count)
                scores = matdot(k[keys, lanes], one_head(qt[lanes, here], head), 1, 0)
                if allowed is not None:
                    scores = jnp.where(allowed, scores, -1e30)
                probs = jnp.exp(scores - lse[head : head + 1, here])
                grad_probs = matdot(v[keys, lanes], one_head(grad_t[lanes, here], head), 1, 0)
                grad_scores = (probs * (grad_probs - row_dots[dots, here])).astype(BF)
                part = matdot(kt[wide, keys], grad_scores, 1, 0)
                grad_query = part if grad_query is None else grad_query + part
                dkt[mine, keys] += matdot(qt[wide, here], grad_scores, 1, 1)
                dvt[mine, keys] += matdot(grad_t[wide, here], probs.astype(BF), 1, 1)
            dqt[mine, here] = grad_query * HEAD_DIM**-0.5

    def finish(pair):
        def part(i, sums):
            cols = pl.ds(pl.multiple_of(i * TILE, TILE), TILE)
            cosine, sine = cos_t[:, cols], sin_t[:, cols]

            def turned(ref):
                parts = []
                for at_row in range(0, 128, HEAD_DIM):
                    first = ref[at_row : at_row + half, cols]
                    second = ref[at_row + half : at_row + HEAD_DIM, cols]
                    parts.append(first * cosine + second * sine)
                    parts.append(second * cosine - first * sine)
                return jnp.concatenate(parts, 0)

            columns = jnp.concatenate([turned(dqt), turned(dkt), dvt[:, cols]], 0)
            nat_ref[:, pl.ds(pl.multiple_of(TILE + i * TILE, TILE), TILE)] = columns.astype(BF)
            low = columns.T.astype(BF)
            rolled[cols, :] = low
            return sums + jnp.sum(low.astype(F32), axis=0, keepdims=True)

        sums = lax.fori_loop(0, steps, part, jnp.zeros((1, 384), F32))
        if pair == 1:
            for copy in copies_of("d0", 0):
                copy.wait_send()
        unroll(
            [got_d.at[my_row, pair]] + [send_d.at[j] for j in range(3)], nat_ref, my_row, offset, block
        )
        chains[f"d{pair}"] = [
            (
                lambda: [(send_d.at[j - 1], got_d.at[my_row, pair], by_row(j)) for j in (1, 2, 3)],
                nothing,
            )
        ]
        start(f"d{pair}")
        run_hook(("fin", pair, 0))
        if pair == 0:
            loads[1].wait()
        for shard in range(4):
            columns = mixed[:, shard * 256 : (shard + 1) * 256]
            dw[pair, shard] = contract_rows(columns, rolled[...]).astype(BF)
        lane = 0
        for number, (count, order) in enumerate(HEAD_PIECES[pair]):
            heads_chain(f"q{pair}{number}", pair, number, pl.ds(lane, count), order)
            start(f"q{pair}{number}")
            lane += count
        return sums

    bias_sums = []
    for pair in range(2):
        dkt[...] = jnp.zeros_like(dkt)
        dvt[...] = jnp.zeros_like(dvt)

        def tile(i, carry):
            run(pair, pl.ds(pl.multiple_of(i * TILE, TILE), TILE), BACK_SPANS, None)
            for when in range(steps - 1):
                if ("tile", pair, when) in HOOKS:
                    pl.when(i == when)(functools.partial(run_hook, ("tile", pair, when)))
            return carry

        lax.fori_loop(0, steps - 1, tile, 0)
        tail = total - LONGEST
        run(pair, pl.ds(LONGEST, tail), [(LONGEST, tail)], tail_allowed(ends, offset, total))
        run_hook(("tile", pair, steps - 1))
        bias_sums.append(finish(pair))
        if pair == 1:
            for load in loads[2:4]:
                load.start()
        run_hook(("fin", pair, 1))

    for pair in range(2):
        advance(f"d{pair}", 0)
    for load in loads[2:]:
        load.wait()
    late = [jnp.zeros((1, 2 * D), F32) for _ in range(4)]
    for part in range(block // TILE):
        rows = slice(part * TILE, (part + 1) * TILE)
        grad = jnp.zeros((TILE, D), F32)
        for kind in range(3):
            pieces = [
                got_d[owner, pair, rows, kind * 128 : (kind + 1) * 128]
                for owner in range(4)
                for pair in range(2)
            ]
            weight = weights[...] if kind == 2 else mixed[kind * D : (kind + 1) * D]
            grad = grad + against(jnp.concatenate(pieces, 1), weight)
        normed, factor = normalize(frames[rows, :].astype(F32))
        spots = my_row * block + part * TILE + lax.broadcasted_iota(jnp.int32, (TILE, 1), 0)
        marks = marks_of(spots, starts, ends)
        scale = jnp.ones((TILE, D), F32)
        for u in range(4):
            scale = scale + marks[u] * scale_rows[u : u + 1, D : 2 * D]
        back = normalize_back(grad * scale, normed, factor)
        frames_grad[rows, :] = (middle[rows, :] + back).astype(BF)
        for u in range(4):
            mark = marks[u]
            late[u] += jnp.concatenate(
                [jnp.sum(t * mark, axis=0, keepdims=True) for t in (grad, grad * normed)], 1
            )
        if part == 0:
            run_hook(("epi", 0, 0))

    widths = [slice(kind * 128, (kind + 1) * 128) for kind in range(3)]
    bias_row = jnp.concatenate(
        [bias_sums[pair][:, w] for w in widths for pair in range(2)]
        + [jnp.zeros((1, 2 * D - 768), F32)],
        1,
    )
    index = lax.broadcasted_iota(jnp.int32, (8, 2 * D), 0)
    gather_chain(
        "l", late_got, late_out, lambda sums: fold(jnp.where(index == 4, bias_row, sums))
    )
    late_got[my_row] = jnp.concatenate(late + [jnp.zeros((4, 2 * D), F32)], 0)
    start("l")

    slots = [mixed.at[pl.ds(0, D)], mixed.at[pl.ds(D, D)], weights]
    blocks = [2, 3, 4, 5, 0, 1]
    fetches = [
        pltpu.make_async_copy(
            mod_hbm.at[:, pl.ds(block * D, D)], slots[i % 3], load_sem.at[len(loads) + i % 3]
        )
        for i, block in enumerate(blocks)
    ]
    for fetch in fetches[:3]:
        fetch.start()
    embed_out[...] = jnp.zeros_like(embed_out)

    def embed_step(i):
        block = blocks[i]
        fetches[i].wait()
        if block < 2:
            rows = late_out[0].astype(F32)[8 * block : 8 * block + 8]
        else:
            part, lane = divmod(block - 2, 2)
            rows = early_out[0, :, lane * D : (lane + 1) * D].astype(F32)[8 * part : 8 * part + 8]
        embed_out[...] += against(rows.astype(BF), slots[i % 3][...])
        if i + 3 < len(blocks):
            fetches[i + 3].start()

    done, late_ready = 0, False
    for number, (name, step) in enumerate(HOOKS[("epi", 1, 0)]):
        advance(name, step)
        late_ready = late_ready or (name, step) == ("l", 0)
        if number % 3 == 2 and done < (6 if late_ready else 4):
            embed_step(done)
            done += 1
    for i in range(done, 6):
        embed_step(i)
    for number in range(3, len(bits)):
        advance("e", number + 1)
        advance("l", number + 1)
    for name, step in started:
        if name != "d0":
            for copy in copies_of(name, step):
                copy.wait_send()


def attend_back(
    n_grp, lengths, qt, k, kt, v, heads_t, lse, cos_t, sin_t, early, scale_rows, grads, mixed, packed, weights, frames, middle, mod_weight,
):
    total = k.shape[0]
    block = total // 4
    rows = packed.shape[1]
    extra = max(0, len(bits_of(n_grp)) - 3)
    inputs = [
        qt, k, kt, v, *heads_t, *lse, cos_t, sin_t, early, scale_rows, grads,
    ]
    far = [mixed, packed, *weights, frames, middle, mod_weight]
    copies = 160
    return pl.pallas_call(
        functools.partial(back_kernel, n_grp),
        out_shape=[
            jax.ShapeDtypeStruct((block, D), BF),
            jax.ShapeDtypeStruct((rows, D), BF),
            jax.ShapeDtypeStruct((4, 256, 384), BF),
            jax.ShapeDtypeStruct((4, 256, 384), BF),
            jax.ShapeDtypeStruct((n_grp, 16, 2 * D), BF),
            jax.ShapeDtypeStruct((n_grp, 16, D), BF),
            jax.ShapeDtypeStruct((8, D), F32),
        ],
        in_specs=[pl.BlockSpec(memory_space=SMEM)]
        + [pl.BlockSpec(memory_space=VMEM)] * len(inputs)
        + [pl.BlockSpec(memory_space=pl.ANY)] * len(far),
        out_specs=[pl.BlockSpec(memory_space=VMEM)] * 7,
        scratch_shapes=[
            VMEM((256, total), BF),
            VMEM((8, total), F32),
            VMEM((128, total), F32),
            VMEM((128, total), F32),
            VMEM((128, total), F32),
            VMEM((384, total + TILE), BF),
            VMEM((total, 384), BF),
            VMEM((total, D), BF),
            VMEM((2, rows, D), BF),
            VMEM((D, D), BF),
            VMEM((block, D), BF),
            VMEM((block, D), F32),
            VMEM((rows * (15 + extra) // 8, D), BF),
            VMEM((2, 4, 256, 384), BF),
            VMEM((3, block, 384), BF),
            VMEM((4, 2, block, 384), BF),
            VMEM((4, 8, 4 * D), F32),
            VMEM((4, 8, 2 * D), F32),
            VMEM((2, 4, 256, 384), BF),
            VMEM((max(1, 8 * extra), 32, 384), BF),
            pltpu.SemaphoreType.DMA((copies,)),
            pltpu.SemaphoreType.DMA((copies,)),
            pltpu.SemaphoreType.DMA((len(far) + 3,)),
        ],
        compiler_params=pltpu.CompilerParams(
            vmem_limit_bytes=62 << 20, collective_id=1, has_side_effects=True
        ),
        cost_estimate=pl.CostEstimate(
            flops=4 * 2 * 5 * total * LONGEST * 256,
            bytes_accessed=40 << 20,
            transcendentals=4 * total * LONGEST,
        ),
        name="attend_back",
    )(lengths, *inputs, *far)


def feed_kernel(
    lengths, o, frames, cot, mod, act, out_bias, up_bias, down_bias, out_hbm, up_hbm, down_hbm,
    output, middle_out, grads_out, packed, early_out,
    w_out, w_up, w_down, h_s, a_s, ez_s, eb_s, ea_s, send_o, send_w, got_w, load_sem, send_sem, recv_sem,
):
    my_row = lax.axis_index("row")
    by_row = lambda j: {"row": my_row ^ j}
    rows_all = frames.shape[0]
    _, starts, ends, _ = layout_of(lengths)
    width = D // 4
    loads = [
        pltpu.make_async_copy(
            out_hbm.at[pl.ds(pl.multiple_of((my_row ^ j) * width, width), width)],
            w_out.at[pl.ds(j * width, width)],
            load_sem.at[j],
        )
        for j in range(4)
    ] + [
        pltpu.make_async_copy(up_hbm, w_up, load_sem.at[4]),
        pltpu.make_async_copy(down_hbm, w_down, load_sem.at[5]),
    ]
    for load in loads:
        load.start()
    barrier = pltpu.get_barrier_semaphore()
    for j in (1, 2, 3):
        pl.semaphore_signal(barrier, inc=1, device_id=by_row(j), device_id_type=MESH)
    pl.semaphore_wait(barrier, 3)

    def remote(number, src, dst, j):
        return pltpu.make_async_remote_copy(
            src, dst, send_sem.at[number], recv_sem.at[number], device_id=by_row(j), device_id_type=MESH
        )

    copies = []
    coef = math.sqrt(2.0 / math.pi)
    sums = [[jnp.zeros((1, D), F32) for _ in range(4)] for _ in range(4)]
    bias_sums = [jnp.zeros((1, n), F32) for n in (D, 2 * D, D)]
    for tile in range(rows_all // TILE):
        rows = slice(tile * TILE, (tile + 1) * TILE)
        spots = my_row * rows_all + tile * TILE + lax.broadcasted_iota(jnp.int32, (TILE, 1), 0)
        marks = marks_of(spots, starts, ends)

        def per_row(block):
            total = marks[0] * mod[0:1, block * D : (block + 1) * D]
            for u in range(1, 4):
                total = total + marks[u] * mod[u : u + 1, block * D : (block + 1) * D]
            return total

        gate_a, shift_f, scale_f, gate_f = per_row(2), per_row(3), 1.0 + per_row(4), per_row(5)
        if tile == 0:
            for load in loads[:4]:
                load.wait()
        heads = jnp.concatenate([o[j, rows, :] for j in range(4)], 1)
        attended = matdot(heads, w_out[...], 1, 0) + out_bias[...]
        middle = frames[rows, :].astype(F32) + gate_a * attended
        normed, factor = normalize(middle)
        h = (normed * scale_f + shift_f).astype(BF)
        h_s[rows, :] = h
        if tile == 0:
            loads[4].wait()
        z = matdot(h, w_up[...], 1, 0) + up_bias[...]
        square = z * z
        curve = jnp.tanh(coef * (z * (1.0 + 0.044715 * square)))
        share = 0.5 * (1.0 + curve)
        a = (z * share).astype(BF)
        a_s[rows, :] = a
        slope = share + (0.5 * coef) * z * (1.0 - curve * curve) * (1.0 + (3 * 0.044715) * square)
        if tile == 0:
            loads[5].wait()
        branch = matdot(a, w_down[...], 1, 0) + down_bias[...]
        output[rows, :] = (middle + gate_f * branch).astype(BF)
        upstream = cot[rows, :].astype(F32)
        e_b = (upstream * gate_f).astype(BF)
        eb_s[rows, :] = e_b
        e_z = (against(e_b, w_down[...]) * slope).astype(BF)
        ez_s[rows, :] = e_z
        e_h = against(e_z, w_up[...])
        e_mid = upstream + normalize_back(e_h * scale_f, normed, factor)
        middle_out[rows, :] = e_mid
        e_att = (e_mid * gate_a).astype(BF)
        ea_s[rows, :] = e_att
        e_o = against(e_att, w_out[...]).astype(BF)
        grads_out[0, rows, :] = e_o[:, :width]
        for j in (1, 2, 3):
            send_o[j - 1, rows, :] = e_o[:, j * width : (j + 1) * width]
            copies.append(
                remote(
                    len(copies), send_o.at[j - 1, pl.ds(tile * TILE, TILE)],
                    grads_out.at[j, pl.ds(tile * TILE, TILE)], j,
                )
            )
            copies[-1].start()
        for block, part in enumerate((e_mid * attended, e_h, e_h * normed, upstream * branch)):
            for u in range(4):
                sums[u][block] += jnp.sum(part * marks[u], axis=0, keepdims=True)
        for number, part in enumerate((e_att, e_z, e_b)):
            bias_sums[number] += jnp.sum(part.astype(F32), axis=0, keepdims=True)

    early_out[...] = jnp.concatenate(
        [jnp.concatenate(row, 1) for row in sums + [bias_sums]]
        + [act[...] * 0.25, jnp.zeros((2, 4 * D), F32)],
        0,
    )

    def shard(j, store):
        owner = my_row ^ j
        columns = pl.ds(pl.multiple_of(owner * 2 * width, 2 * width), 2 * width)
        store(768, contract_rows(a_s[:, columns], eb_s[...]))
        columns = pl.ds(pl.multiple_of(owner * width, width), width)
        store(256, contract_rows(h_s[:, columns], ez_s[:, :D]))
        store(512, contract_rows(h_s[:, columns], ez_s[:, D:]))
        store(0, contract_rows(o[j], ea_s[...]))

    for slot, j in enumerate((1, 3)):

        def store(first, value):
            send_w[slot, first : first + value.shape[0], :] = value.astype(BF)

        shard(j, store)
        copies.append(remote(len(copies), send_w.at[slot], got_w.at[slot], 1))
        copies[-1].start()
    for slot, j in enumerate((0, 2)):

        def store(first, value):
            packed[slot, first : first + value.shape[0], :] = value.astype(BF)

        shard(j, store)
    for slot in range(2):
        copies[-2 + slot].wait_recv()
        packed[slot] = add_low(packed[slot], got_w[slot])
    for copy in copies[:-2]:
        copy.wait_recv()
    for copy in copies:
        copy.wait_send()


def feed(lengths, o, frames, cot, mod, act, biases, weights):
    rows = frames.shape[0]
    inputs = [o, frames, cot, mod, act, *[b[None] for b in biases]]
    return pl.pallas_call(
        feed_kernel,
        out_shape=[
            jax.ShapeDtypeStruct((rows, D), BF),
            jax.ShapeDtypeStruct((rows, D), F32),
            jax.ShapeDtypeStruct((4, rows, D // 4), BF),
            jax.ShapeDtypeStruct((2, 1280, D), BF),
            jax.ShapeDtypeStruct((8, 4 * D), F32),
        ],
        in_specs=[pl.BlockSpec(memory_space=SMEM)]
        + [pl.BlockSpec(memory_space=VMEM)] * len(inputs)
        + [pl.BlockSpec(memory_space=pl.ANY)] * 3,
        out_specs=[pl.BlockSpec(memory_space=VMEM)] * 5,
        scratch_shapes=[
            VMEM((D, D), BF),
            VMEM((D, 2 * D), BF),
            VMEM((2 * D, D), BF),
            VMEM((rows, D), BF),
            VMEM((rows, 2 * D), BF),
            VMEM((rows, 2 * D), BF),
            VMEM((rows, D), BF),
            VMEM((rows, D), BF),
            VMEM((3, rows, D // 4), BF),
            VMEM((2, 1280, D), BF),
            VMEM((2, 1280, D), BF),
            pltpu.SemaphoreType.DMA((6,)),
            pltpu.SemaphoreType.DMA((3 * rows // TILE + 2,)),
            pltpu.SemaphoreType.DMA((3 * rows // TILE + 2,)),
        ],
        compiler_params=pltpu.CompilerParams(
            vmem_limit_bytes=LIMIT, collective_id=2, has_side_effects=True
        ),
        cost_estimate=pl.CostEstimate(
            flops=2 * rows * D * 15 * D, bytes_accessed=30 << 20, transcendentals=rows * 2 * D
        ),
        name="feed",
    )(lengths, *inputs, *weights)


def outputs_kernel(
    packed, heads_0, heads_1, early, late, embedding, embed_in,
    out_far, up_far, down_far, query_far, key_far, value_far, mod_far,
    mod_b, embed, out_b, up_b, down_b, query_b, key_b, value_b,
    out_w, up_w, down_w, query_w, key_w, value_w, mod_w, rows_ref, mod_ref, store_sem,
):
    my_row = lax.axis_index("row")
    width = D // 4
    stores = []

    def store(src, dst):
        stores.append(pltpu.make_async_copy(src, dst, store_sem.at[len(stores)]))
        stores[-1].start()

    n_grp = early.shape[0]
    out_w[...] = packed[:width].astype(F32)
    up_w[:, :D] = packed[width : 2 * width].astype(F32)
    up_w[:, D:] = packed[2 * width : 3 * width].astype(F32)
    store(out_w, out_far)
    store(up_w, up_far)
    down_w[...] = packed[3 * width :].astype(F32)
    store(down_w, down_far)
    for pair, heads in enumerate((heads_0, heads_1)):
        for j in range(4):
            lanes = pl.ds(pl.multiple_of((my_row ^ j) * width + pair * 128, 128), 128)
            for kind, out in enumerate((query_w, key_w, value_w)):
                out[:, lanes] = heads[j, :, kind * 128 : (kind + 1) * 128].astype(F32)
    store(query_w, query_far)
    store(key_w, key_far)
    store(value_w, value_far)
    for first, source, count in ((0, late, D), (2 * D, early, 2 * D)):
        for part in range(2):
            rows = source[:, 8 * part : 8 * part + 8].astype(F32).reshape(n_grp * 8, count)
            mod_ref[:, first + part * count : first + (part + 1) * count] = rows
    number = lax.broadcasted_iota(jnp.int32, (n_grp * 8, 1), 0) % 8
    utterance, bias = (number < 4).astype(F32), (number == 4).astype(F32)
    act = jnp.zeros((n_grp * 8, width), F32)
    for u in range(4):
        lanes = pl.ds(pl.multiple_of((2 + u) * D + my_row * width, width), width)
        moved = pltpu.roll(mod_ref[:, lanes], (u - 5) % (n_grp * 8), 0)
        act = jnp.where(number == u, moved, act)
    act = act.astype(BF)
    for block in range(6):
        lanes = slice(block * D, (block + 1) * D)
        rows = mod_ref[:, lanes]
        mod_w[:, lanes] = contract_rows(act, rows.astype(BF))
        store(mod_w.at[:, pl.ds(block * D, D)], mod_far.at[:, pl.ds(block * D, D)])
        sums = [jnp.sum(rows * mark, axis=0, keepdims=True) for mark in (utterance, bias)]
        rows_ref[:, lanes] = jnp.concatenate(sums + [jnp.zeros((6, D), F32)], 0)

    def own(row, first, size):
        lanes = pl.ds(pl.multiple_of(first + my_row * size, 128), size)
        return rows_ref[row, lanes]

    mod_b[...] = own(0, 0, 6 * width)
    for i, out in enumerate((query_b, key_b, value_b)):
        out[...] = rows_ref[1, i * width : (i + 1) * width]
    out_b[...] = own(1, 2 * D, width)
    up_b[...] = own(1, 3 * D, 2 * width)
    down_b[...] = own(1, 5 * D, width)
    gate = 1.0 / (1.0 + jnp.exp(-embedding[...]))
    embed[...] = embed_in[:4] * (gate * (1.0 + embedding[...] * (1.0 - gate)))
    for copy in stores:
        copy.wait()


def outputs(packed, heads_0, heads_1, early, late, embedding, embed_in):
    width = D // 4
    n_grp = early.shape[0]
    shapes = [(width, D), (width, 2 * D), (2 * width, D)] + [(width, D)] * 3 + [(width, 6 * D)]
    shapes += [(6 * width,), (4, D)] + [(n,) for n in (width, 2 * width, width, width, width, width)]
    return pl.pallas_call(
        outputs_kernel,
        out_shape=[jax.ShapeDtypeStruct(shape, F32) for shape in shapes],
        in_specs=[pl.BlockSpec(memory_space=VMEM)] * 7,
        out_specs=[pl.BlockSpec(memory_space=pl.ANY)] * 7
        + [pl.BlockSpec(memory_space=VMEM)] * (len(shapes) - 7),
        scratch_shapes=[VMEM(shape, F32) for shape in shapes[:7]]
        + [
            VMEM((8, 6 * D), F32),
            VMEM((n_grp * 8, 6 * D), F32),
            pltpu.SemaphoreType.DMA((12,)),
        ],
        compiler_params=pltpu.CompilerParams(vmem_limit_bytes=LIMIT),
        name="outputs",
    )(packed, heads_0, heads_1, early, late, embedding, embed_in)


def local(
    frames, time_embed, lengths, mod_weight, mod_bias, query_weight, query_bias, key_weight, key_bias,
    value_weight, value_bias, out_weight, out_bias, up_weight, up_bias, down_weight, down_bias, cotangent,
):
    n_grp = lax.axis_size("grp")
    lengths, embedding = lengths[0], time_embed[0]
    weights = (query_weight, key_weight, value_weight)
    mixed, qt, kt, k_rows, v_rows, cos_t, sin_t, modulation, act, *heads_t, lse_0, lse_1, o_all = front(
        lengths, frames, embedding, mod_weight, mod_bias, weights, (query_bias, key_bias, value_bias)
    )
    output, grad_middle, grad_pieces, packed, early = feed(
        lengths, o_all, frames, cotangent, modulation, act, (out_bias, up_bias, down_bias),
        (out_weight, up_weight, down_weight),
    )
    grad_frames, packed_total, heads_0, heads_1, early_all, late_all, embed_part = attend_back(
        n_grp, lengths, qt, k_rows, kt, v_rows, heads_t, (lse_0, lse_1), cos_t, sin_t, early,
        modulation, grad_pieces, mixed, packed, weights, frames, grad_middle, mod_weight,
    )
    grads = outputs(packed_total, heads_0, heads_1, early_all, late_all, embedding, embed_part)
    out_grad, up_grad, down_grad, query_grad, key_grad, value_grad, mod_weight_grad = grads[:7]
    mod_bias_grad, grad_embedding = grads[7], grads[8]
    out_b, up_b, down_b, query_b, key_b, value_b = grads[9:]
    return (
        output,
        grad_frames,
        grad_embedding[None],
        mod_weight_grad,
        mod_bias_grad,
        query_grad,
        query_b,
        key_grad,
        key_b,
        value_grad,
        value_b,
        out_grad,
        out_b,
        up_grad,
        up_b,
        down_grad,
        down_b,
    )


def solution(mesh):
    placed = (
        (P(("grp", "row"), None), P("grp", None, None), P("grp", None))
        + (P(),) * 14
        + (P(("grp", "row"), None),)
    )
    return jax.shard_map(
        local,
        mesh=mesh,
        in_specs=placed,
        out_specs=(
            P(("grp", "row"), None),
            P(("grp", "row"), None),
            P("grp", None, None),
        )
        + (P("row", None), P("row")) * 7,
        check_vma=False,
    )
```
